32 devices in a mesh: dp: 16 (over z, x, core), tensor: 2 (over y).
Axes of the slice: x: 2, y: 2, z: 4, core: 2. Of those that a mesh axis runs over, the one named last changes fastest.
Arguments:
- token_ids: int32 [32, 1024], P(('dp', 'tensor')), may hold values from 0 to 30719
- lengths: int32 [16, 2], P('dp'), may hold values from 256 to 1024, as said below
- token_table: float32 [30720, 768], P(('dp', 'tensor')), may hold values from -0.75 to 0.75
- table_first: float32 [30720, 768], P(('dp', 'tensor')), may hold values from -1.0430813e-07 to 1.0430813e-07
- table_second: float32 [30720, 768], P(('dp', 'tensor')), may hold values from 3.3302913e-15 to 1.3321165e-14
- qkv_weight: float32 [768, 3, 768], P('dp', None, 'tensor'), may hold values from -0.21875 to 0.21875
- qkv_first: float32 [768, 3, 768], P('dp', None, 'tensor'), may hold values from -8.34465e-07 to 8.34465e-07
- qkv_second: float32 [768, 3, 768], P('dp', None, 'tensor'), may hold values from 3.3302914e-16 to 1.3321165e-15
- out_weight: float32 [768, 768], P('dp', 'tensor'), may hold values from -1.25 to 1.25
- out_first: float32 [768, 768], P('dp', 'tensor'), may hold values from -1.4901161e-07 to 1.4901161e-07
- out_second: float32 [768, 768], P('dp', 'tensor'), may hold values from 1.0899135e-17 to 4.359654e-17
- gate_up_weight: float32 [768, 2, 3072], P('dp', None, 'tensor'), may hold values from -0.21875 to 0.21875
- gate_up_first: float32 [768, 2, 3072], P('dp', None, 'tensor'), may hold values from -4.172325e-07 to 4.172325e-07
- gate_up_second: float32 [768, 2, 3072], P('dp', None, 'tensor'), may hold values from 8.7798585e-17 to 3.5119434e-16
- down_weight: float32 [768, 3072], P('dp', 'tensor'), may hold values from -0.109375 to 0.109375
- down_first: float32 [768, 3072], P('dp', 'tensor'), may hold values from -5.9604645e-07 to 5.9604645e-07
- down_second: float32 [768, 3072], P('dp', 'tensor'), may hold values from 1.6651457e-16 to 6.6605827e-16
- norm_params: float32 [6, 768], replicated, may hold values from -0.8 to 1.4
- norm_first: float32 [6, 768], replicated, may hold values from -9.536743e-07 to 9.536743e-07
- norm_second: float32 [6, 768], replicated, may hold values from 8.1743513e-16 to 3.2697405e-15
- log_inverse_warmth: float32 [], replicated, may hold values from 2 to 2.7
- scale_first: float32 [], replicated, may hold values from -2.2888184e-05 to 2.2888184e-05
- scale_second: float32 [], replicated, may hold values from 3.0275376e-11 to 1.211015e-10
Outputs:
- batch_loss: float32 [], replicated
- grad_norm: float32 [], replicated
- table_first_next: float32 [30720, 768], P(('dp', 'tensor'))
- table_second_next: float32 [30720, 768], P(('dp', 'tensor'))
- table_change: float32 [30720, 768], P(('dp', 'tensor'))
- qkv_first_next: float32 [768, 3, 768], P('dp', None, 'tensor')
- qkv_second_next: float32 [768, 3, 768], P('dp', None, 'tensor')
- qkv_change: float32 [768, 3, 768], P('dp', None, 'tensor')
- out_first_next: float32 [768, 768], P('dp', 'tensor')
- out_second_next: float32 [768, 768], P('dp', 'tensor')
- out_change: float32 [768, 768], P('dp', 'tensor')
- gate_up_first_moment_updated: float32 [768, 2, 3072], P('dp', None, 'tensor')
- gate_up_second_next: float32 [768, 2, 3072], P('dp', None, 'tensor')
- gate_up_change: float32 [768, 2, 3072], P('dp', None, 'tensor')
- down_first_next: float32 [768, 3072], P('dp', 'tensor')
- down_second_next: float32 [768, 3072], P('dp', 'tensor')
- down_change: float32 [768, 3072], P('dp', 'tensor')
- norm_first_next: float32 [6, 768], replicated
- norm_second_next: float32 [6, 768], replicated
- norm_change: float32 [6, 768], replicated
- scale_first_next: float32 [], replicated
- scale_second_next: float32 [], replicated
- scale_change: float32 [], replicated
The draws below stay inside these ranges and needn't reach their ends.
Inputs may be any that keep to these rules, and one draw needn't show every extreme that they name: `lengths`: each sequence's real tokens come first in its slot of 1024; at least one sequence fills its slot.
All inputs are finite; a program needn't handle non-finite values.
Results may differ from the reference program's by a relative error of at most 0.0095.
Values may be sent and summed in bfloat16 or wider, within the bound.
A program may use at most 256 MiB of HBM per device.

```python
import math
from functools import partial
import jax
import jax.numpy as jnp
import numpy as np
from jax import lax

D = 768
FF = 3072
HEAD = 64
VOCAB = 30720
SLOT = 1024
STEP = 8
PAIRS = 16
SEQS = 32


def draw_lengths(key, part):
    counts = jax.random.randint(key, (PAIRS * 2,), SLOT // 4, SLOT + 1)
    chosen = jax.random.randint(jax.random.fold_in(key, 7), (), 0, PAIRS * 2)
    filled = jnp.where(jnp.arange(PAIRS * 2) == chosen, SLOT, counts)
    return filled.reshape(PAIRS, 2).astype(jnp.int32)


def draw_norm_params(key, part):
    noise = jnp.clip(jax.random.normal(key, (6, D), jnp.float32), -4.0, 4.0)
    gain_rows = jnp.arange(6) % 2 == 0
    return jnp.where(gain_rows[:, None], 1.0 + 0.1 * noise, 0.2 * noise).astype(jnp.float32)


def touch_ends(values, key, smallest, largest):
    longest = values.shape.index(max(values.shape))
    spots = []
    for shift in (0, 1):
        where = [jax.random.randint(jax.random.fold_in(key, axis), (), 0, length) for axis, length in enumerate(values.shape)]
        where[longest] = (where[longest] + shift) % values.shape[longest]
        spots.append(tuple(where))
    return values.at[spots[0]].set(smallest).at[spots[1]].set(largest)


def block_levels(stream_key, dims, cuts, smallest, high):
    level = 1.0
    for dim, parts in cuts:
        steps = jax.random.uniform(jax.random.fold_in(jax.random.fold_in(stream_key, 6), dim), (parts,), jnp.float32, smallest / len(cuts), high / len(cuts))
        level = level * jnp.repeat(jnp.exp(steps), dims[dim] // parts).reshape((-1,) + (1,) * (len(dims) - 1 - dim))
    return level


def rank_bounds(count, slope):
    portions = [(1 << 20) // math.isqrt(rank ** slope) + 1 for rank in range(1, count + 1)]
    scale = 1 + sum(portions) // (1 << 30)
    return np.cumsum(np.array([max(1, weight // scale) for weight in portions]))


def ranked_ids(key, extent, number_of, skew):
    grid = rank_bounds(number_of, skew)
    ticket = jax.random.randint(jax.random.fold_in(key, 1), extent, 0, int(grid[number_of - 1]))
    rank = jnp.searchsorted(jnp.asarray(grid, jnp.int32), ticket, side="right")
    return jax.random.permutation(jax.random.fold_in(key, 2), number_of)[rank].astype(jnp.int32)


def scatter_about(own_key, shape, spread, limit, split=(), held_as=jnp.bfloat16):
    array = spread * jax.random.normal(own_key, shape, jnp.float32)
    if split:
        array = array * block_levels(own_key, shape, split, -0.22, 0.18)
    return jnp.clip(array, -limit, limit).astype(held_as)


def setup_inputs(seed: int = 0) -> dict:
    key_list = jax.random.split(jax.random.key(seed), 24)
    token_ids = touch_ends(ranked_ids(key_list[0], (SEQS, SLOT), VOCAB, 2), jax.random.fold_in(key_list[0], 3), 0, VOCAB - 1).astype(jnp.int32)
    lengths = draw_lengths(jax.random.fold_in(key_list[23], 71), 0)
    token_table = scatter_about(key_list[2], (VOCAB, D), 0.05, 0.75, ((0, 32),), jnp.float32)
    table_first = scatter_about(key_list[3], (VOCAB, D), (0.00004 / (VOCAB * D + 4 * D * D + 3 * D * FF) ** 0.5), 1.043081283569336e-07, ((0, 32),), jnp.float32)
    table_second = jnp.clip(jnp.exp(math.log(1.3321165188723977e-14) - 1.3862944 * jax.random.uniform(key_list[4], (VOCAB, D), jnp.float32) ** block_levels(key_list[4], (VOCAB, D), ((0, 32),), -0.2, 0.2)), 3.3302912971809942e-15, 1.3321165188723977e-14)
    qkv_weight = scatter_about(key_list[5], (D, 3, D), D ** -0.5, 0.21875, ((0, 16), (2, 2)), jnp.float32)
    qkv_first = scatter_about(key_list[6], (D, 3, D), (0.0003 / (VOCAB * D + 4 * D * D + 3 * D * FF) ** 0.5), 8.344650268554688e-07, ((0, 16), (2, 2)), jnp.float32)
    qkv_second = jnp.clip(jnp.exp(math.log(1.3321165400482214e-15) - 1.3862944 * jax.random.uniform(key_list[7], (D, 3, D), jnp.float32) ** block_levels(key_list[7], (D, 3, D), ((0, 16), (2, 2)), -0.2, 0.2)), 3.3302913501205534e-16, 1.3321165400482214e-15)
    out_weight = scatter_about(key_list[8], (D, D), (D // 32) ** -0.5, 1.25, ((0, 16), (1, 2)), jnp.float32)
    out_first = scatter_about(key_list[9], (D, D), (0.00006 / (VOCAB * D + 4 * D * D + 3 * D * FF) ** 0.5), 1.4901161193847656e-07, ((0, 16), (1, 2)), jnp.float32)
    out_second = jnp.clip(jnp.exp(math.log(4.359654094971752e-17) - 1.3862944 * jax.random.uniform(key_list[10], (D, D), jnp.float32) ** block_levels(key_list[10], (D, D), ((0, 16), (1, 2)), -0.2, 0.2)), 1.089913523742938e-17, 4.359654094971752e-17)
    gate_up_weight = scatter_about(key_list[11], (D, 2, FF), D ** -0.5, 0.21875, ((0, 16), (2, 2)), jnp.float32)
    gate_up_first = scatter_about(key_list[12], (D, 2, FF), (0.00017 / (VOCAB * D + 4 * D * D + 3 * D * FF) ** 0.5), 4.172325134277344e-07, ((0, 16), (2, 2)), jnp.float32)
    gate_up_second = jnp.clip(jnp.exp(math.log(3.5119433890107505e-16) - 1.3862944 * jax.random.uniform(key_list[13], (D, 2, FF), jnp.float32) ** block_levels(key_list[13], (D, 2, FF), ((0, 16), (2, 2)), -0.2, 0.2)), 8.779858472526876e-17, 3.5119433890107505e-16)
    down_weight = scatter_about(key_list[14], (D, FF), FF ** -0.5, 0.109375, ((0, 16), (1, 2)), jnp.float32)
    down_first = scatter_about(key_list[15], (D, FF), (0.00023 / (VOCAB * D + 4 * D * D + 3 * D * FF) ** 0.5), 5.960464477539062e-07, ((0, 16), (1, 2)), jnp.float32)
    down_second = jnp.clip(jnp.exp(math.log(6.660582700241107e-16) - 1.3862944 * jax.random.uniform(key_list[16], (D, FF), jnp.float32) ** block_levels(key_list[16], (D, FF), ((0, 16), (1, 2)), -0.2, 0.2)), 1.6651456750602767e-16, 6.660582700241107e-16)
    norm_params = draw_norm_params(jax.random.fold_in(key_list[23], 71), 0)
    norm_first = scatter_about(key_list[18], (6, D), (0.0004 / (VOCAB * D + 4 * D * D + 3 * D * FF) ** 0.5), 9.5367431640625e-07, (), jnp.float32)
    norm_second = jnp.clip(jnp.exp(jax.random.uniform(key_list[19], (6, D), jnp.float32, math.log(8.174351279179525e-16), math.log(3.26974051167181e-15))), 8.174351279179525e-16, 3.26974051167181e-15)
    log_inverse_warmth = jnp.clip(jax.random.uniform(key_list[20], (), jnp.float32, 2.0, 2.7), 2.0, 2.7)
    scale_first = scatter_about(key_list[21], (), (0.009 / (VOCAB * D + 4 * D * D + 3 * D * FF) ** 0.5), 2.288818359375e-05, (), jnp.float32)
    scale_second = jnp.clip(jnp.exp(jax.random.uniform(key_list[22], (), jnp.float32, math.log(3.027537595623464e-11), math.log(1.2110150382493856e-10))), 3.027537595623464e-11, 1.2110150382493856e-10)
    return dict(token_ids=token_ids, lengths=lengths, token_table=token_table, table_first=table_first, table_second=table_second, qkv_weight=qkv_weight, qkv_first=qkv_first, qkv_second=qkv_second, out_weight=out_weight, out_first=out_first, out_second=out_second, gate_up_weight=gate_up_weight, gate_up_first=gate_up_first, gate_up_second=gate_up_second, down_weight=down_weight, down_first=down_first, down_second=down_second, norm_params=norm_params, norm_first=norm_first, norm_second=norm_second, log_inverse_warmth=log_inverse_warmth, scale_first=scale_first, scale_second=scale_second)


@jax.custom_vjp
def low(v):
    return lax.optimization_barrier(v.astype(jnp.bfloat16)).astype(jnp.float32)

@jax.custom_vjp
def low_back(v):
    return v

def low_keep(v):
    return (low(v), None)

def low_pass(kept, grad):
    return (grad,)

def back_keep(v):
    return (v, None)

def back_low(kept, grad):
    return (low(grad),)
low.defvjp(low_keep, low_pass)
low_back.defvjp(back_keep, back_low)
highest = lax.Precision.HIGHEST
norm_epsilon = 1e-12
rope_base = 1000.0
beta_one = 0.9
beta_two = 0.999
adam_epsilon = 1e-08
learn_rate = 0.01
weight_decay = 0.01
clip_limit = 0.001
masked_score = -1e+30

def layer_norm(values, gain, shift):
    centered = values - lax.optimization_barrier(jnp.mean(values, axis=-1, keepdims=True))
    inverse = lax.rsqrt(lax.optimization_barrier(jnp.mean(centered * centered, axis=-1, keepdims=True)) + norm_epsilon)
    return centered * inverse * gain + shift

def rotary_tables(length, width):
    half_width = width // 2
    steps_half = jnp.arange(half_width, dtype=jnp.int32).astype(jnp.float32)
    frequency = rope_base ** (-2.0 * steps_half / width)
    positions = jnp.arange(length, dtype=jnp.int32).astype(jnp.float32)
    angles = positions[:, None] * frequency[None, :]
    return (jnp.cos(angles)[:, None, :], jnp.sin(angles)[:, None, :])

def rotate(values, cosine_table, sine_table):
    half_width = values.shape[-1] // 2
    leading = values[..., :half_width]
    trailing = values[..., half_width:]
    return jnp.concatenate([leading * cosine_table - trailing * sine_table, trailing * cosine_table + leading * sine_table], axis=-1)

def encode_pair(weights, batch_pair):
    table_low, qkv_low, out_low, gate_low, down_low, norm_rows = weights
    pair_ids, pair_lengths = batch_pair
    pair_lengths = pair_lengths.astype(jnp.int32)
    embedded = jnp.take(table_low, pair_ids.reshape(-1).astype(jnp.int32), axis=0)
    first_out = layer_norm(embedded, norm_rows[0], norm_rows[1])
    qkv = low_back(jnp.einsum('td,dkc->tkc', low(first_out), qkv_low, precision=highest))
    qkv_view = qkv.reshape(2, SLOT, 3, D // HEAD, HEAD)
    cosine_table, sine_table = rotary_tables(SLOT, HEAD)
    query_all = low(rotate(qkv_view[:, :, 0], cosine_table, sine_table))
    key_all = low(rotate(qkv_view[:, :, 1], cosine_table, sine_table))
    value_all = low(qkv_view[:, :, 2])
    scores = low_back(HEAD ** (-0.5) * jnp.einsum('sqhe,skhe->shqk', query_all, key_all, precision=highest))
    key_valid = jnp.arange(SLOT, dtype=jnp.int32)[None, :] < pair_lengths[:, None]
    scores = jnp.where(key_valid[:, None, None, :], scores, masked_score)
    attention = low(jax.nn.softmax(scores, axis=-1))
    mixed = low(low_back(jnp.einsum('shqk,skhe->sqhe', attention, value_all, precision=highest))).reshape(2 * SLOT, D)
    attended = low_back(jnp.einsum('tc,oc->to', mixed, out_low, precision=highest))
    second_out = layer_norm(first_out + attended, norm_rows[2], norm_rows[3])
    gate_up = low_back(jnp.einsum('td,dkf->tkf', low(second_out), gate_low, precision=highest))
    hidden = low(jax.nn.silu(gate_up[:, 0]) * gate_up[:, 1])
    branch = low_back(jnp.einsum('tf,of->to', hidden, down_low, precision=highest))
    third_out = layer_norm(second_out + branch, norm_rows[4], norm_rows[5]).reshape(2, SLOT, D)
    pooled = lax.optimization_barrier(jnp.sum(jnp.where(key_valid[:, :, None], third_out, 0.0), axis=1)) / pair_lengths[:, None].astype(jnp.float32)
    return pooled * lax.rsqrt(lax.optimization_barrier(jnp.sum(pooled * pooled, axis=-1, keepdims=True)) + norm_epsilon)

def forward(token_table, qkv_weight, out_weight, gate_up_weight, down_weight, norm_params, log_inverse_warmth, token_ids, lengths):
    weights = (low(token_table), low(qkv_weight), low(out_weight), low(gate_up_weight), low(down_weight), norm_params)
    vectors = lax.map(jax.checkpoint(partial(encode_pair, weights)), (token_ids.astype(jnp.int32).reshape(PAIRS, 2, SLOT), lengths.astype(jnp.int32)))
    queries = vectors[:, 0]
    documents = vectors[:, 1]
    cosine_match_matrix = jnp.exp(log_inverse_warmth) * jnp.dot(queries, documents.T, precision=highest)
    diagonal = jnp.diagonal(cosine_match_matrix)
    by_rows = jnp.mean(jax.nn.logsumexp(cosine_match_matrix, axis=1) - diagonal)
    by_columns = jnp.mean(jax.nn.logsumexp(cosine_match_matrix, axis=0) - diagonal)
    return 0.5 * (by_rows + by_columns)

def adam_step(weight, first_moment, second_moment, gradient, factor):
    clipped = gradient * factor
    first_next = beta_one * first_moment + (1.0 - beta_one) * clipped
    second_next = beta_two * second_moment + (1.0 - beta_two) * clipped * clipped
    corrected_first = first_next / (1.0 - beta_one ** STEP)
    corrected_second = second_next / (1.0 - beta_two ** STEP)
    change = -learn_rate * (corrected_first / (jnp.sqrt(corrected_second) + adam_epsilon) + weight_decay * weight)
    return (first_next, second_next, change)

def reference(token_ids, lengths, token_table, table_first, table_second, qkv_weight, qkv_first, qkv_second, out_weight, out_first, out_second, gate_up_weight, gate_up_first, gate_up_second, down_weight, down_first, down_second, norm_params, norm_first, norm_second, log_inverse_warmth, scale_first, scale_second):
    batch_loss, pullback = jax.vjp(partial(forward, token_ids=token_ids, lengths=lengths), token_table, qkv_weight, out_weight, gate_up_weight, down_weight, norm_params, log_inverse_warmth)
    grad_table, grad_qkv, grad_out, grad_gate, grad_down, grad_norms, grad_scale = pullback(jnp.ones_like(batch_loss))
    squares = jnp.sum(grad_table * grad_table) + jnp.sum(grad_qkv * grad_qkv) + jnp.sum(grad_out * grad_out)
    squares = squares + jnp.sum(grad_gate * grad_gate) + jnp.sum(grad_down * grad_down)
    squares = squares + jnp.sum(grad_norms * grad_norms) + grad_scale * grad_scale
    grad_norm = jnp.sqrt(squares)
    factor = jnp.minimum(1.0, clip_limit / (grad_norm + 1e-06))
    table_new = adam_step(token_table, table_first, table_second, grad_table, factor)
    qkv_new = adam_step(qkv_weight, qkv_first, qkv_second, grad_qkv, factor)
    out_new = adam_step(out_weight, out_first, out_second, grad_out, factor)
    gate_new = adam_step(gate_up_weight, gate_up_first, gate_up_second, grad_gate, factor)
    down_new = adam_step(down_weight, down_first, down_second, grad_down, factor)
    norm_new = adam_step(norm_params, norm_first, norm_second, grad_norms, factor)
    scale_new = adam_step(log_inverse_warmth, scale_first, scale_second, grad_scale, factor)
    return (batch_loss, grad_norm, table_new[0], table_new[1], table_new[2], qkv_new[0], qkv_new[1], qkv_new[2], out_new[0], out_new[1], out_new[2], gate_new[0], gate_new[1], gate_new[2], down_new[0], down_new[1], down_new[2], norm_new[0], norm_new[1], norm_new[2], scale_new[0], scale_new[1], scale_new[2])
```

```python
import functools

import jax
import jax.numpy as jnp
from jax import lax
from jax.experimental import pallas as pl
from jax.experimental.pallas import tpu as pltpu
from jax.sharding import PartitionSpec as P

HEAD = 64
STEP = 8

norm_epsilon = 1e-12
rope_base = 1000.0
beta_one = 0.9
beta_two = 0.999
adam_epsilon = 1e-08
learn_rate = 0.01
weight_decay = 0.01
clip_limit = 0.001
masked_score = -1e30

AXES = ("dp", "tensor")
F32 = jnp.float32
BF16 = jnp.bfloat16
LANES = 128
VMEM_LIMIT = 58 * 1024 * 1024
ROW_BLOCK = 256
HIDDEN_BLOCK = 256


class Plan:
    def __init__(self, mesh, width):
        self.dp = mesh.shape["dp"]
        self.tensor = mesh.shape["tensor"]
        self.count = self.dp * self.tensor
        self.shard = width // self.dp
        self.stepped = self.dp % 4 == 0 and self.shard % 16 == 0
        if self.stepped:
            self.nc, self.nx, self.nz = 2, 2, self.dp // 4
        else:
            self.nc, self.nx, self.nz = 1, 1, 1
        self.rows = width // (self.nc * self.nx * self.nz)

    def places(self):
        dp_index, tensor_index = lax.axis_index("dp"), lax.axis_index("tensor")
        if not self.stepped:
            zero = jnp.int32(0)
            return zero, zero, zero, zero
        core = lax.rem(dp_index, self.nc)
        across = lax.rem(dp_index // self.nc, self.nx)
        return dp_index // (self.nc * self.nx), across, core, tensor_index

    def size(self, axis):
        return {"z": self.nz, "x": self.nx, "c": self.nc, "y": self.tensor}[axis]

    def shift(self, values, axis, by):
        pairs = []
        for z in range(self.nz):
            for x in range(self.nx):
                for c in range(self.nc):
                    for y in range(self.tensor):
                        place = {"z": z, "x": x, "c": c, "y": y}
                        source = self.flat(place)
                        place[axis] = (place[axis] + by) % self.size(axis)
                        pairs.append((source, self.flat(place)))
        return lax.ppermute(values, AXES, pairs)

    def flat(self, place):
        dp_index = (place["z"] * self.nx + place["x"]) * self.nc + place["c"]
        return dp_index * self.tensor + place["y"]

    def gather(self, values, order):
        if not self.stepped:
            whole = lax.all_gather(values, ("tensor", "dp"), axis=0, tiled=True)
            shape = (self.tensor, 1) if order == "yx" else (1, self.tensor)
            return whole.reshape((1,) + shape + (1, self.rows, values.shape[1]))
        stack = values
        for axis in ("z",) + tuple(reversed(order)) + ("c",):
            parts = [stack]
            for far in range(1, self.size(axis)):
                parts.append(self.shift(stack, axis, -far))
            stack = jnp.stack(parts)
        return stack

    def scatter(self, parts, order, scale):
        if not self.stepped:
            whole = parts[0].reshape(self.tensor * self.rows, parts[0].shape[-1])
            return lax.psum_scatter(
                whole.astype(F32), ("tensor", "dp"), scatter_dimension=0, tiled=True
            )
        keep, send = parts
        total = keep.astype(F32) + self.shift(send, "c", 1).astype(F32)
        for axis in tuple(order) + ("z",):
            kept = total[0]
            for far in range(1, self.size(axis)):
                sent = (total[far] * scale).astype(jnp.float16)
                kept = kept + self.shift(sent, axis, far).astype(F32) / scale
            total = kept
        return total


    def weight_spec(self, order, columns, locate):
        def index(i, place):
            part, column = locate(i)
            far = lax.rem(part - place[3] + self.tensor, self.tensor)
            if order == "yx":
                return (0, far, 0, 0, 0, column)
            return (0, 0, far, 0, 0, column)

        middle = (None, self.nx) if order == "yx" else (self.nx, None)
        return pl.BlockSpec((self.nc,) + middle + (self.nz, self.rows, columns), index)

    def grad_specs(self, order, columns, locate):
        def index(i, place):
            part, column = locate(i)
            far = lax.rem(part - place[3] + self.tensor, self.tensor)
            if order == "yx":
                return (far, 0, 0, 0, column)
            return (0, far, 0, 0, column)

        middle = (None, self.nx) if order == "yx" else (self.nx, None)
        spec = pl.BlockSpec(middle + (self.nz, self.rows, columns), index)
        return [spec] * self.nc

    def grad_shapes(self, order, columns):
        middle = (self.tensor, self.nx) if order == "yx" else (self.nx, self.tensor)
        shape = middle + (self.nz, self.rows, columns)
        return [jax.ShapeDtypeStruct(shape, F32)] * self.nc

    def assemble(self, place, block, target, first_column):
        columns = block.shape[-1]
        for z in range(self.nz):
            far_z = lax.rem(z - place[0] + self.nz, self.nz)
            for x in range(self.nx):
                far_x = lax.rem(x - place[1] + self.nx, self.nx)
                for c in range(self.nc):
                    far_c = lax.rem(c - place[2] + self.nc, self.nc)
                    start = ((z * self.nx + x) * self.nc + c) * self.rows
                    target[start : start + self.rows, first_column : first_column + columns] = (
                        block[far_c, far_x, far_z]
                    )

    def disperse(self, place, source, first_column, targets):
        columns = targets[0].shape[-1]
        for far_z in range(self.nz):
            z = lax.rem(place[0] + far_z, self.nz)
            for far_x in range(self.nx):
                x = lax.rem(place[1] + far_x, self.nx)
                for far_c in range(self.nc):
                    c = lax.rem(place[2] + far_c, self.nc)
                    start = ((z * self.nx + x) * self.nc + c) * self.rows
                    start = pl.multiple_of(start, 16)
                    targets[far_c][far_x, far_z] = source[
                        pl.ds(start, self.rows), first_column : first_column + columns
                    ]


def dot(left, right):
    return lax.dot_general(left, right, (((1,), (0,)), ((), ())), preferred_element_type=F32)


def dot_last(left, right):
    return lax.dot_general(left, right, (((1,), (1,)), ((), ())), preferred_element_type=F32)


def normalize(values):
    centered = values - jnp.mean(values, axis=-1, keepdims=True)
    inverse = lax.rsqrt(jnp.mean(centered * centered, axis=-1, keepdims=True) + norm_epsilon)
    return centered * inverse, inverse


def normalize_back(grad_output, normal, inverse, gain):
    grad_normal = grad_output * gain
    mean_grad = jnp.mean(grad_normal, axis=-1, keepdims=True)
    mean_cross = jnp.mean(grad_normal * normal, axis=-1, keepdims=True)
    return inverse * (grad_normal - mean_grad - normal * mean_cross)


def rotary_tables(length):
    half_width = HEAD // 2
    steps_half = jnp.arange(half_width, dtype=jnp.int32).astype(F32)
    frequency = rope_base ** (-2.0 * steps_half / HEAD)
    positions = jnp.arange(length, dtype=jnp.int32).astype(F32)
    angles = positions[:, None] * frequency[None, :]
    cosine, sine = jnp.cos(angles), jnp.sin(angles)
    heads = LANES // HEAD
    return (
        jnp.concatenate([cosine, cosine] * heads, axis=1),
        jnp.concatenate([-sine, sine] * heads, axis=1),
    )


def swap_halves(values):
    lane = lax.broadcasted_iota(jnp.int32, values.shape, 1)
    ahead = pltpu.roll(values, LANES - HEAD // 2, 1)
    behind = pltpu.roll(values, HEAD // 2, 1)
    return jnp.where(lax.rem(lane, HEAD) < HEAD // 2, ahead, behind)


def of_head(values, head):
    lane = lax.broadcasted_iota(jnp.int32, values.shape, 1)
    return jnp.where(lane // HEAD == head, values, jnp.zeros_like(values))


def note_peak(peak_out, product):
    largest = jnp.max(jnp.abs(product[...]), axis=0, keepdims=True)
    largest = jnp.broadcast_to(jnp.max(largest, axis=1, keepdims=True), peak_out.shape)

    @pl.when(pl.program_id(0) == 0)
    def _():
        peak_out[...] = largest

    @pl.when(pl.program_id(0) > 0)
    def _():
        peak_out[...] = jnp.maximum(peak_out[...], largest)


def params(**more):
    return pltpu.CompilerParams(vmem_limit_bytes=VMEM_LIMIT, **more)


def whole(shape):
    zeros = (0,) * len(shape)
    return pl.BlockSpec(shape, lambda i, place: zeros, pipeline_mode=pl.Buffered(1))


def result(shape):
    zeros = (0,) * len(shape)
    return pl.BlockSpec(shape, lambda i, place: zeros)


def exchange_partner(me, step):
    distance = 1 << step
    return me + distance - 2 * distance * lax.rem(me // distance, 2)


def exchange_barrier(me, steps, tensor):
    barrier = pltpu.get_barrier_semaphore()
    for step in range(steps):
        partner = exchange_partner(me, step)
        pl.semaphore_signal(
            barrier,
            inc=1,
            device_id=(partner // tensor, lax.rem(partner, tensor)),
            device_id_type=pl.DeviceIdType.MESH,
        )
    pl.semaphore_wait(barrier, steps)


def exchange_blocks(me, steps, tensor, held, send_sem, recv_sem):
    for step in range(steps):
        partner = exchange_partner(me, step)
        size = 1 << step
        base = (me // size) * size
        copy = pltpu.make_async_remote_copy(
            src_ref=held.at[pl.ds(base, size)],
            dst_ref=held.at[pl.ds(base, size)],
            send_sem=send_sem.at[step],
            recv_sem=recv_sem.at[step],
            device_id=(partner // tensor, lax.rem(partner, tensor)),
            device_id_type=pl.DeviceIdType.MESH,
        )
        copy.start()
        copy.wait()


def share_kernel(steps, tensor, block_ref, out_ref, held, send_sem, recv_sem):
    me = lax.axis_index("dp") * tensor + lax.axis_index("tensor")
    exchange_barrier(me, steps, tensor)
    held[pl.ds(me, 1)] = block_ref[...][None]
    exchange_blocks(me, steps, tensor, held, send_sem, recv_sem)
    out_ref[...] = held[...]


def share(plan, block):
    steps = plan.count.bit_length() - 1
    shape = (plan.count,) + block.shape
    return pl.pallas_call(
        functools.partial(share_kernel, steps, plan.tensor),
        name="share",
        out_shape=jax.ShapeDtypeStruct(shape, block.dtype),
        in_specs=[pl.BlockSpec(memory_space=pltpu.VMEM)],
        out_specs=pl.BlockSpec(memory_space=pltpu.VMEM),
        scratch_shapes=[
            pltpu.VMEM(shape, block.dtype),
            pltpu.SemaphoreType.DMA((steps,)),
            pltpu.SemaphoreType.DMA((steps,)),
        ],
        compiler_params=params(collective_id=0, has_side_effects=True),
    )(block)


def total_kernel(steps, tensor, block_ref, out_ref, held, came, send_sem, recv_sem):
    me = lax.axis_index("dp") * tensor + lax.axis_index("tensor")
    exchange_barrier(me, steps, tensor)
    held[0] = block_ref[...]
    for step in range(steps):
        partner = exchange_partner(me, step)
        copy = pltpu.make_async_remote_copy(
            src_ref=held.at[step],
            dst_ref=came.at[step],
            send_sem=send_sem.at[step],
            recv_sem=recv_sem.at[step],
            device_id=(partner // tensor, lax.rem(partner, tensor)),
            device_id_type=pl.DeviceIdType.MESH,
        )
        copy.start()
        copy.wait()
        held[step + 1] = held[step] + came[step]
    out_ref[...] = held[steps]


def total(plan, block, collective_id):
    steps = plan.count.bit_length() - 1
    return pl.pallas_call(
        functools.partial(total_kernel, steps, plan.tensor),
        name="total",
        out_shape=jax.ShapeDtypeStruct(block.shape, block.dtype),
        in_specs=[pl.BlockSpec(memory_space=pltpu.VMEM)],
        out_specs=pl.BlockSpec(memory_space=pltpu.VMEM),
        scratch_shapes=[
            pltpu.VMEM((steps + 1,) + block.shape, block.dtype),
            pltpu.VMEM((steps,) + block.shape, block.dtype),
            pltpu.SemaphoreType.DMA((steps,)),
            pltpu.SemaphoreType.DMA((steps,)),
        ],
        compiler_params=params(collective_id=collective_id, has_side_effects=True),
    )(block)


def wire_scale(plan, peak):
    bound = total(plan, peak, 3)[0, 0]
    exponent = jnp.floor(jnp.log2(32768.0 / jnp.maximum(bound, 1e-30)))
    return jnp.exp2(jnp.clip(exponent, -60.0, 60.0))


def token_places(slot_ids, length, vocab_shard):
    count = slot_ids.shape[0]
    order = jnp.arange(count, dtype=jnp.int32)
    key = jnp.where(order < length, slot_ids, -1)
    owner = key // vocab_shard
    row = key - owner * vocab_shard
    same = key[:, None] == key[None, :]
    first_at = jnp.min(jnp.where(same, order[None, :], count), axis=1)
    first = (first_at == order) & (key >= 0)
    earlier = first[None, :] & (owner[:, None] == owner[None, :])
    place = jnp.sum(
        (earlier & (order[None, :] < first_at[:, None])).astype(jnp.int32), axis=1
    )
    return owner, row, first, jnp.where(key >= 0, place, -1)


def round_slots(owner, place, room, turn):
    within = place - turn * room
    served = (within >= 0) & (within < room)
    return jnp.where(served, owner * room + within, -1)


def round_wants(slot, first, row, slots):
    wanted = first[None, :] & (slot[None, :] == jnp.arange(slots, dtype=jnp.int32)[:, None])
    return jnp.max(jnp.where(wanted, row[None, :], -1), axis=1)


def picked_rows(wants, table_low):
    chosen = wants.reshape(-1)[:, None] == jnp.arange(table_low.shape[0], dtype=jnp.int32)[None, :]
    return jnp.dot(chosen.astype(BF16), table_low, preferred_element_type=F32).astype(BF16)


def spread_rows(slot, rows):
    chosen = slot[:, None] == jnp.arange(rows.shape[0], dtype=jnp.int32)[None, :]
    return jnp.dot(chosen.astype(BF16), rows, preferred_element_type=F32)


def summed_rows(index, rows, count):
    chosen = jnp.arange(count, dtype=jnp.int32)[:, None] == index[None, :]
    return jnp.dot(chosen.astype(BF16), rows, preferred_element_type=F32)


def swap_rows(plan, rows):
    parts = rows.reshape(plan.count, rows.shape[0] // plan.count, rows.shape[1])
    return lax.all_to_all(parts, AXES, 0, 0, tiled=True).reshape(rows.shape)


def attend_kernel(plan, place, x, wq, wk, wv, cosine, sine, q, k, v, mixed, log_total, weights):
    rows = x.shape[0]
    plan.assemble(place, wq, weights, 0)
    plan.assemble(place, wk, weights, LANES)
    plan.assemble(place, wv, weights, 2 * LANES)
    for start in range(0, rows, ROW_BLOCK):
        at = slice(start, start + ROW_BLOCK)
        made = dot(x[at, :], weights[...])
        query, key = made[:, :LANES], made[:, LANES : 2 * LANES]
        query = query * cosine[at, :] + swap_halves(query) * sine[at, :]
        key = key * cosine[at, :] + swap_halves(key) * sine[at, :]
        q[at, :] = (query * HEAD**-0.5).astype(BF16)
        k[at, :] = key.astype(BF16)
        v[at, :] = made[:, 2 * LANES :].astype(BF16)
    position = lax.broadcasted_iota(jnp.int32, (rows, 1), 0)
    bias = jnp.where(position < place[4], 0.0, masked_score)
    keys = k[...]
    values = v[...].T
    for start in range(0, rows, ROW_BLOCK):
        at = slice(start, start + ROW_BLOCK)
        outs = []
        for head in range(LANES // HEAD):
            scores = dot_last(keys, of_head(q[at, :], head)) + bias
            top = jnp.max(scores, axis=0, keepdims=True)
            exponent = jnp.exp(scores - top)
            summed = jnp.sum(exponent, axis=0, keepdims=True)
            out = dot(values[head * HEAD : (head + 1) * HEAD, :], exponent.astype(BF16))
            outs.append(out / summed)
            log_total[head : head + 1, at] = top + jnp.log(summed)
        mixed[at, :] = jnp.concatenate(outs, axis=0).T.astype(BF16)


def attend(plan, place, x, wq, wk, wv, cosine, sine):
    rows, width = x.shape
    pairs = wq.shape[-1] // LANES
    steps = plan.tensor * pairs

    def locate(i):
        return i // pairs, lax.rem(i, pairs)

    by_pair = pl.BlockSpec((None, rows, LANES), lambda i, place: (i, 0, 0))
    shape = jax.ShapeDtypeStruct((steps, rows, LANES), BF16)
    return pl.pallas_call(
        functools.partial(attend_kernel, plan),
        name="attend",
        out_shape=[
            shape,
            shape,
            shape,
            jax.ShapeDtypeStruct((rows, steps * LANES), BF16),
            jax.ShapeDtypeStruct((steps, 8, rows), F32),
        ],
        grid_spec=pltpu.PrefetchScalarGridSpec(
            num_scalar_prefetch=1,
            grid=(steps,),
            in_specs=[
                whole((rows, width)),
                plan.weight_spec("yx", LANES, locate),
                plan.weight_spec("xy", LANES, locate),
                plan.weight_spec("yx", LANES, locate),
                whole((rows, LANES)),
                whole((rows, LANES)),
            ],
            out_specs=[
                by_pair,
                by_pair,
                by_pair,
                pl.BlockSpec((rows, LANES), lambda i, place: (0, i)),
                pl.BlockSpec((None, 8, rows), lambda i, place: (i, 0, 0)),
            ],
            scratch_shapes=[pltpu.VMEM((width, 3 * LANES), BF16)],
        ),
        compiler_params=params(),
        cost_estimate=pl.CostEstimate(
            flops=2 * rows * width * 3 * width + 16 * rows * rows * width,
            bytes_accessed=rows * width * 12,
            transcendentals=0,
        ),
    )(place, x, wq, wk, wv, cosine, sine)


def project_kernel(plan, place, mixed, wo, normal_one, norms, low_out, normal_out, inverse_out, weights):
    rows, width = mixed.shape
    part = wo.shape[-1]
    plan.assemble(place, wo, weights, 0)
    first = pl.program_id(0) == 0

    for start in range(0, rows, ROW_BLOCK):
        at = slice(start, start + ROW_BLOCK)
        product = dot_last(mixed[at, :], weights[...])

        @pl.when(first)
        def _():
            normal_out[at, :] = product

        @pl.when(jnp.logical_not(first))
        def _():
            normal_out[at, :] = normal_out[at, :] + product

    @pl.when(pl.program_id(0) == pl.num_programs(0) - 1)
    def _():
        for start in range(0, rows, ROW_BLOCK):
            at = slice(start, start + ROW_BLOCK)
            first_out = normal_one[at, :] * norms[0:1, :] + norms[1:2, :]
            normal, inverse = normalize(first_out + normal_out[at, :])
            normal_out[at, :] = normal
            inverse_out[at, :] = inverse
            low_out[at, :] = (normal * norms[2:3, :] + norms[3:4, :]).astype(BF16)


def project(plan, place, mixed, wo, normal_one, norms):
    rows, width = mixed.shape
    part = wo.shape[-1]
    return pl.pallas_call(
        functools.partial(project_kernel, plan),
        name="project",
        out_shape=[
            jax.ShapeDtypeStruct((rows, width), BF16),
            jax.ShapeDtypeStruct((rows, width), F32),
            jax.ShapeDtypeStruct((rows, 1), F32),
        ],
        grid_spec=pltpu.PrefetchScalarGridSpec(
            num_scalar_prefetch=1,
            grid=(plan.tensor,),
            in_specs=[
                pl.BlockSpec((rows, part), lambda i, place: (0, i)),
                plan.weight_spec("xy", part, lambda i: (i, 0)),
                whole((rows, width)),
                whole(norms.shape),
            ],
            out_specs=[result((rows, width)), result((rows, width)), result((rows, 1))],
            scratch_shapes=[pltpu.VMEM((width, part), BF16)],
        ),
        compiler_params=params(),
        cost_estimate=pl.CostEstimate(
            flops=2 * rows * width * width, bytes_accessed=rows * width * 14, transcendentals=0
        ),
    )(place, mixed, wo, normal_one, norms)


def feed_kernel(
    plan,
    place,
    x,
    wg,
    wu,
    wd,
    normal_two,
    norms,
    gate_out,
    up_out,
    hidden_out,
    normal_out,
    inverse_out,
    pool_out,
    weights,
    down,
):
    rows, width = x.shape
    plan.assemble(place, wg, weights, 0)
    plan.assemble(place, wu, weights, HIDDEN_BLOCK)
    plan.assemble(place, wd, down, 0)
    first = pl.program_id(0) == 0

    @pl.when(first)
    def _():
        normal_out[...] = jnp.zeros_like(normal_out)

    for start in range(0, rows, ROW_BLOCK):
        at = slice(start, start + ROW_BLOCK)
        made = dot(x[at, :], weights[...])
        gate, up = made[:, :HIDDEN_BLOCK], made[:, HIDDEN_BLOCK:]
        hidden = (gate * jax.nn.sigmoid(gate) * up).astype(BF16)
        gate_out[at, :] = gate.astype(BF16)
        up_out[at, :] = up.astype(BF16)
        hidden_out[at, :] = hidden
        normal_out[at, :] = normal_out[at, :] + dot_last(hidden, down[...])

    @pl.when(pl.program_id(0) == pl.num_programs(0) - 1)
    def _():
        pooled = jnp.zeros((1, width), F32)
        for start in range(0, rows, ROW_BLOCK):
            at = slice(start, start + ROW_BLOCK)
            second_out = normal_two[at, :] * norms[2:3, :] + norms[3:4, :]
            normal, inverse = normalize(second_out + normal_out[at, :])
            normal_out[at, :] = normal
            inverse_out[at, :] = inverse
            position = start + lax.broadcasted_iota(jnp.int32, (ROW_BLOCK, 1), 0)
            kept = jnp.where(position < place[4], normal, 0.0)
            pooled = pooled + jnp.sum(kept, axis=0, keepdims=True)
        pool_out[...] = pooled


def feed(plan, place, x, wg, wu, wd, normal_two, norms):
    rows, width = x.shape
    hidden = wg.shape[-1]
    chunks = hidden // HIDDEN_BLOCK
    steps = plan.tensor * chunks

    def locate(i):
        return i // chunks, lax.rem(i, chunks)

    by_chunk = pl.BlockSpec((rows, HIDDEN_BLOCK), lambda i, place: (0, i))
    shape = jax.ShapeDtypeStruct((rows, plan.tensor * hidden), BF16)
    return pl.pallas_call(
        functools.partial(feed_kernel, plan),
        name="feed",
        out_shape=[
            shape,
            shape,
            shape,
            jax.ShapeDtypeStruct((rows, width), F32),
            jax.ShapeDtypeStruct((rows, 1), F32),
            jax.ShapeDtypeStruct((1, width), F32),
        ],
        grid_spec=pltpu.PrefetchScalarGridSpec(
            num_scalar_prefetch=1,
            grid=(steps,),
            in_specs=[
                whole((rows, width)),
                plan.weight_spec("yx", HIDDEN_BLOCK, locate),
                plan.weight_spec("xy", HIDDEN_BLOCK, locate),
                plan.weight_spec("xy", HIDDEN_BLOCK, locate),
                whole((rows, width)),
                whole(norms.shape),
            ],
            out_specs=[
                by_chunk,
                by_chunk,
                by_chunk,
                result((rows, width)),
                result((rows, 1)),
                result((1, width)),
            ],
            scratch_shapes=[
                pltpu.VMEM((width, 2 * HIDDEN_BLOCK), BF16),
                pltpu.VMEM((width, HIDDEN_BLOCK), BF16),
            ],
        ),
        compiler_params=params(),
        cost_estimate=pl.CostEstimate(
            flops=6 * rows * width * plan.tensor * hidden,
            bytes_accessed=rows * width * 40,
            transcendentals=0,
        ),
    )(place, x, wg, wu, wd, normal_two, norms)


def contrast_kernel(
    steps, tensor, place, pool_ref, norms, scale_ref, loss_ref, grad_ref, held, send_sem, recv_sem
):
    count = held.shape[0]
    me = lax.axis_index("dp") * tensor + lax.axis_index("tensor")
    exchange_barrier(me, steps, tensor)
    length = jnp.full((1, 1), place[4], jnp.int32).astype(F32)
    pooled = pool_ref[...] / length * norms[4:5, :] + norms[5:6, :]
    inverse = lax.rsqrt(jnp.sum(pooled * pooled, axis=-1, keepdims=True) + norm_epsilon)
    vector = pooled * inverse
    held[pl.ds(me, 1)] = vector[None]
    exchange_blocks(me, steps, tensor, held, send_sem, recv_sem)
    vectors = held[...].reshape(count, held.shape[2])
    scale = jnp.exp(scale_ref[...])
    logits = scale * lax.dot_general(
        vectors,
        vectors,
        (((1,), (1,)), ((), ())),
        precision=lax.Precision.HIGHEST,
        preferred_element_type=F32,
    )
    row = lax.broadcasted_iota(jnp.int32, (count, count), 0)
    column = lax.broadcasted_iota(jnp.int32, (count, count), 1)
    crossed = (lax.rem(row, 2) == 0) & (lax.rem(column, 2) == 1)
    shown = jnp.where(crossed, logits, masked_score)
    row_max = jnp.max(shown, axis=1, keepdims=True)
    row_exp = jnp.where(crossed, jnp.exp(shown - row_max), 0.0)
    row_sum = jnp.sum(row_exp, axis=1, keepdims=True)
    column_max = jnp.max(shown, axis=0, keepdims=True)
    column_exp = jnp.where(crossed, jnp.exp(shown - column_max), 0.0)
    column_sum = jnp.sum(column_exp, axis=0, keepdims=True)
    even = lax.rem(lax.broadcasted_iota(jnp.int32, (count, 1), 0), 2) == 0
    odd = lax.rem(lax.broadcasted_iota(jnp.int32, (1, count), 1), 2) == 1
    row_safe = jnp.where(even, row_sum, 1.0)
    column_safe = jnp.where(odd, column_sum, 1.0)
    row_lse = jnp.where(even, row_max + jnp.log(row_safe), 0.0)
    column_lse = jnp.where(odd, column_max + jnp.log(column_safe), 0.0)
    own = crossed & (column == row + 1)
    diagonal = jnp.sum(jnp.where(own, logits, 0.0))
    half = 1.0 / count
    loss = half * (jnp.sum(row_lse) + jnp.sum(column_lse) - 2.0 * diagonal)
    grad_logits = half * (
        row_exp / row_safe + column_exp / column_safe - 2.0 * own.astype(F32)
    )
    grad_scale = jnp.sum(grad_logits * jnp.where(crossed, logits, 0.0))
    both = grad_logits + grad_logits.T
    grad_vectors = scale * lax.dot_general(
        both,
        vectors,
        (((1,), (0,)), ((), ())),
        precision=lax.Precision.HIGHEST,
        preferred_element_type=F32,
    )
    mine = lax.broadcasted_iota(jnp.int32, (count, 1), 0) == me
    grad_own = jnp.sum(jnp.where(mine, grad_vectors, 0.0), axis=0, keepdims=True)
    along = jnp.sum(grad_own * vector, axis=-1, keepdims=True)
    grad_ref[...] = inverse * (grad_own - vector * along) / length
    lane = lax.broadcasted_iota(jnp.int32, loss_ref.shape, 1)
    loss_ref[...] = jnp.where(lane == 0, loss, grad_scale)


def contrast(plan, place, pool, norms, log_scale):
    steps = plan.count.bit_length() - 1
    width = pool.shape[1]
    in_vmem = pl.BlockSpec(memory_space=pltpu.VMEM)
    loss, grad = pl.pallas_call(
        functools.partial(contrast_kernel, steps, plan.tensor),
        name="contrast",
        out_shape=[
            jax.ShapeDtypeStruct((1, LANES), F32),
            jax.ShapeDtypeStruct((1, width), F32),
        ],
        in_specs=[pl.BlockSpec(memory_space=pltpu.SMEM), in_vmem, in_vmem, in_vmem],
        out_specs=[in_vmem, in_vmem],
        scratch_shapes=[
            pltpu.VMEM((plan.count, 1, width), F32),
            pltpu.SemaphoreType.DMA((steps,)),
            pltpu.SemaphoreType.DMA((steps,)),
        ],
        compiler_params=params(collective_id=2, has_side_effects=True),
    )(place, pool, norms, log_scale.reshape(1, 1))
    return loss[0, 0], loss[0, 1], grad


def feed_back_body(plan, place, *refs):
    (
        grad_pool,
        x,
        gate_ref,
        up_ref,
        hidden_ref,
        wg,
        wu,
        wd,
        normal_three,
        inverse_three,
        normal_two,
        inverse_two,
        norms,
    ) = refs[:13]
    nc = plan.nc
    gate_grads = refs[13 : 13 + nc]
    up_grads = refs[13 + nc : 13 + 2 * nc]
    down_grads = refs[13 + 2 * nc : 13 + 3 * nc]
    grad_out, low_out, norm_out, peak_out = refs[13 + 3 * nc : 17 + 3 * nc]
    low, low_turned, x_turned, weights, down, made, product = refs[17 + 3 * nc :]
    rows, width = x.shape

    @pl.when(pl.program_id(0) == 0)
    def _():
        for start in range(0, rows, ROW_BLOCK):
            at = slice(start, start + ROW_BLOCK)
            position = start + lax.broadcasted_iota(jnp.int32, (ROW_BLOCK, 1), 0)
            grad_third = jnp.where(position < place[4], grad_pool[...], 0.0)
            grad = normalize_back(
                grad_third, normal_three[at, :], inverse_three[at, :], norms[4:5, :]
            )
            grad_out[at, :] = grad
            low[at, :] = grad.astype(BF16)
            low_turned[:, at] = grad.astype(BF16).T
            x_turned[:, at] = x[at, :].T

    plan.assemble(place, wg, weights, 0)
    plan.assemble(place, wu, weights, HIDDEN_BLOCK)
    plan.assemble(place, wd, down, 0)
    for start in range(0, rows, ROW_BLOCK):
        at = slice(start, start + ROW_BLOCK)
        grad_hidden = dot(low[at, :], down[...])
        gate = gate_ref[at, :].astype(F32)
        up = up_ref[at, :].astype(F32)
        share_gate = jax.nn.sigmoid(gate)
        grad_up = grad_hidden * gate * share_gate
        grad_gate = grad_hidden * up * share_gate * (1.0 + gate * (1.0 - share_gate))
        made[at, :HIDDEN_BLOCK] = grad_gate.astype(BF16)
        made[at, HIDDEN_BLOCK:] = grad_up.astype(BF16)
        grad_out[at, :] = grad_out[at, :] + dot_last(made[at, :], weights[...])
    product[:, : 2 * HIDDEN_BLOCK] = dot(x_turned[...], made[...])
    product[:, 2 * HIDDEN_BLOCK :] = dot(low_turned[...], hidden_ref[...])
    note_peak(peak_out, product)
    plan.disperse(place, product, 0, gate_grads)
    plan.disperse(place, product, HIDDEN_BLOCK, up_grads)
    plan.disperse(place, product, 2 * HIDDEN_BLOCK, down_grads)

    @pl.when(pl.program_id(0) == pl.num_programs(0) - 1)
    def _():
        gain_grad = jnp.zeros((1, width), F32)
        shift_grad = jnp.zeros((1, width), F32)
        for start in range(0, rows, ROW_BLOCK):
            at = slice(start, start + ROW_BLOCK)
            grad_second = grad_out[at, :]
            normal = normal_two[at, :]
            grad = normalize_back(grad_second, normal, inverse_two[at, :], norms[2:3, :])
            gain_grad = gain_grad + jnp.sum(grad_second * normal, axis=0, keepdims=True)
            shift_grad = shift_grad + jnp.sum(grad_second, axis=0, keepdims=True)
            grad_out[at, :] = grad
            low_out[at, :] = grad.astype(BF16)
        norm_out[0:1, :] = gain_grad
        norm_out[1:2, :] = shift_grad


def feed_back(
    plan,
    place,
    grad_pool,
    x,
    gate,
    up,
    hidden_low,
    wg,
    wu,
    wd,
    normal_three,
    inverse_three,
    normal_two,
    inverse_two,
    norms,
):
    rows, width = x.shape
    hidden = wg.shape[-1]
    chunks = hidden // HIDDEN_BLOCK
    steps = plan.tensor * chunks

    def locate(i):
        return i // chunks, lax.rem(i, chunks)

    by_chunk = pl.BlockSpec((rows, HIDDEN_BLOCK), lambda i, place: (0, i))
    outs = pl.pallas_call(
        functools.partial(feed_back_body, plan),
        name="feed_back",
        out_shape=plan.grad_shapes("yx", hidden)
        + plan.grad_shapes("xy", hidden)
        + plan.grad_shapes("xy", hidden)
        + [
            jax.ShapeDtypeStruct((rows, width), F32),
            jax.ShapeDtypeStruct((rows, width), BF16),
            jax.ShapeDtypeStruct((8, width), F32),
            jax.ShapeDtypeStruct((8, LANES), F32),
        ],
        grid_spec=pltpu.PrefetchScalarGridSpec(
            num_scalar_prefetch=1,
            grid=(steps,),
            in_specs=[
                whole((1, width)),
                whole((rows, width)),
                by_chunk,
                by_chunk,
                by_chunk,
                plan.weight_spec("yx", HIDDEN_BLOCK, locate),
                plan.weight_spec("xy", HIDDEN_BLOCK, locate),
                plan.weight_spec("xy", HIDDEN_BLOCK, locate),
                whole((rows, width)),
                whole((rows, 1)),
                whole((rows, width)),
                whole((rows, 1)),
                whole(norms.shape),
            ],
            out_specs=plan.grad_specs("yx", HIDDEN_BLOCK, locate)
            + plan.grad_specs("xy", HIDDEN_BLOCK, locate)
            + plan.grad_specs("xy", HIDDEN_BLOCK, locate)
            + [
                result((rows, width)),
                result((rows, width)),
                result((8, width)),
                result((8, LANES)),
            ],
            scratch_shapes=[
                pltpu.VMEM((rows, width), BF16),
                pltpu.VMEM((width, rows), BF16),
                pltpu.VMEM((width, rows), BF16),
                pltpu.VMEM((width, 2 * HIDDEN_BLOCK), BF16),
                pltpu.VMEM((width, HIDDEN_BLOCK), BF16),
                pltpu.VMEM((rows, 2 * HIDDEN_BLOCK), BF16),
                pltpu.VMEM((width, 3 * HIDDEN_BLOCK), F32),
            ],
        ),
        compiler_params=params(),
        cost_estimate=pl.CostEstimate(
            flops=12 * rows * width * plan.tensor * hidden,
            bytes_accessed=rows * width * 60,
            transcendentals=0,
        ),
    )(
        place,
        grad_pool,
        x,
        gate,
        up,
        hidden_low,
        wg,
        wu,
        wd,
        normal_three,
        inverse_three,
        normal_two,
        inverse_two,
        norms,
    )
    nc = plan.nc
    return (outs[:nc], outs[nc : 2 * nc], outs[2 * nc : 3 * nc]) + tuple(outs[3 * nc :])


def attend_back_kernel(plan, place, *refs):
    (
        ga,
        x,
        q,
        k,
        v,
        mixed,
        log_total,
        wq,
        wk,
        wv,
        wo,
        cosine,
        sine,
        grad_res,
        normal_one,
        inverse_one,
        norms,
    ) = refs[:17]
    nc = plan.nc
    grads = [refs[17 + n * nc : 17 + (n + 1) * nc] for n in range(4)]
    low_out, norm_out, peak_out = refs[17 + 4 * nc : 20 + 4 * nc]
    (
        ga_turned,
        x_turned,
        weights,
        out_weights,
        total_grad,
        gm,
        made,
        key_grad,
        value_grad,
        product,
    ) = refs[20 + 4 * nc :]
    rows, width = x.shape

    @pl.when(pl.program_id(0) == 0)
    def _():
        for start in range(0, rows, ROW_BLOCK):
            at = slice(start, start + ROW_BLOCK)
            ga_turned[:, at] = ga[at, :].T
            x_turned[:, at] = x[at, :].T
            total_grad[at, :] = grad_res[at, :]

    plan.assemble(place, wq, weights, 0)
    plan.assemble(place, wk, weights, LANES)
    plan.assemble(place, wv, weights, 2 * LANES)
    plan.assemble(place, wo, out_weights, 0)
    for start in range(0, rows, ROW_BLOCK):
        at = slice(start, start + ROW_BLOCK)
        gm[at, :] = dot(ga[at, :], out_weights[...]).astype(BF16)
    position = lax.broadcasted_iota(jnp.int32, (rows, 1), 0)
    bias = jnp.where(position < place[4], 0.0, masked_score)
    keys, values = k[...], v[...]
    keys_turned = keys.T
    for start in range(0, rows, ROW_BLOCK):
        at = slice(start, start + ROW_BLOCK)
        inner = (gm[at, :].astype(F32) * mixed[at, :].astype(F32)).T
        outs = []
        for head in range(LANES // HEAD):
            of = slice(head * HEAD, (head + 1) * HEAD)
            query = of_head(q[at, :], head)
            grad = of_head(gm[at, :], head)
            inner_sum = jnp.sum(inner[of, :], axis=0, keepdims=True)
            scores = dot_last(keys, query) + bias
            probs = jnp.exp(scores - log_total[head : head + 1, at])
            grad_probs = dot_last(values, grad)
            grad_scores = (probs * (grad_probs - inner_sum)).astype(BF16)
            value_part = dot(probs.astype(BF16), grad)
            key_part = dot(grad_scores, query)
            if start == 0 and head == 0:
                value_grad[...] = value_part
                key_grad[...] = key_part
            else:
                value_grad[...] = value_grad[...] + value_part
                key_grad[...] = key_grad[...] + key_part
            outs.append(dot(keys_turned[of, :], grad_scores))
        grad_query = jnp.concatenate(outs, axis=0).T * HEAD**-0.5
        grad_query = grad_query * cosine[at, :] - swap_halves(grad_query) * sine[at, :]
        made[at, :LANES] = grad_query.astype(BF16)
    for start in range(0, rows, ROW_BLOCK):
        at = slice(start, start + ROW_BLOCK)
        grad_key = key_grad[at, :]
        grad_key = grad_key * cosine[at, :] - swap_halves(grad_key) * sine[at, :]
        made[at, LANES : 2 * LANES] = grad_key.astype(BF16)
        made[at, 2 * LANES :] = value_grad[at, :].astype(BF16)
        total_grad[at, :] = total_grad[at, :] + dot_last(made[at, :], weights[...])
    product[:, : 3 * LANES] = dot(x_turned[...], made[...])
    product[:, 3 * LANES :] = dot(ga_turned[...], mixed[...])
    note_peak(peak_out, product)
    for n in range(4):
        plan.disperse(place, product, n * LANES, grads[n])

    @pl.when(pl.program_id(0) == pl.num_programs(0) - 1)
    def _():
        gain_grad = jnp.zeros((1, width), F32)
        shift_grad = jnp.zeros((1, width), F32)
        for start in range(0, rows, ROW_BLOCK):
            at = slice(start, start + ROW_BLOCK)
            grad_first = total_grad[at, :]
            normal = normal_one[at, :]
            grad = normalize_back(grad_first, normal, inverse_one[at, :], norms[0:1, :])
            gain_grad = gain_grad + jnp.sum(grad_first * normal, axis=0, keepdims=True)
            shift_grad = shift_grad + jnp.sum(grad_first, axis=0, keepdims=True)
            low_out[at, :] = grad.astype(BF16)
        norm_out[0:1, :] = gain_grad
        norm_out[1:2, :] = shift_grad


def attend_back(
    plan,
    place,
    ga,
    x,
    q,
    k,
    v,
    mixed,
    log_total,
    wq,
    wk,
    wv,
    wo,
    cosine,
    sine,
    grad_res,
    normal_one,
    inverse_one,
    norms,
):
    rows, width = x.shape
    part = wq.shape[-1]
    pairs = part // LANES
    steps = plan.tensor * pairs

    def locate(i):
        return i // pairs, lax.rem(i, pairs)

    by_pair = pl.BlockSpec((None, rows, LANES), lambda i, place: (i, 0, 0))
    orders = ("yx", "xy", "yx", "xy")
    shapes, specs = [], []
    for order in orders:
        shapes += plan.grad_shapes(order, part)
        specs += plan.grad_specs(order, LANES, locate)
    outs = pl.pallas_call(
        functools.partial(attend_back_kernel, plan),
        name="attend_back",
        out_shape=shapes
        + [
            jax.ShapeDtypeStruct((rows, width), BF16),
            jax.ShapeDtypeStruct((8, width), F32),
            jax.ShapeDtypeStruct((8, LANES), F32),
        ],
        grid_spec=pltpu.PrefetchScalarGridSpec(
            num_scalar_prefetch=1,
            grid=(steps,),
            in_specs=[
                whole((rows, width)),
                whole((rows, width)),
                by_pair,
                by_pair,
                by_pair,
                pl.BlockSpec((rows, LANES), lambda i, place: (0, i)),
                pl.BlockSpec((None, 8, rows), lambda i, place: (i, 0, 0)),
            ]
            + [plan.weight_spec(order, LANES, locate) for order in orders]
            + [
                whole((rows, LANES)),
                whole((rows, LANES)),
                whole((rows, width)),
                whole((rows, width)),
                whole((rows, 1)),
                whole(norms.shape),
            ],
            out_specs=specs + [result((rows, width)), result((8, width)), result((8, LANES))],
            scratch_shapes=[
                pltpu.VMEM((width, rows), BF16),
                pltpu.VMEM((width, rows), BF16),
                pltpu.VMEM((width, 3 * LANES), BF16),
                pltpu.VMEM((width, LANES), BF16),
                pltpu.VMEM((rows, width), F32),
                pltpu.VMEM((rows, LANES), BF16),
                pltpu.VMEM((rows, 3 * LANES), BF16),
                pltpu.VMEM((rows, LANES), F32),
                pltpu.VMEM((rows, LANES), F32),
                pltpu.VMEM((width, 4 * LANES), F32),
            ],
        ),
        compiler_params=params(),
        cost_estimate=pl.CostEstimate(
            flops=16 * rows * width * width + 40 * rows * rows * width,
            bytes_accessed=rows * width * 30,
            transcendentals=0,
        ),
    )(
        place,
        ga,
        x,
        q,
        k,
        v,
        mixed,
        log_total,
        wq,
        wk,
        wv,
        wo,
        cosine,
        sine,
        grad_res,
        normal_one,
        inverse_one,
        norms,
    )
    nc = plan.nc
    return tuple(outs[n * nc : (n + 1) * nc] for n in range(4)) + tuple(outs[4 * nc :])


def adam_step(weight, first_moment, second_moment, gradient, factor):
    clipped = gradient * factor
    first_next = beta_one * first_moment + (1.0 - beta_one) * clipped
    second_next = beta_two * second_moment + (1.0 - beta_two) * clipped * clipped
    corrected_first = first_next / (1.0 - beta_one**STEP)
    corrected_second = second_next / (1.0 - beta_two**STEP)
    change = -learn_rate * (
        corrected_first / (jnp.sqrt(corrected_second) + adam_epsilon) + weight_decay * weight
    )
    return (first_next, second_next, change)


def per_device(
    plan,
    token_ids,
    lengths,
    token_table,
    table_first,
    table_second,
    qkv_weight,
    qkv_first,
    qkv_second,
    out_weight,
    out_first,
    out_second,
    gate_up_weight,
    gate_up_first,
    gate_up_second,
    down_weight,
    down_first,
    down_second,
    norm_params,
    norm_first,
    norm_second,
    log_inverse_warmth,
    scale_first,
    scale_second,
):
    slot_ids = token_ids[0]
    rows = slot_ids.shape[0]
    vocab_shard, width = token_table.shape
    own_length = lax.dynamic_index_in_dim(
        lengths[0], lax.axis_index("tensor"), 0, keepdims=False
    ).astype(jnp.int32)
    place = jnp.stack([jnp.asarray(p, jnp.int32) for p in plan.places()] + [own_length])
    me = lax.axis_index(AXES)

    qkv_low = qkv_weight.astype(BF16)
    gate_up_low = gate_up_weight.astype(BF16)
    wq = plan.gather(qkv_low[:, 0], "yx")
    wk = plan.gather(qkv_low[:, 1], "xy")
    wv = plan.gather(qkv_low[:, 2], "yx")
    wo = plan.gather(out_weight.astype(BF16), "xy")
    wg = plan.gather(gate_up_low[:, 0], "yx")
    wu = plan.gather(gate_up_low[:, 1], "xy")
    wd = plan.gather(down_weight.astype(BF16), "xy")

    table_low = token_table.astype(BF16)
    room = 8 * -(-(5 * rows) // (4 * plan.count * 8))
    slots = room * plan.count
    owner, row, first, token_place = token_places(slot_ids, own_length, vocab_shard)
    slot = round_slots(owner, token_place, room, 0)
    wants = round_wants(slot, first, row, slots)
    rounds = jnp.max(token_place) // room + 1
    note_rows = 8 * -(-(slots + LANES) // (8 * LANES))
    note = jnp.concatenate(
        [wants, jnp.full((note_rows * LANES - slots,), rounds, jnp.int32)]
    ).reshape(note_rows, LANES)
    notes = share(plan, note).reshape(plan.count, note_rows * LANES)
    asked = lax.dynamic_slice_in_dim(notes, me * room, room, axis=1)
    rounds = jnp.max(notes[:, slots])
    embedded = spread_rows(slot, swap_rows(plan, picked_rows(asked, table_low)))

    def ask(turn):
        later = round_slots(owner, token_place, room, turn)
        later_wants = round_wants(later, first, row, slots).reshape(plan.count, room)
        return later, lax.all_to_all(later_wants, AXES, 0, 0, tiled=True)

    def fetch_more(turn, sofar):
        later, later_asked = ask(turn)
        return sofar + spread_rows(later, swap_rows(plan, picked_rows(later_asked, table_low)))

    embedded = lax.fori_loop(1, rounds, fetch_more, embedded)
    normal_one, inverse_one = normalize(embedded)
    first_low = (normal_one * norm_params[0] + norm_params[1]).astype(BF16)

    cosine, sine = rotary_tables(rows)
    q, k, v, mixed, log_total = attend(plan, place, first_low, wq, wk, wv, cosine, sine)
    second_low, normal_two, inverse_two = project(plan, place, mixed, wo, normal_one, norm_params)
    gate, up, hidden_low, normal_three, inverse_three, pool = feed(
        plan, place, second_low, wg, wu, wd, normal_two, norm_params
    )
    batch_loss, grad_log_scale, grad_pool = contrast(
        plan, place, pool, norm_params, log_inverse_warmth
    )
    gate_parts, up_parts, down_parts, grad_first_res, attended_low, norm_two, peak_two = feed_back(
        plan,
        place,
        grad_pool,
        second_low,
        gate,
        up,
        hidden_low,
        wg,
        wu,
        wd,
        normal_three,
        inverse_three,
        normal_two,
        inverse_two,
        norm_params,
    )
    scale_two = wire_scale(plan, peak_two)
    grad_gate = plan.scatter(gate_parts, "yx", scale_two)
    grad_up = plan.scatter(up_parts, "xy", scale_two)
    grad_down_own = plan.scatter(down_parts, "xy", scale_two)
    q_parts, k_parts, v_parts, out_parts, embedded_low, norm_one, peak_one = attend_back(
        plan,
        place,
        attended_low,
        first_low,
        q,
        k,
        v,
        mixed,
        log_total,
        wq,
        wk,
        wv,
        wo,
        cosine,
        sine,
        grad_first_res,
        normal_one,
        inverse_one,
        norm_params,
    )
    grad_rows = summed_rows(slot, embedded_low, slots).astype(BF16)
    grad_table = summed_rows(asked.reshape(-1), swap_rows(plan, grad_rows), vocab_shard)

    def return_more(turn, sofar):
        later, later_asked = ask(turn)
        later_rows = summed_rows(later, embedded_low, slots).astype(BF16)
        return sofar + summed_rows(
            later_asked.reshape(-1), swap_rows(plan, later_rows), vocab_shard
        )

    grad_table = lax.fori_loop(1, rounds, return_more, grad_table)
    scale_one = wire_scale(plan, peak_one)
    grad_qkv_own = jnp.stack(
        [
            plan.scatter(q_parts, "yx", scale_one),
            plan.scatter(k_parts, "xy", scale_one),
            plan.scatter(v_parts, "yx", scale_one),
        ],
        axis=1,
    )
    grad_out_own = plan.scatter(out_parts, "xy", scale_one)
    grad_gate_own = jnp.stack([grad_gate, grad_up], axis=1)

    owned_squares = (
        jnp.sum(grad_table * grad_table)
        + jnp.sum(grad_qkv_own * grad_qkv_own)
        + jnp.sum(grad_out_own * grad_out_own)
        + jnp.sum(grad_gate * grad_gate)
        + jnp.sum(grad_up * grad_up)
        + jnp.sum(grad_down_own * grad_down_own)
    )
    length_float = own_length.astype(F32)
    sums = total(
        plan,
        jnp.concatenate(
            [
                norm_one[0:2],
                norm_two[0:2],
                grad_pool * pool,
                grad_pool * length_float,
                jnp.full((1, width), owned_squares, F32),
                jnp.zeros((1, width), F32),
            ],
            axis=0,
        ),
        1,
    )
    norm_grads = sums[0:6]
    square_total = sums[6, 0]
    squares = square_total + jnp.sum(norm_grads * norm_grads) + grad_log_scale * grad_log_scale
    grad_norm = jnp.sqrt(squares)
    factor = jnp.minimum(1.0, clip_limit / (grad_norm + 1e-06))
    return (
        (batch_loss, grad_norm)
        + adam_step(token_table, table_first, table_second, grad_table, factor)
        + adam_step(qkv_weight, qkv_first, qkv_second, grad_qkv_own, factor)
        + adam_step(out_weight, out_first, out_second, grad_out_own, factor)
        + adam_step(gate_up_weight, gate_up_first, gate_up_second, grad_gate_own, factor)
        + adam_step(down_weight, down_first, down_second, grad_down_own, factor)
        + adam_step(norm_params, norm_first, norm_second, norm_grads, factor)
        + adam_step(log_inverse_warmth, scale_first, scale_second, grad_log_scale, factor)
    )


def solution(mesh):
    rows = P(AXES, None)
    deep = P("dp", None, "tensor")
    flat = P("dp", "tensor")
    in_specs = (
        (rows, P("dp", None)) + (rows,) * 3 + (deep,) * 3 + (flat,) * 3 + (deep,) * 3 + (flat,) * 3
    ) + (P(),) * 6
    out_specs = (
        (P(), P()) + (rows,) * 3 + (deep,) * 3 + (flat,) * 3 + (deep,) * 3 + (flat,) * 3
    ) + (P(),) * 6

    def run(*args):
        plan = Plan(mesh, args[2].shape[1])
        return jax.shard_map(
            functools.partial(per_device, plan),
            mesh=mesh,
            in_specs=in_specs,
            out_specs=out_specs,
            check_vma=False,
        )(*args)

    return run
```

```python
import functools

import jax
import jax.numpy as jnp
from jax import lax
from jax.experimental import pallas as pl
from jax.experimental.pallas import tpu as pltpu
from jax.sharding import PartitionSpec as P

HEAD = 64
STEP = 8

norm_epsilon = 1e-12
rope_base = 1000.0
beta_one = 0.9
beta_two = 0.999
adam_epsilon = 1e-08
learn_rate = 0.01
weight_decay = 0.01
clip_limit = 0.001
masked_score = -1e30

AXES = ("dp", "tensor")
F32 = jnp.float32
BF16 = jnp.bfloat16
LANES = 128
VMEM_LIMIT = 58 * 1024 * 1024
ROW_BLOCK = 256
HIDDEN_BLOCK = 256


class Plan:
    def __init__(self, mesh, width):
        self.dp = mesh.shape["dp"]
        self.tensor = mesh.shape["tensor"]
        self.count = self.dp * self.tensor
        self.shard = width // self.dp
        self.stepped = self.dp % 4 == 0 and self.shard % 16 == 0
        if self.stepped:
            self.nc, self.nx, self.nz = 2, 2, self.dp // 4
        else:
            self.nc, self.nx, self.nz = 1, 1, 1
        self.rows = width // (self.nc * self.nx * self.nz)

    def places(self):
        dp_index, tensor_index = lax.axis_index("dp"), lax.axis_index("tensor")
        if not self.stepped:
            zero = jnp.int32(0)
            return zero, zero, zero, zero
        core = lax.rem(dp_index, self.nc)
        across = lax.rem(dp_index // self.nc, self.nx)
        return dp_index // (self.nc * self.nx), across, core, tensor_index

    def size(self, axis):
        return {"z": self.nz, "x": self.nx, "c": self.nc, "y": self.tensor}[axis]

    def shift(self, values, axis, by):
        pairs = []
        for z in range(self.nz):
            for x in range(self.nx):
                for c in range(self.nc):
                    for y in range(self.tensor):
                        place = {"z": z, "x": x, "c": c, "y": y}
                        source = self.flat(place)
                        place[axis] = (place[axis] + by) % self.size(axis)
                        pairs.append((source, self.flat(place)))
        return lax.ppermute(values, AXES, pairs)

    def flat(self, place):
        dp_index = (place["z"] * self.nx + place["x"]) * self.nc + place["c"]
        return dp_index * self.tensor + place["y"]

    def gather_whole(self, values):
        whole = lax.all_gather(values, ("tensor", "dp"), axis=0, tiled=True)
        return whole.reshape(self.tensor, -1, values.shape[1])

    def gathered_shape(self, shard):
        rows, columns = shard.shape
        return jax.ShapeDtypeStruct(
            (self.tensor, self.nz, self.nx, self.nc, rows, columns), shard.dtype
        )

    def scatter(self, parts, order, scale):
        if not self.stepped:
            whole = parts[0].reshape(self.tensor * self.rows, parts[0].shape[-1])
            return lax.psum_scatter(
                whole.astype(F32), ("tensor", "dp"), scatter_dimension=0, tiled=True
            )
        keep, send = parts
        total = keep.astype(F32) + self.shift(send, "c", 1).astype(F32)
        for axis in tuple(order) + ("z",):
            kept = total[0]
            for far in range(1, self.size(axis)):
                sent = (total[far] * scale).astype(jnp.float16)
                kept = kept + self.shift(sent, axis, far).astype(F32) / scale
            total = kept
        return total


    def weight_spec(self, width, columns, locate):
        def index(i, place):
            part, column = locate(i)
            return (part, 0, column)

        return pl.BlockSpec((None, width, columns), index)

    def grad_specs(self, order, columns, locate):
        def index(i, place):
            part, column = locate(i)
            far = lax.rem(part - place[3] + self.tensor, self.tensor)
            if order == "yx":
                return (far, 0, 0, 0, column)
            return (0, far, 0, 0, column)

        middle = (None, self.nx) if order == "yx" else (self.nx, None)
        spec = pl.BlockSpec(middle + (self.nz, self.rows, columns), index)
        return [spec] * self.nc

    def grad_shapes(self, order, columns):
        middle = (self.tensor, self.nx) if order == "yx" else (self.nx, self.tensor)
        shape = middle + (self.nz, self.rows, columns)
        return [jax.ShapeDtypeStruct(shape, F32)] * self.nc

    def disperse(self, place, source, first_column, targets):
        columns = targets[0].shape[-1]
        for far_z in range(self.nz):
            z = lax.rem(place[0] + far_z, self.nz)
            for far_x in range(self.nx):
                x = lax.rem(place[1] + far_x, self.nx)
                for far_c in range(self.nc):
                    c = lax.rem(place[2] + far_c, self.nc)
                    start = ((z * self.nx + x) * self.nc + c) * self.rows
                    start = pl.multiple_of(start, 16)
                    targets[far_c][far_x, far_z] = source[
                        pl.ds(start, self.rows), first_column : first_column + columns
                    ]


def dot(left, right):
    return lax.dot_general(left, right, (((1,), (0,)), ((), ())), preferred_element_type=F32)


def dot_last(left, right):
    return lax.dot_general(left, right, (((1,), (1,)), ((), ())), preferred_element_type=F32)


def normalize(values):
    centered = values - jnp.mean(values, axis=-1, keepdims=True)
    inverse = lax.rsqrt(jnp.mean(centered * centered, axis=-1, keepdims=True) + norm_epsilon)
    return centered * inverse, inverse


def normalize_back(grad_output, normal, inverse, gain):
    grad_normal = grad_output * gain
    mean_grad = jnp.mean(grad_normal, axis=-1, keepdims=True)
    mean_cross = jnp.mean(grad_normal * normal, axis=-1, keepdims=True)
    return inverse * (grad_normal - mean_grad - normal * mean_cross)


def rotary_tables(length):
    half_width = HEAD // 2
    steps_half = jnp.arange(half_width, dtype=jnp.int32).astype(F32)
    frequency = rope_base ** (-2.0 * steps_half / HEAD)
    positions = jnp.arange(length, dtype=jnp.int32).astype(F32)
    angles = positions[:, None] * frequency[None, :]
    cosine, sine = jnp.cos(angles), jnp.sin(angles)
    heads = LANES // HEAD
    return (
        jnp.concatenate([cosine, cosine] * heads, axis=1),
        jnp.concatenate([-sine, sine] * heads, axis=1),
    )


def swap_halves(values):
    lane = lax.broadcasted_iota(jnp.int32, values.shape, 1)
    ahead = pltpu.roll(values, LANES - HEAD // 2, 1)
    behind = pltpu.roll(values, HEAD // 2, 1)
    return jnp.where(lax.rem(lane, HEAD) < HEAD // 2, ahead, behind)


def of_head(values, head):
    lane = lax.broadcasted_iota(jnp.int32, values.shape, 1)
    return jnp.where(lane // HEAD == head, values, jnp.zeros_like(values))


def note_peak(peak_out, product):
    largest = jnp.max(jnp.abs(product[...]), axis=0, keepdims=True)
    largest = jnp.broadcast_to(jnp.max(largest, axis=1, keepdims=True), peak_out.shape)

    @pl.when(pl.program_id(0) == 0)
    def _():
        peak_out[...] = largest

    @pl.when(pl.program_id(0) > 0)
    def _():
        peak_out[...] = jnp.maximum(peak_out[...], largest)


def params(**more):
    return pltpu.CompilerParams(vmem_limit_bytes=VMEM_LIMIT, **more)


def whole(shape):
    zeros = (0,) * len(shape)
    return pl.BlockSpec(shape, lambda i, place: zeros, pipeline_mode=pl.Buffered(1))


def result(shape):
    zeros = (0,) * len(shape)
    return pl.BlockSpec(shape, lambda i, place: zeros)


def own_index(tensor):
    return lax.axis_index("dp") * tensor + lax.axis_index("tensor")


def device_at(index, tensor):
    return (index // tensor, lax.rem(index, tensor))


def greet_all(me, count, tensor):
    barrier = pltpu.get_barrier_semaphore()

    def greet(far, carry):
        pl.semaphore_signal(
            barrier,
            inc=1,
            device_id=device_at(lax.rem(me + far, count), tensor),
            device_id_type=pl.DeviceIdType.MESH,
        )
        return carry

    lax.fori_loop(1, count, greet, 0)
    pl.semaphore_wait(barrier, count - 1)


def for_all(me, count, tensor, source, target, send_sem, recv_sem, start):
    def act(far, carry):
        peer = lax.rem(me + far, count)
        copy = pltpu.make_async_remote_copy(
            src_ref=source(peer),
            dst_ref=target,
            send_sem=send_sem.at[far - 1],
            recv_sem=recv_sem.at[far - 1],
            device_id=device_at(peer, tensor),
            device_id_type=pl.DeviceIdType.MESH,
        )
        if start:
            copy.start()
        else:
            copy.wait()
        return carry

    lax.fori_loop(1, count, act, 0)


def swap_blocks_kernel(tensor, block_ref, out_ref, held, send_sem, recv_sem):
    count = held.shape[0]
    me = own_index(tensor)
    greet_all(me, count, tensor)
    for start in (True, False):
        for_all(
            me,
            count,
            tensor,
            lambda peer: block_ref.at[peer],
            held.at[me],
            send_sem,
            recv_sem,
            start,
        )
        if start:
            held[pl.ds(me, 1)] = block_ref[pl.ds(me, 1)]
    out_ref[...] = held[...]


def in_vmem():
    return pl.BlockSpec(memory_space=pltpu.VMEM)


def in_place():
    return pl.BlockSpec(memory_space=pl.ANY)


def swap_blocks(plan, blocks):
    return pl.pallas_call(
        functools.partial(swap_blocks_kernel, plan.tensor),
        name="swap_blocks",
        out_shape=jax.ShapeDtypeStruct(blocks.shape, blocks.dtype),
        in_specs=[in_vmem()],
        out_specs=in_vmem(),
        scratch_shapes=[
            pltpu.VMEM(blocks.shape, blocks.dtype),
            pltpu.SemaphoreType.DMA((plan.count - 1,)),
            pltpu.SemaphoreType.DMA((plan.count - 1,)),
        ],
        compiler_params=params(collective_id=0, has_side_effects=True),
    )(blocks)


def largest_sum_kernel(count, tensor, block_ref, out_ref, held, send_sem, recv_sem):
    me = own_index(tensor)
    greet_all(me, count, tensor)
    for start in (True, False):
        for_all(
            me, count, tensor, lambda peer: block_ref, held.at[me], send_sem, recv_sem, start
        )
        if start:
            held[pl.ds(me, 1)] = block_ref[...][None]
    out_ref[...] = jnp.sum(held[...], axis=0)


def largest_sum(plan, block):
    return pl.pallas_call(
        functools.partial(largest_sum_kernel, plan.count, plan.tensor),
        name="largest_sum",
        out_shape=jax.ShapeDtypeStruct(block.shape, block.dtype),
        in_specs=[in_vmem()],
        out_specs=in_vmem(),
        scratch_shapes=[
            pltpu.VMEM((plan.count,) + block.shape, block.dtype),
            pltpu.SemaphoreType.DMA((plan.count - 1,)),
            pltpu.SemaphoreType.DMA((plan.count - 1,)),
        ],
        compiler_params=params(collective_id=3, has_side_effects=True),
    )(block)


def total_kernel(
    tensor, block_ref, out_ref, came, held, own, send_sem, recv_sem, late_send, late_recv
):
    count = held.shape[0]
    me = own_index(tensor)
    greet_all(me, count, tensor)
    for start in (True, False):
        for_all(
            me,
            count,
            tensor,
            lambda peer: block_ref.at[peer],
            came.at[me],
            send_sem,
            recv_sem,
            start,
        )
        if start:
            came[pl.ds(me, 1)] = block_ref[pl.ds(me, 1)]
    summed = jnp.sum(came[...], axis=0)
    own[...] = summed
    for start in (True, False):
        for_all(me, count, tensor, lambda peer: own, held.at[me], late_send, late_recv, start)
        if start:
            held[pl.ds(me, 1)] = summed[None]
    out_ref[...] = held[...]


def total(plan, values, scalar):
    count = plan.count
    part = -(-values.shape[0] // count)
    padded = jnp.pad(values, (0, part * count - values.shape[0])).reshape(count, part)
    tail = jnp.full((count, 8 * LANES - part), scalar, values.dtype)
    blocks = jnp.concatenate([padded, tail], axis=1).reshape(count, 8, LANES)
    sums = pl.pallas_call(
        functools.partial(total_kernel, plan.tensor),
        name="total",
        out_shape=jax.ShapeDtypeStruct(blocks.shape, blocks.dtype),
        in_specs=[in_vmem()],
        out_specs=in_vmem(),
        scratch_shapes=[
            pltpu.VMEM(blocks.shape, blocks.dtype),
            pltpu.VMEM(blocks.shape, blocks.dtype),
            pltpu.VMEM(blocks.shape[1:], blocks.dtype),
        ]
        + [pltpu.SemaphoreType.DMA((count - 1,))] * 4,
        compiler_params=params(collective_id=1, has_side_effects=True),
    )(blocks).reshape(count, 8 * LANES)
    return sums[:, :part].reshape(-1)[: values.shape[0]], sums[0, part]


class Transport:
    def __init__(self, plan, shard, out, at, order, send_sem, recv_sem):
        self.plan, self.shard, self.out, self.at, self.order = plan, shard, out, at, order
        self.send_sem, self.recv_sem = send_sem, recv_sem
        self.dp_index, self.y = lax.axis_index("dp"), lax.axis_index("tensor")
        self.c = lax.rem(self.dp_index, plan.nc)
        self.x = lax.rem(self.dp_index // plan.nc, plan.nx)
        self.z = self.dp_index // (plan.nc * plan.nx)

    def device(self, z, x, c, y):
        return ((z * self.plan.nx + x) * self.plan.nc + c, y)

    def copies(self, stage):
        plan = self.plan
        z, x, c, y = self.z, self.x, self.c, self.y
        if stage == 0:
            target = self.out.at[y, z, x, c, self.at]
            return [
                pltpu.make_async_remote_copy(
                    src_ref=self.shard.at[self.at],
                    dst_ref=target,
                    send_sem=self.send_sem.at[far - 1],
                    recv_sem=self.recv_sem.at[far - 1],
                    device_id=self.device(lax.rem(z + far, plan.nz), x, c, y),
                    device_id_type=pl.DeviceIdType.MESH,
                )
                for far in range(1, plan.nz)
            ]
        path = self.order + ("c",)
        done = path[: stage - 1]
        axis = path[stage - 1]
        every = slice(None)
        block = self.out.at[
            every if "y" in done else y,
            every,
            every if "x" in done else x,
            every if "c" in done else c,
            self.at,
        ]
        device = {
            "x": self.device(z, 1 - x, c, y),
            "y": self.device(z, x, c, 1 - y),
            "c": self.device(z, x, 1 - c, y),
        }[axis]
        slot = plan.nz - 2 + stage
        return [
            pltpu.make_async_remote_copy(
                src_ref=block,
                dst_ref=block,
                send_sem=self.send_sem.at[slot],
                recv_sem=self.recv_sem.at[slot],
                device_id=device,
                device_id_type=pl.DeviceIdType.MESH,
            )
        ]

    def own(self):
        slot = self.plan.nz + 2
        return pltpu.make_async_copy(
            self.shard.at[self.at],
            self.out.at[self.y, self.z, self.x, self.c, self.at],
            self.send_sem.at[slot],
        )

    def advance(self, stage):
        if stage == 0:
            self.own().start()
        elif stage == 1:
            self.own().wait()
        if stage > 0:
            for copy in self.copies(stage - 1):
                copy.wait_recv()
        if stage < 4:
            for copy in self.copies(stage):
                copy.start()
        else:
            for earlier in range(4):
                for copy in self.copies(earlier):
                    copy.wait_send()


def greet_neighbours(plan):
    dp_index, y = lax.axis_index("dp"), lax.axis_index("tensor")
    c = lax.rem(dp_index, plan.nc)
    x = lax.rem(dp_index // plan.nc, plan.nx)
    z = dp_index // (plan.nc * plan.nx)
    places = [(lax.rem(z + far, plan.nz), x, c, y) for far in range(1, plan.nz)]
    places += [(z, 1 - x, c, y), (z, x, c, 1 - y), (z, x, 1 - c, y)]
    barrier = pltpu.get_barrier_semaphore()
    for to_z, to_x, to_c, to_y in places:
        pl.semaphore_signal(
            barrier,
            inc=1,
            device_id=((to_z * plan.nx + to_x) * plan.nc + to_c, to_y),
            device_id_type=pl.DeviceIdType.MESH,
        )
    pl.semaphore_wait(barrier, len(places))


def transport_slots(plan):
    return plan.nz + 3


def fetch_kernel(plan, orders, rows_ref, *refs):
    number = len(orders)
    shards, came = refs[:number], refs[number]
    outs = refs[number + 1 : 2 * number + 1]
    send_sem, recv_sem, own_sem, weight_send, weight_recv = refs[2 * number + 1 :]
    count, tensor = plan.count, plan.tensor
    me = own_index(tensor)
    greet_all(me, count, tensor)
    units = [
        Transport(
            plan,
            shards[n],
            outs[n],
            slice(None),
            orders[n],
            weight_send.at[n],
            weight_recv.at[n],
        )
        for n in range(number)
    ]
    for unit in units:
        unit.advance(0)
    own = pltpu.make_async_copy(rows_ref.at[me], came.at[me], own_sem)
    own.start()

    def rows(start):
        for_all(
            me,
            count,
            tensor,
            lambda peer: rows_ref.at[peer],
            came.at[me],
            send_sem,
            recv_sem,
            start,
        )

    rows(True)
    for stage in range(1, 5):
        for unit in units:
            unit.advance(stage)
    own.wait()
    rows(False)


def fetch(plan, rows, shards, orders):
    number = len(shards)
    slots = transport_slots(plan)
    outs = pl.pallas_call(
        functools.partial(fetch_kernel, plan, orders),
        name="fetch",
        out_shape=[jax.ShapeDtypeStruct(rows.shape, rows.dtype)]
        + [plan.gathered_shape(shard) for shard in shards],
        in_specs=[in_place()] * (1 + number),
        out_specs=[in_place()] * (1 + number),
        scratch_shapes=[
            pltpu.SemaphoreType.DMA((plan.count - 1,)),
            pltpu.SemaphoreType.DMA((plan.count - 1,)),
            pltpu.SemaphoreType.DMA(()),
            pltpu.SemaphoreType.DMA((number, slots)),
            pltpu.SemaphoreType.DMA((number, slots)),
        ],
        compiler_params=params(collective_id=4, has_side_effects=True),
    )(rows, *shards)
    return outs[0], [w.reshape(plan.tensor, -1, w.shape[-1]) for w in outs[1:]]


def wire_scale(plan, peak):
    bound = largest_sum(plan, peak)[0, 0]
    exponent = jnp.floor(jnp.log2(32768.0 / jnp.maximum(bound, 1e-30)))
    return jnp.exp2(jnp.clip(exponent, -60.0, 60.0))


def token_places(slot_ids, length, vocab_shard):
    count = slot_ids.shape[0]
    order = jnp.arange(count, dtype=jnp.int32)
    key = jnp.where(order < length, slot_ids, -1)
    owner = key // vocab_shard
    row = key - owner * vocab_shard
    same = key[:, None] == key[None, :]
    first_at = jnp.min(jnp.where(same, order[None, :], count), axis=1)
    first = (first_at == order) & (key >= 0)
    earlier = first[None, :] & (owner[:, None] == owner[None, :])
    place = jnp.sum(
        (earlier & (order[None, :] < first_at[:, None])).astype(jnp.int32), axis=1
    )
    return owner, row, first, jnp.where(key >= 0, place, -1)


def round_slots(owner, place, room, turn):
    within = place - turn * room
    served = (within >= 0) & (within < room)
    return jnp.where(served, owner * room + within, -1)


def round_wants(slot, first, row, slots):
    wanted = first[None, :] & (slot[None, :] == jnp.arange(slots, dtype=jnp.int32)[:, None])
    return jnp.max(jnp.where(wanted, row[None, :], -1), axis=1)


def picked_rows(wants, table_low):
    chosen = wants.reshape(-1)[:, None] == jnp.arange(table_low.shape[0], dtype=jnp.int32)[None, :]
    return jnp.dot(chosen.astype(BF16), table_low, preferred_element_type=F32).astype(BF16)


def spread_rows(slot, rows):
    chosen = slot[:, None] == jnp.arange(rows.shape[0], dtype=jnp.int32)[None, :]
    return jnp.dot(chosen.astype(BF16), rows, preferred_element_type=F32)


def summed_rows(index, rows, count):
    chosen = jnp.arange(count, dtype=jnp.int32)[:, None] == index[None, :]
    return jnp.dot(chosen.astype(BF16), rows, preferred_element_type=F32)


def swap_rows(plan, rows):
    parts = rows.reshape(plan.count, rows.shape[0] // plan.count, rows.shape[1])
    return lax.all_to_all(parts, AXES, 0, 0, tiled=True).reshape(rows.shape)


def transport_units(plan, shards, outs, send_sem, recv_sem):
    units = []
    for n in range(len(shards)):
        rows = shards[n].shape[0]
        cut = 16 * (rows // 16 * 2 // 3)
        orders = (("x", "y"), ("y", "x")) if n % 2 == 0 else (("y", "x"), ("x", "y"))
        ranges = ((0, cut), (cut, rows - cut))
        for (start, size), order in zip(ranges, orders):
            number = len(units)
            units.append(
                Transport(
                    plan,
                    shards[n],
                    outs[n],
                    pl.ds(start, size),
                    order,
                    send_sem.at[number],
                    recv_sem.at[number],
                )
            )
    return units


SLOTS_PER_STEP = 2
TRANSPORT_SLOTS = {
    3: ((0, 1),),
    4: ((1, 1),),
    6: ((2, 1), (0, 2), (1, 2)),
    7: ((3, 1),),
    8: ((2, 2),),
    9: ((3, 2), (0, 3), (1, 3)),
    10: ((4, 1),),
    11: ((5, 1), (2, 3)),
}
TRANSPORT_END = (
    (4, 2),
    (5, 2),
    (3, 3),
    (4, 3),
    (5, 3),
    (0, 4),
    (1, 4),
    (2, 4),
    (3, 4),
    (4, 4),
    (5, 4),
)


def attend_kernel(plan, number, place, *refs):
    (embedded, wq, wk, wv, wo, cosine, sine, norms) = refs[:8]
    shards = refs[8 : 8 + number]
    (q, k, v, mixed_out, log_total, low_one, normal_one, inverse_one) = refs[8 + number : 16 + number]
    (low_two, normal_two, inverse_two) = refs[16 + number : 19 + number]
    gathered = refs[19 + number : 19 + 2 * number]
    scratch = refs[19 + 2 * number :]
    weights, mixed = scratch[:2]
    rows = embedded.shape[0]
    step = pl.program_id(0)
    if number:
        units = transport_units(plan, shards, gathered, *scratch[2:4])

        @pl.when(step == 0)
        def _():
            greet_neighbours(plan)
            for unit in units:
                unit.advance(0)

    def transport(part):
        if number:
            for slot, events in TRANSPORT_SLOTS.items():
                if slot % SLOTS_PER_STEP == part:

                    @pl.when(step == slot // SLOTS_PER_STEP)
                    def _():
                        for unit, stage in events:
                            units[unit].advance(stage)

    @pl.when(step == 0)
    def _():
        for start in range(0, rows, ROW_BLOCK):
            at = slice(start, start + ROW_BLOCK)
            normal, inverse = normalize(embedded[at, :])
            normal_one[at, :] = normal
            inverse_one[at, :] = inverse
            low_one[at, :] = (normal * norms[0:1, :] + norms[1:2, :]).astype(BF16)

    transport(0)
    weights[:, :LANES] = wq[...]
    weights[:, LANES : 2 * LANES] = wk[...]
    weights[:, 2 * LANES :] = wv[...]
    for start in range(0, rows, ROW_BLOCK):
        at = slice(start, start + ROW_BLOCK)
        made = dot(low_one[at, :], weights[...])
        query, key = made[:, :LANES], made[:, LANES : 2 * LANES]
        query = query * cosine[at, :] + swap_halves(query) * sine[at, :]
        key = key * cosine[at, :] + swap_halves(key) * sine[at, :]
        q[at, :] = (query * HEAD**-0.5).astype(BF16)
        k[at, :] = key.astype(BF16)
        v[at, :] = made[:, 2 * LANES :].astype(BF16)
    position = lax.broadcasted_iota(jnp.int32, (rows, 1), 0)
    bias = jnp.where(position < place[4], 0.0, masked_score)
    keys = k[...]
    values = v[...].T
    for start in range(0, rows, ROW_BLOCK):
        at = slice(start, start + ROW_BLOCK)
        if start == rows // 2:
            transport(1)
        outs = []
        for head in range(LANES // HEAD):
            scores = dot_last(keys, of_head(q[at, :], head)) + bias
            top = jnp.max(scores, axis=0, keepdims=True)
            exponent = jnp.exp(scores - top)
            summed = jnp.sum(exponent, axis=0, keepdims=True)
            out = dot(values[head * HEAD : (head + 1) * HEAD, :], exponent.astype(BF16))
            outs.append(out / summed)
            log_total[head : head + 1, at] = top + jnp.log(summed)
        made = jnp.concatenate(outs, axis=0).T.astype(BF16)
        mixed_out[at, :] = made
        mixed[step, at, :] = made

    @pl.when(step == pl.num_programs(0) - 1)
    def _():
        per_part = wo.shape[2] // LANES
        for start in range(0, rows, ROW_BLOCK):
            at = slice(start, start + ROW_BLOCK)
            product = normal_one[at, :] * norms[0:1, :] + norms[1:2, :]
            for part in range(plan.tensor):
                whole_mixed = jnp.concatenate(
                    [mixed[part * per_part + n, at, :] for n in range(per_part)], axis=1
                )
                product = product + dot_last(whole_mixed, wo[part])
            normal, inverse = normalize(product)
            normal_two[at, :] = normal
            inverse_two[at, :] = inverse
            low_two[at, :] = (normal * norms[2:3, :] + norms[3:4, :]).astype(BF16)
        if number:
            for unit, stage in TRANSPORT_END:
                units[unit].advance(stage)


def attend(plan, place, embedded, wq, wk, wv, wo, cosine, sine, norms, shards):
    rows, width = embedded.shape
    pairs = wq.shape[-1] // LANES
    steps = plan.tensor * pairs
    number = len(shards)

    def locate(i):
        return i // pairs, lax.rem(i, pairs)

    by_pair = pl.BlockSpec((None, rows, LANES), lambda i, place: (i, 0, 0))
    shape = jax.ShapeDtypeStruct((steps, rows, LANES), BF16)
    normed = [
        jax.ShapeDtypeStruct((rows, width), BF16),
        jax.ShapeDtypeStruct((rows, width), F32),
        jax.ShapeDtypeStruct((rows, 1), F32),
    ]
    normed_specs = [result((rows, width)), result((rows, width)), result((rows, 1))]
    scratch = [pltpu.VMEM((width, 3 * LANES), BF16), pltpu.VMEM((steps, rows, LANES), BF16)]
    more = {}
    if number:
        slots = transport_slots(plan)
        scratch += [pltpu.SemaphoreType.DMA((2 * number, slots))] * 2
        more = dict(collective_id=5, has_side_effects=True)
    outs = pl.pallas_call(
        functools.partial(attend_kernel, plan, number),
        name="attend",
        out_shape=[
            shape,
            shape,
            shape,
            jax.ShapeDtypeStruct((rows, steps * LANES), BF16),
            jax.ShapeDtypeStruct((steps, 8, rows), F32),
        ]
        + normed
        + normed
        + [plan.gathered_shape(shard) for shard in shards],
        grid_spec=pltpu.PrefetchScalarGridSpec(
            num_scalar_prefetch=1,
            grid=(steps,),
            in_specs=[whole((rows, width))]
            + [plan.weight_spec(width, LANES, locate)] * 3
            + [
                whole(wo.shape),
                whole((rows, LANES)),
                whole((rows, LANES)),
                whole(norms.shape),
            ]
            + [in_place()] * number,
            out_specs=[
                by_pair,
                by_pair,
                by_pair,
                pl.BlockSpec((rows, LANES), lambda i, place: (0, i)),
                pl.BlockSpec((None, 8, rows), lambda i, place: (i, 0, 0)),
            ]
            + normed_specs
            + normed_specs
            + [in_place()] * number,
            scratch_shapes=scratch,
        ),
        compiler_params=params(**more),
        cost_estimate=pl.CostEstimate(
            flops=8 * rows * width * width + 16 * rows * rows * width,
            bytes_accessed=rows * width * 30,
            transcendentals=0,
        ),
    )(place, embedded, wq, wk, wv, wo, cosine, sine, norms, *shards)
    return outs[:11], [w.reshape(plan.tensor, -1, w.shape[-1]) for w in outs[11:]]


def feed_kernel(
    plan,
    place,
    x,
    wg,
    wu,
    wd,
    normal_two,
    norms,
    gate_out,
    up_out,
    hidden_out,
    normal_out,
    inverse_out,
    pool_out,
):
    rows, width = x.shape
    first = pl.program_id(0) == 0

    @pl.when(first)
    def _():
        normal_out[...] = jnp.zeros_like(normal_out)

    for start in range(0, rows, ROW_BLOCK):
        at = slice(start, start + ROW_BLOCK)
        gate, up = dot(x[at, :], wg[...]), dot(x[at, :], wu[...])
        hidden = (gate * jax.nn.sigmoid(gate) * up).astype(BF16)
        gate_out[at, :] = gate.astype(BF16)
        up_out[at, :] = up.astype(BF16)
        hidden_out[at, :] = hidden
        normal_out[at, :] = normal_out[at, :] + dot_last(hidden, wd[...])

    @pl.when(pl.program_id(0) == pl.num_programs(0) - 1)
    def _():
        pooled = jnp.zeros((1, width), F32)
        for start in range(0, rows, ROW_BLOCK):
            at = slice(start, start + ROW_BLOCK)
            second_out = normal_two[at, :] * norms[2:3, :] + norms[3:4, :]
            normal, inverse = normalize(second_out + normal_out[at, :])
            normal_out[at, :] = normal
            inverse_out[at, :] = inverse
            position = start + lax.broadcasted_iota(jnp.int32, (ROW_BLOCK, 1), 0)
            kept = jnp.where(position < place[4], normal, 0.0)
            pooled = pooled + jnp.sum(kept, axis=0, keepdims=True)
        pool_out[...] = pooled


def feed(plan, place, x, wg, wu, wd, normal_two, norms):
    rows, width = x.shape
    hidden = wg.shape[-1]
    chunks = hidden // HIDDEN_BLOCK
    steps = plan.tensor * chunks

    def locate(i):
        return i // chunks, lax.rem(i, chunks)

    by_chunk = pl.BlockSpec((rows, HIDDEN_BLOCK), lambda i, place: (0, i))
    shape = jax.ShapeDtypeStruct((rows, plan.tensor * hidden), BF16)
    return pl.pallas_call(
        functools.partial(feed_kernel, plan),
        name="feed",
        out_shape=[
            shape,
            shape,
            shape,
            jax.ShapeDtypeStruct((rows, width), F32),
            jax.ShapeDtypeStruct((rows, 1), F32),
            jax.ShapeDtypeStruct((1, width), F32),
        ],
        grid_spec=pltpu.PrefetchScalarGridSpec(
            num_scalar_prefetch=1,
            grid=(steps,),
            in_specs=[
                whole((rows, width)),
                plan.weight_spec(width, HIDDEN_BLOCK, locate),
                plan.weight_spec(width, HIDDEN_BLOCK, locate),
                plan.weight_spec(width, HIDDEN_BLOCK, locate),
                whole((rows, width)),
                whole(norms.shape),
            ],
            out_specs=[
                by_chunk,
                by_chunk,
                by_chunk,
                result((rows, width)),
                result((rows, 1)),
                result((1, width)),
            ],
        ),
        compiler_params=params(),
        cost_estimate=pl.CostEstimate(
            flops=6 * rows * width * plan.tensor * hidden,
            bytes_accessed=rows * width * 40,
            transcendentals=0,
        ),
    )(place, x, wg, wu, wd, normal_two, norms)


def contrast_kernel(
    tensor, place, pool_ref, norms, scale_ref, loss_ref, grad_ref, held, own, send_sem, recv_sem
):
    count = held.shape[0]
    me = own_index(tensor)
    greet_all(me, count, tensor)
    length = jnp.full((1, 1), place[4], jnp.int32).astype(F32)
    pooled = pool_ref[...] / length * norms[4:5, :] + norms[5:6, :]
    inverse = lax.rsqrt(jnp.sum(pooled * pooled, axis=-1, keepdims=True) + norm_epsilon)
    vector = pooled * inverse
    own[...] = vector
    for start in (True, False):
        for_all(me, count, tensor, lambda peer: own, held.at[me], send_sem, recv_sem, start)
        if start:
            held[pl.ds(me, 1)] = vector[None]
    vectors = held[...].reshape(count, held.shape[2])
    scale = jnp.exp(scale_ref[...])
    logits = scale * lax.dot_general(
        vectors,
        vectors,
        (((1,), (1,)), ((), ())),
        precision=lax.Precision.HIGHEST,
        preferred_element_type=F32,
    )
    row = lax.broadcasted_iota(jnp.int32, (count, count), 0)
    column = lax.broadcasted_iota(jnp.int32, (count, count), 1)
    crossed = (lax.rem(row, 2) == 0) & (lax.rem(column, 2) == 1)
    shown = jnp.where(crossed, logits, masked_score)
    row_max = jnp.max(shown, axis=1, keepdims=True)
    row_exp = jnp.where(crossed, jnp.exp(shown - row_max), 0.0)
    row_sum = jnp.sum(row_exp, axis=1, keepdims=True)
    column_max = jnp.max(shown, axis=0, keepdims=True)
    column_exp = jnp.where(crossed, jnp.exp(shown - column_max), 0.0)
    column_sum = jnp.sum(column_exp, axis=0, keepdims=True)
    even = lax.rem(lax.broadcasted_iota(jnp.int32, (count, 1), 0), 2) == 0
    odd = lax.rem(lax.broadcasted_iota(jnp.int32, (1, count), 1), 2) == 1
    row_safe = jnp.where(even, row_sum, 1.0)
    column_safe = jnp.where(odd, column_sum, 1.0)
    row_lse = jnp.where(even, row_max + jnp.log(row_safe), 0.0)
    column_lse = jnp.where(odd, column_max + jnp.log(column_safe), 0.0)
    own = crossed & (column == row + 1)
    diagonal = jnp.sum(jnp.where(own, logits, 0.0))
    half = 1.0 / count
    loss = half * (jnp.sum(row_lse) + jnp.sum(column_lse) - 2.0 * diagonal)
    grad_logits = half * (
        row_exp / row_safe + column_exp / column_safe - 2.0 * own.astype(F32)
    )
    grad_scale = jnp.sum(grad_logits * jnp.where(crossed, logits, 0.0))
    both = grad_logits + grad_logits.T
    grad_vectors = scale * lax.dot_general(
        both,
        vectors,
        (((1,), (0,)), ((), ())),
        precision=lax.Precision.HIGHEST,
        preferred_element_type=F32,
    )
    mine = lax.broadcasted_iota(jnp.int32, (count, 1), 0) == me
    grad_own = jnp.sum(jnp.where(mine, grad_vectors, 0.0), axis=0, keepdims=True)
    along = jnp.sum(grad_own * vector, axis=-1, keepdims=True)
    grad_ref[...] = inverse * (grad_own - vector * along) / length
    lane = lax.broadcasted_iota(jnp.int32, loss_ref.shape, 1)
    loss_ref[...] = jnp.where(lane == 0, loss, grad_scale)


def contrast(plan, place, pool, norms, log_scale):
    width = pool.shape[1]
    loss, grad = pl.pallas_call(
        functools.partial(contrast_kernel, plan.tensor),
        name="contrast",
        out_shape=[
            jax.ShapeDtypeStruct((1, LANES), F32),
            jax.ShapeDtypeStruct((1, width), F32),
        ],
        in_specs=[pl.BlockSpec(memory_space=pltpu.SMEM)] + [in_vmem()] * 3,
        out_specs=[in_vmem()] * 2,
        scratch_shapes=[
            pltpu.VMEM((plan.count, 1, width), F32),
            pltpu.VMEM((1, width), F32),
            pltpu.SemaphoreType.DMA((plan.count - 1,)),
            pltpu.SemaphoreType.DMA((plan.count - 1,)),
        ],
        compiler_params=params(collective_id=2, has_side_effects=True),
    )(place, pool, norms, log_scale.reshape(1, 1))
    return loss[0, 0], loss[0, 1], grad


def feed_back_body(plan, place, *refs):
    (
        grad_pool,
        x,
        gate_ref,
        up_ref,
        hidden_ref,
        wg,
        wu,
        wd,
        normal_three,
        inverse_three,
        normal_two,
        inverse_two,
        norms,
    ) = refs[:13]
    nc = plan.nc
    gate_grads = refs[13 : 13 + nc]
    up_grads = refs[13 + nc : 13 + 2 * nc]
    down_grads = refs[13 + 2 * nc : 13 + 3 * nc]
    grad_out, low_out, norm_out, peak_out = refs[13 + 3 * nc : 17 + 3 * nc]
    low, low_turned, x_turned, made, product = refs[17 + 3 * nc :]
    rows, width = x.shape

    @pl.when(pl.program_id(0) == 0)
    def _():
        for start in range(0, rows, ROW_BLOCK):
            at = slice(start, start + ROW_BLOCK)
            position = start + lax.broadcasted_iota(jnp.int32, (ROW_BLOCK, 1), 0)
            grad_third = jnp.where(position < place[4], grad_pool[...], 0.0)
            grad = normalize_back(
                grad_third, normal_three[at, :], inverse_three[at, :], norms[4:5, :]
            )
            grad_out[at, :] = grad
            low[at, :] = grad.astype(BF16)
            low_turned[:, at] = grad.astype(BF16).T
            x_turned[:, at] = x[at, :].T

    for start in range(0, rows, ROW_BLOCK):
        at = slice(start, start + ROW_BLOCK)
        grad_hidden = dot(low[at, :], wd[...])
        gate = gate_ref[at, :].astype(F32)
        up = up_ref[at, :].astype(F32)
        share_gate = jax.nn.sigmoid(gate)
        grad_up = grad_hidden * gate * share_gate
        grad_gate = grad_hidden * up * share_gate * (1.0 + gate * (1.0 - share_gate))
        made[at, :HIDDEN_BLOCK] = grad_gate.astype(BF16)
        made[at, HIDDEN_BLOCK:] = grad_up.astype(BF16)
        grad_out[at, :] = (
            grad_out[at, :]
            + dot_last(made[at, :HIDDEN_BLOCK], wg[...])
            + dot_last(made[at, HIDDEN_BLOCK:], wu[...])
        )
    product[:, : 2 * HIDDEN_BLOCK] = dot(x_turned[...], made[...])
    product[:, 2 * HIDDEN_BLOCK :] = dot(low_turned[...], hidden_ref[...])
    note_peak(peak_out, product)
    plan.disperse(place, product, 0, gate_grads)
    plan.disperse(place, product, HIDDEN_BLOCK, up_grads)
    plan.disperse(place, product, 2 * HIDDEN_BLOCK, down_grads)

    @pl.when(pl.program_id(0) == pl.num_programs(0) - 1)
    def _():
        gain_grad = jnp.zeros((1, width), F32)
        shift_grad = jnp.zeros((1, width), F32)
        for start in range(0, rows, ROW_BLOCK):
            at = slice(start, start + ROW_BLOCK)
            grad_second = grad_out[at, :]
            normal = normal_two[at, :]
            grad = normalize_back(grad_second, normal, inverse_two[at, :], norms[2:3, :])
            gain_grad = gain_grad + jnp.sum(grad_second * normal, axis=0, keepdims=True)
            shift_grad = shift_grad + jnp.sum(grad_second, axis=0, keepdims=True)
            grad_out[at, :] = grad
            low_out[at, :] = grad.astype(BF16)
        norm_out[0:1, :] = gain_grad
        norm_out[1:2, :] = shift_grad


def feed_back(
    plan,
    place,
    grad_pool,
    x,
    gate,
    up,
    hidden_low,
    wg,
    wu,
    wd,
    normal_three,
    inverse_three,
    normal_two,
    inverse_two,
    norms,
):
    rows, width = x.shape
    hidden = wg.shape[-1]
    chunks = hidden // HIDDEN_BLOCK
    steps = plan.tensor * chunks

    def locate(i):
        return i // chunks, lax.rem(i, chunks)

    by_chunk = pl.BlockSpec((rows, HIDDEN_BLOCK), lambda i, place: (0, i))
    outs = pl.pallas_call(
        functools.partial(feed_back_body, plan),
        name="feed_back",
        out_shape=plan.grad_shapes("yx", hidden)
        + plan.grad_shapes("xy", hidden)
        + plan.grad_shapes("xy", hidden)
        + [
            jax.ShapeDtypeStruct((rows, width), F32),
            jax.ShapeDtypeStruct((rows, width), BF16),
            jax.ShapeDtypeStruct((8, width), F32),
            jax.ShapeDtypeStruct((8, LANES), F32),
        ],
        grid_spec=pltpu.PrefetchScalarGridSpec(
            num_scalar_prefetch=1,
            grid=(steps,),
            in_specs=[
                whole((1, width)),
                whole((rows, width)),
                by_chunk,
                by_chunk,
                by_chunk,
                plan.weight_spec(width, HIDDEN_BLOCK, locate),
                plan.weight_spec(width, HIDDEN_BLOCK, locate),
                plan.weight_spec(width, HIDDEN_BLOCK, locate),
                whole((rows, width)),
                whole((rows, 1)),
                whole((rows, width)),
                whole((rows, 1)),
                whole(norms.shape),
            ],
            out_specs=plan.grad_specs("yx", HIDDEN_BLOCK, locate)
            + plan.grad_specs("xy", HIDDEN_BLOCK, locate)
            + plan.grad_specs("xy", HIDDEN_BLOCK, locate)
            + [
                result((rows, width)),
                result((rows, width)),
                result((8, width)),
                result((8, LANES)),
            ],
            scratch_shapes=[
                pltpu.VMEM((rows, width), BF16),
                pltpu.VMEM((width, rows), BF16),
                pltpu.VMEM((width, rows), BF16),
                pltpu.VMEM((rows, 2 * HIDDEN_BLOCK), BF16),
                pltpu.VMEM((width, 3 * HIDDEN_BLOCK), F32),
            ],
        ),
        compiler_params=params(),
        cost_estimate=pl.CostEstimate(
            flops=12 * rows * width * plan.tensor * hidden,
            bytes_accessed=rows * width * 60,
            transcendentals=0,
        ),
    )(
        place,
        grad_pool,
        x,
        gate,
        up,
        hidden_low,
        wg,
        wu,
        wd,
        normal_three,
        inverse_three,
        normal_two,
        inverse_two,
        norms,
    )
    nc = plan.nc
    return (outs[:nc], outs[nc : 2 * nc], outs[2 * nc : 3 * nc]) + tuple(outs[3 * nc :])


def attend_back_kernel(plan, place, *refs):
    (
        ga,
        x,
        q,
        k,
        v,
        mixed,
        log_total,
        wq,
        wk,
        wv,
        wo,
        cosine,
        sine,
        grad_res,
        normal_one,
        inverse_one,
        norms,
    ) = refs[:17]
    nc = plan.nc
    grads = [refs[17 + n * nc : 17 + (n + 1) * nc] for n in range(4)]
    low_out, norm_out, peak_out = refs[17 + 4 * nc : 20 + 4 * nc]
    (
        ga_turned,
        x_turned,
        weights,
        total_grad,
        gm,
        made,
        key_grad,
        value_grad,
        product,
    ) = refs[20 + 4 * nc :]
    rows, width = x.shape

    @pl.when(pl.program_id(0) == 0)
    def _():
        for start in range(0, rows, ROW_BLOCK):
            at = slice(start, start + ROW_BLOCK)
            ga_turned[:, at] = ga[at, :].T
            x_turned[:, at] = x[at, :].T
            total_grad[at, :] = grad_res[at, :]

    weights[:, :LANES] = wq[...]
    weights[:, LANES : 2 * LANES] = wk[...]
    weights[:, 2 * LANES :] = wv[...]
    for start in range(0, rows, ROW_BLOCK):
        at = slice(start, start + ROW_BLOCK)
        gm[at, :] = dot(ga[at, :], wo[...]).astype(BF16)
    position = lax.broadcasted_iota(jnp.int32, (rows, 1), 0)
    bias = jnp.where(position < place[4], 0.0, masked_score)
    keys, values = k[...], v[...]
    keys_turned = keys.T
    for start in range(0, rows, ROW_BLOCK):
        at = slice(start, start + ROW_BLOCK)
        inner = (gm[at, :].astype(F32) * mixed[at, :].astype(F32)).T
        outs = []
        for head in range(LANES // HEAD):
            of = slice(head * HEAD, (head + 1) * HEAD)
            query = of_head(q[at, :], head)
            grad = of_head(gm[at, :], head)
            inner_sum = jnp.sum(inner[of, :], axis=0, keepdims=True)
            scores = dot_last(keys, query) + bias
            probs = jnp.exp(scores - log_total[head : head + 1, at])
            grad_probs = dot_last(values, grad)
            grad_scores = (probs * (grad_probs - inner_sum)).astype(BF16)
            value_part = dot(probs.astype(BF16), grad)
            key_part = dot(grad_scores, query)
            if start == 0 and head == 0:
                value_grad[...] = value_part
                key_grad[...] = key_part
            else:
                value_grad[...] = value_grad[...] + value_part
                key_grad[...] = key_grad[...] + key_part
            outs.append(dot(keys_turned[of, :], grad_scores))
        grad_query = jnp.concatenate(outs, axis=0).T * HEAD**-0.5
        grad_query = grad_query * cosine[at, :] - swap_halves(grad_query) * sine[at, :]
        made[at, :LANES] = grad_query.astype(BF16)
    for start in range(0, rows, ROW_BLOCK):
        at = slice(start, start + ROW_BLOCK)
        grad_key = key_grad[at, :]
        grad_key = grad_key * cosine[at, :] - swap_halves(grad_key) * sine[at, :]
        made[at, LANES : 2 * LANES] = grad_key.astype(BF16)
        made[at, 2 * LANES :] = value_grad[at, :].astype(BF16)
        total_grad[at, :] = total_grad[at, :] + dot_last(made[at, :], weights[...])
    product[:, : 3 * LANES] = dot(x_turned[...], made[...])
    product[:, 3 * LANES :] = dot(ga_turned[...], mixed[...])
    note_peak(peak_out, product)
    for n in range(4):
        plan.disperse(place, product, n * LANES, grads[n])

    @pl.when(pl.program_id(0) == pl.num_programs(0) - 1)
    def _():
        gain_grad = jnp.zeros((1, width), F32)
        shift_grad = jnp.zeros((1, width), F32)
        for start in range(0, rows, ROW_BLOCK):
            at = slice(start, start + ROW_BLOCK)
            grad_first = total_grad[at, :]
            normal = normal_one[at, :]
            grad = normalize_back(grad_first, normal, inverse_one[at, :], norms[0:1, :])
            gain_grad = gain_grad + jnp.sum(grad_first * normal, axis=0, keepdims=True)
            shift_grad = shift_grad + jnp.sum(grad_first, axis=0, keepdims=True)
            low_out[at, :] = grad.astype(BF16)
        norm_out[0:1, :] = gain_grad
        norm_out[1:2, :] = shift_grad


def attend_back(
    plan,
    place,
    ga,
    x,
    q,
    k,
    v,
    mixed,
    log_total,
    wq,
    wk,
    wv,
    wo,
    cosine,
    sine,
    grad_res,
    normal_one,
    inverse_one,
    norms,
):
    rows, width = x.shape
    part = wq.shape[-1]
    pairs = part // LANES
    steps = plan.tensor * pairs

    def locate(i):
        return i // pairs, lax.rem(i, pairs)

    by_pair = pl.BlockSpec((None, rows, LANES), lambda i, place: (i, 0, 0))
    orders = ("yx", "xy", "yx", "xy")
    shapes, specs = [], []
    for order in orders:
        shapes += plan.grad_shapes(order, part)
        specs += plan.grad_specs(order, LANES, locate)
    outs = pl.pallas_call(
        functools.partial(attend_back_kernel, plan),
        name="attend_back",
        out_shape=shapes
        + [
            jax.ShapeDtypeStruct((rows, width), BF16),
            jax.ShapeDtypeStruct((8, width), F32),
            jax.ShapeDtypeStruct((8, LANES), F32),
        ],
        grid_spec=pltpu.PrefetchScalarGridSpec(
            num_scalar_prefetch=1,
            grid=(steps,),
            in_specs=[
                whole((rows, width)),
                whole((rows, width)),
                by_pair,
                by_pair,
                by_pair,
                pl.BlockSpec((rows, LANES), lambda i, place: (0, i)),
                pl.BlockSpec((None, 8, rows), lambda i, place: (i, 0, 0)),
            ]
            + [plan.weight_spec(width, LANES, locate)] * 4
            + [
                whole((rows, LANES)),
                whole((rows, LANES)),
                whole((rows, width)),
                whole((rows, width)),
                whole((rows, 1)),
                whole(norms.shape),
            ],
            out_specs=specs + [result((rows, width)), result((8, width)), result((8, LANES))],
            scratch_shapes=[
                pltpu.VMEM((width, rows), BF16),
                pltpu.VMEM((width, rows), BF16),
                pltpu.VMEM((width, 3 * LANES), BF16),
                pltpu.VMEM((rows, width), F32),
                pltpu.VMEM((rows, LANES), BF16),
                pltpu.VMEM((rows, 3 * LANES), BF16),
                pltpu.VMEM((rows, LANES), F32),
                pltpu.VMEM((rows, LANES), F32),
                pltpu.VMEM((width, 4 * LANES), F32),
            ],
        ),
        compiler_params=params(),
        cost_estimate=pl.CostEstimate(
            flops=16 * rows * width * width + 40 * rows * rows * width,
            bytes_accessed=rows * width * 30,
            transcendentals=0,
        ),
    )(
        place,
        ga,
        x,
        q,
        k,
        v,
        mixed,
        log_total,
        wq,
        wk,
        wv,
        wo,
        cosine,
        sine,
        grad_res,
        normal_one,
        inverse_one,
        norms,
    )
    nc = plan.nc
    return tuple(outs[n * nc : (n + 1) * nc] for n in range(4)) + tuple(outs[4 * nc :])


def adam_step(weight, first_moment, second_moment, gradient, factor):
    clipped = gradient * factor
    first_next = beta_one * first_moment + (1.0 - beta_one) * clipped
    second_next = beta_two * second_moment + (1.0 - beta_two) * clipped * clipped
    corrected_first = first_next / (1.0 - beta_one**STEP)
    corrected_second = second_next / (1.0 - beta_two**STEP)
    change = -learn_rate * (
        corrected_first / (jnp.sqrt(corrected_second) + adam_epsilon) + weight_decay * weight
    )
    return (first_next, second_next, change)


def per_device(
    plan,
    token_ids,
    lengths,
    token_table,
    table_first,
    table_second,
    qkv_weight,
    qkv_first,
    qkv_second,
    out_weight,
    out_first,
    out_second,
    gate_up_weight,
    gate_up_first,
    gate_up_second,
    down_weight,
    down_first,
    down_second,
    norm_params,
    norm_first,
    norm_second,
    log_inverse_warmth,
    scale_first,
    scale_second,
):
    slot_ids = token_ids[0]
    rows = slot_ids.shape[0]
    vocab_shard, width = token_table.shape
    own_length = lax.dynamic_index_in_dim(
        lengths[0], lax.axis_index("tensor"), 0, keepdims=False
    ).astype(jnp.int32)
    place = jnp.stack([jnp.asarray(p, jnp.int32) for p in plan.places()] + [own_length])
    me = lax.axis_index(AXES)

    qkv_low = qkv_weight.astype(BF16)
    gate_up_low = gate_up_weight.astype(BF16)
    early = [qkv_low[:, 0], qkv_low[:, 1], qkv_low[:, 2], out_weight.astype(BF16)]
    late = [gate_up_low[:, 0], gate_up_low[:, 1], down_weight.astype(BF16)]

    table_low = token_table.astype(BF16)
    room = 8 * -(-(5 * rows) // (4 * plan.count * 8))
    slots = room * plan.count
    owner, row, first, token_place = token_places(slot_ids, own_length, vocab_shard)
    slot = round_slots(owner, token_place, room, 0)
    wants = round_wants(slot, first, row, slots).reshape(plan.count, room)
    rounds = jnp.max(token_place) // room + 1
    note = jnp.concatenate(
        [wants, jnp.broadcast_to(rounds, (plan.count, 8 * LANES - room))], axis=1
    )
    notes = swap_blocks(plan, note.reshape(plan.count, 8, LANES)).reshape(plan.count, 8 * LANES)
    asked = notes[:, :room]
    rounds = jnp.max(notes[:, room])
    picked = picked_rows(asked, table_low)
    if plan.stepped:
        half = width // 2
        folded = jnp.concatenate(
            [
                picked[:, :half].reshape(plan.count, room, half),
                picked[:, half:].reshape(plan.count, room, half),
            ],
            axis=1,
        )
        came, (wq, wk, wv, wo) = fetch(
            plan, folded, early, (("x", "y"), ("y", "x"), ("x", "y"), ("y", "x"))
        )
        came = jnp.concatenate([came[:, :room], came[:, room:]], axis=2).reshape(slots, width)
    else:
        came = swap_rows(plan, picked)
        wq, wk, wv, wo = [plan.gather_whole(shard) for shard in early]
    embedded = spread_rows(slot, came)

    def ask(turn):
        later = round_slots(owner, token_place, room, turn)
        later_wants = round_wants(later, first, row, slots).reshape(plan.count, room)
        return later, lax.all_to_all(later_wants, AXES, 0, 0, tiled=True)

    def fetch_more(turn, sofar):
        later, later_asked = ask(turn)
        return sofar + spread_rows(later, swap_rows(plan, picked_rows(later_asked, table_low)))

    embedded = lax.fori_loop(1, rounds, fetch_more, embedded)
    cosine, sine = rotary_tables(rows)
    made, gathered = attend(
        plan,
        place,
        embedded,
        wq,
        wk,
        wv,
        wo,
        cosine,
        sine,
        norm_params,
        late if plan.stepped else [],
    )
    q, k, v, mixed, log_total, first_low, normal_one, inverse_one = made[:8]
    second_low, normal_two, inverse_two = made[8:]
    if plan.stepped:
        wg, wu, wd = gathered
    else:
        wg, wu, wd = [plan.gather_whole(shard) for shard in late]
    gate, up, hidden_low, normal_three, inverse_three, pool = feed(
        plan, place, second_low, wg, wu, wd, normal_two, norm_params
    )
    batch_loss, grad_log_scale, grad_pool = contrast(
        plan, place, pool, norm_params, log_inverse_warmth
    )
    gate_parts, up_parts, down_parts, grad_first_res, attended_low, norm_two, peak_two = feed_back(
        plan,
        place,
        grad_pool,
        second_low,
        gate,
        up,
        hidden_low,
        wg,
        wu,
        wd,
        normal_three,
        inverse_three,
        normal_two,
        inverse_two,
        norm_params,
    )
    scale_two = wire_scale(plan, peak_two)
    grad_gate = plan.scatter(gate_parts, "yx", scale_two)
    grad_up = plan.scatter(up_parts, "xy", scale_two)
    grad_down_own = plan.scatter(down_parts, "xy", scale_two)
    q_parts, k_parts, v_parts, out_parts, embedded_low, norm_one, peak_one = attend_back(
        plan,
        place,
        attended_low,
        first_low,
        q,
        k,
        v,
        mixed,
        log_total,
        wq,
        wk,
        wv,
        wo,
        cosine,
        sine,
        grad_first_res,
        normal_one,
        inverse_one,
        norm_params,
    )
    grad_rows = summed_rows(slot, embedded_low, slots).astype(BF16)
    grad_table = summed_rows(asked.reshape(-1), swap_rows(plan, grad_rows), vocab_shard)

    def return_more(turn, sofar):
        later, later_asked = ask(turn)
        later_rows = summed_rows(later, embedded_low, slots).astype(BF16)
        return sofar + summed_rows(
            later_asked.reshape(-1), swap_rows(plan, later_rows), vocab_shard
        )

    grad_table = lax.fori_loop(1, rounds, return_more, grad_table)
    scale_one = wire_scale(plan, peak_one)
    grad_qkv_own = jnp.stack(
        [
            plan.scatter(q_parts, "yx", scale_one),
            plan.scatter(k_parts, "xy", scale_one),
            plan.scatter(v_parts, "yx", scale_one),
        ],
        axis=1,
    )
    grad_out_own = plan.scatter(out_parts, "xy", scale_one)
    grad_gate_own = jnp.stack([grad_gate, grad_up], axis=1)

    owned_squares = (
        jnp.sum(grad_table * grad_table)
        + jnp.sum(grad_qkv_own * grad_qkv_own)
        + jnp.sum(grad_out_own * grad_out_own)
        + jnp.sum(grad_gate * grad_gate)
        + jnp.sum(grad_up * grad_up)
        + jnp.sum(grad_down_own * grad_down_own)
    )
    length_float = own_length.astype(F32)
    norm_grads, square_total = total(
        plan,
        jnp.concatenate(
            [
                norm_one[0:2],
                norm_two[0:2],
                grad_pool * pool,
                grad_pool * length_float,
            ],
            axis=0,
        ).reshape(-1),
        owned_squares,
    )
    norm_grads = norm_grads.reshape(norm_params.shape)
    squares = square_total + jnp.sum(norm_grads * norm_grads) + grad_log_scale * grad_log_scale
    grad_norm = jnp.sqrt(squares)
    factor = jnp.minimum(1.0, clip_limit / (grad_norm + 1e-06))
    return (
        (batch_loss, grad_norm)
        + adam_step(token_table, table_first, table_second, grad_table, factor)
        + adam_step(qkv_weight, qkv_first, qkv_second, grad_qkv_own, factor)
        + adam_step(out_weight, out_first, out_second, grad_out_own, factor)
        + adam_step(gate_up_weight, gate_up_first, gate_up_second, grad_gate_own, factor)
        + adam_step(down_weight, down_first, down_second, grad_down_own, factor)
        + adam_step(norm_params, norm_first, norm_second, norm_grads, factor)
        + adam_step(log_inverse_warmth, scale_first, scale_second, grad_log_scale, factor)
    )


def solution(mesh):
    rows = P(AXES, None)
    deep = P("dp", None, "tensor")
    flat = P("dp", "tensor")
    in_specs = (
        (rows, P("dp", None)) + (rows,) * 3 + (deep,) * 3 + (flat,) * 3 + (deep,) * 3 + (flat,) * 3
    ) + (P(),) * 6
    out_specs = (
        (P(), P()) + (rows,) * 3 + (deep,) * 3 + (flat,) * 3 + (deep,) * 3 + (flat,) * 3
    ) + (P(),) * 6

    def run(*args):
        plan = Plan(mesh, args[2].shape[1])
        return jax.shard_map(
            functools.partial(per_device, plan),
            mesh=mesh,
            in_specs=in_specs,
            out_specs=out_specs,
            check_vma=False,
        )(*args)

    return run
```

```python
import functools

import jax
import jax.numpy as jnp
from jax import lax
from jax.experimental import pallas as pl
from jax.experimental.pallas import tpu as pltpu
from jax.sharding import PartitionSpec as P

HEAD = 64
STEP = 8

norm_epsilon = 1e-12
rope_base = 1000.0
beta_one = 0.9
beta_two = 0.999
adam_epsilon = 1e-08
learn_rate = 0.01
weight_decay = 0.01
clip_limit = 0.001
masked_score = -1e30

AXES = ("dp", "tensor")
F32 = jnp.float32
BF16 = jnp.bfloat16
LANES = 128
VMEM_LIMIT = 58 * 1024 * 1024
ROW_BLOCK = 256
HIDDEN_BLOCK = 256
BACK_BLOCK = 512


class Plan:
    def __init__(self, mesh, width):
        self.dp = mesh.shape["dp"]
        self.tensor = mesh.shape["tensor"]
        self.count = self.dp * self.tensor
        self.shard = width // self.dp
        self.stepped = self.dp % 4 == 0 and self.shard % 16 == 0
        if self.stepped:
            self.nc, self.nx, self.nz = 2, 2, self.dp // 4
        else:
            self.nc, self.nx, self.nz = 1, 1, 1
        self.rows = width // (self.nc * self.nx * self.nz)

    def places(self):
        dp_index, tensor_index = lax.axis_index("dp"), lax.axis_index("tensor")
        if not self.stepped:
            zero = jnp.int32(0)
            return zero, zero, zero, zero
        core = lax.rem(dp_index, self.nc)
        across = lax.rem(dp_index // self.nc, self.nx)
        return dp_index // (self.nc * self.nx), across, core, tensor_index

    def size(self, axis):
        return {"z": self.nz, "x": self.nx, "c": self.nc, "y": self.tensor}[axis]

    def shift(self, values, axis, by):
        pairs = []
        for z in range(self.nz):
            for x in range(self.nx):
                for c in range(self.nc):
                    for y in range(self.tensor):
                        place = {"z": z, "x": x, "c": c, "y": y}
                        source = self.flat(place)
                        place[axis] = (place[axis] + by) % self.size(axis)
                        pairs.append((source, self.flat(place)))
        return lax.ppermute(values, AXES, pairs)

    def flat(self, place):
        dp_index = (place["z"] * self.nx + place["x"]) * self.nc + place["c"]
        return dp_index * self.tensor + place["y"]

    def gather_whole(self, values):
        whole = lax.all_gather(values, ("tensor", "dp"), axis=0, tiled=True)
        return whole.reshape(self.tensor, -1, values.shape[1])

    def gathered_shape(self, shard):
        rows, columns = shard.shape
        return jax.ShapeDtypeStruct(
            (self.tensor, self.nz, self.nx, self.nc, rows, columns), shard.dtype
        )

    def scatter_whole(self, part):
        whole = part.reshape(self.tensor * self.rows, part.shape[-1])
        return lax.psum_scatter(whole, ("tensor", "dp"), scatter_dimension=0, tiled=True)

    def step_along(self, total, axis, scale):
        own_y = lax.axis_index("tensor")
        pick = functools.partial(lax.dynamic_index_in_dim, total, axis=0, keepdims=False)
        kept = pick(own_y) if axis == "y" else total[0]
        for far in range(1, self.size(axis)):
            other = pick(lax.rem(own_y + far, self.tensor)) if axis == "y" else total[far]
            sent = (other * scale).astype(jnp.float16)
            kept = kept + self.shift(sent, axis, far).astype(F32) / scale
        return kept

    def scatter(self, part, order, scale):
        if not self.stepped:
            return self.scatter_whole(part)
        for axis in tuple(order) + ("z",):
            part = self.step_along(part, axis, scale)
        return part


    def weight_spec(self, width, columns, locate):
        def index(i, place):
            part, column = locate(i)
            return (part, 0, column)

        return pl.BlockSpec((None, width, columns), index)

    def grad_spec(self, order, columns, locate):
        def index(i, place):
            part, column = locate(i)
            if order == "yx":
                return (part, 0, 0, 0, column)
            return (0, part, 0, 0, column)

        middle = (None, self.nx) if order == "yx" else (self.nx, None)
        return pl.BlockSpec(middle + (self.nz, self.rows, columns), index)

    def grad_shape(self, order, columns):
        middle = (self.tensor, self.nx) if order == "yx" else (self.nx, self.tensor)
        return jax.ShapeDtypeStruct(middle + (self.nz, self.rows, columns), F32)


class SiblingSum:
    def __init__(self, plan, steps, kept, sent, came, send_sem, recv_sem, free_sem):
        self.plan, self.steps = plan, steps
        self.kept, self.sent, self.came = kept, sent, came
        self.send_sem, self.recv_sem, self.free_sem = send_sem, recv_sem, free_sem
        dp_index, self.y = lax.axis_index("dp"), lax.axis_index("tensor")
        self.c = lax.rem(dp_index, plan.nc)
        self.x = lax.rem(dp_index // plan.nc, plan.nx)
        self.z = dp_index // (plan.nc * plan.nx)
        self.sibling = (dp_index + 1 - 2 * self.c, self.y)

    def greet(self):
        if self.plan.nc > 1:
            barrier = pltpu.get_barrier_semaphore()
            pl.semaphore_signal(
                barrier, inc=1, device_id=self.sibling, device_id_type=pl.DeviceIdType.MESH
            )
            pl.semaphore_wait(barrier, 1)

    def copy(self, slot):
        return pltpu.make_async_remote_copy(
            src_ref=self.sent.at[slot],
            dst_ref=self.came.at[slot],
            send_sem=self.send_sem.at[slot],
            recv_sem=self.recv_sem.at[slot],
            device_id=self.sibling,
            device_id_type=pl.DeviceIdType.MESH,
        )

    def push(self, step, product):
        plan = self.plan
        slot = lax.rem(step, 2)
        if plan.nc > 1:

            @pl.when(step >= 2)
            def _():
                self.copy(slot).wait_send()
                pl.semaphore_wait(self.free_sem, 1)

        for far_x in range(plan.nx):
            x = lax.rem(self.x + far_x, plan.nx)
            for far_z in range(plan.nz):
                z = lax.rem(self.z + far_z, plan.nz)
                base = (z * plan.nx + x) * plan.nc
                to = slice(
                    (far_x * plan.nz + far_z) * plan.rows,
                    (far_x * plan.nz + far_z + 1) * plan.rows,
                )
                start = pl.multiple_of((base + self.c) * plan.rows, 16)
                self.kept[slot, to, :] = product[pl.ds(start, plan.rows), :]
                if plan.nc > 1:
                    start = pl.multiple_of((base + 1 - self.c) * plan.rows, 16)
                    self.sent[slot, to, :] = product[pl.ds(start, plan.rows), :]
        if plan.nc > 1:
            self.copy(slot).start()

    def pull(self, step, targets, widths, peak_out):
        plan = self.plan
        slot = lax.rem(step, 2)
        if plan.nc > 1:
            self.copy(slot).wait_recv()
        peak = jnp.zeros((1, 1), F32)
        for far_x in range(plan.nx):
            for far_z in range(plan.nz):
                at = slice(
                    (far_x * plan.nz + far_z) * plan.rows,
                    (far_x * plan.nz + far_z + 1) * plan.rows,
                )
                value = self.kept[slot, at, :]
                if plan.nc > 1:
                    value = value + self.came[slot, at, :]
                start = 0
                for target, width in zip(targets, widths):
                    target[far_x, far_z] = value[:, start : start + width]
                    start += width
                largest = jnp.max(jnp.abs(value), axis=0, keepdims=True)
                peak = jnp.maximum(peak, jnp.max(largest, axis=1, keepdims=True))
        if plan.nc > 1:

            @pl.when(step < self.steps - 2)
            def _():
                pl.semaphore_signal(
                    self.free_sem,
                    inc=1,
                    device_id=self.sibling,
                    device_id_type=pl.DeviceIdType.MESH,
                )

            @pl.when(step == self.steps - 1)
            def _():
                for last in range(max(self.steps - 2, 0), self.steps):
                    self.copy(last % 2).wait_send()

        peak = jnp.broadcast_to(peak, peak_out.shape)

        @pl.when(step == 0)
        def _():
            peak_out[...] = peak

        @pl.when(step > 0)
        def _():
            peak_out[...] = jnp.maximum(peak_out[...], peak)

    @staticmethod
    def scratch(plan, columns):
        rows = plan.nx * plan.nz * plan.rows
        held = pltpu.VMEM((2, rows, columns), F32)
        if plan.nc == 1:
            return [held]
        return [
            held,
            held,
            held,
            pltpu.SemaphoreType.DMA((2,)),
            pltpu.SemaphoreType.DMA((2,)),
            pltpu.SemaphoreType.REGULAR,
        ]

    @staticmethod
    def made_of(plan, steps, refs):
        return SiblingSum(plan, steps, *(tuple(refs) + (None,) * (6 - len(refs))))

    @staticmethod
    def params(plan, collective_id):
        if plan.nc == 1:
            return params()
        return params(collective_id=collective_id, has_side_effects=True)


def dot(left, right):
    return lax.dot_general(left, right, (((1,), (0,)), ((), ())), preferred_element_type=F32)


def dot_last(left, right):
    return lax.dot_general(left, right, (((1,), (1,)), ((), ())), preferred_element_type=F32)


def normalize(values):
    centered = values - jnp.mean(values, axis=-1, keepdims=True)
    inverse = lax.rsqrt(jnp.mean(centered * centered, axis=-1, keepdims=True) + norm_epsilon)
    return centered * inverse, inverse


def normalize_back(grad_output, normal, inverse, gain):
    grad_normal = grad_output * gain
    mean_grad = jnp.mean(grad_normal, axis=-1, keepdims=True)
    mean_cross = jnp.mean(grad_normal * normal, axis=-1, keepdims=True)
    return inverse * (grad_normal - mean_grad - normal * mean_cross)


def rotary_tables(length):
    half_width = HEAD // 2
    steps_half = jnp.arange(half_width, dtype=jnp.int32).astype(F32)
    frequency = rope_base ** (-2.0 * steps_half / HEAD)
    positions = jnp.arange(length, dtype=jnp.int32).astype(F32)
    angles = positions[:, None] * frequency[None, :]
    cosine, sine = jnp.cos(angles), jnp.sin(angles)
    heads = LANES // HEAD
    return (
        jnp.concatenate([cosine, cosine] * heads, axis=1),
        jnp.concatenate([-sine, sine] * heads, axis=1),
    )


def swap_halves(values):
    lane = lax.broadcasted_iota(jnp.int32, values.shape, 1)
    ahead = pltpu.roll(values, LANES - HEAD // 2, 1)
    behind = pltpu.roll(values, HEAD // 2, 1)
    return jnp.where(lax.rem(lane, HEAD) < HEAD // 2, ahead, behind)


def of_head(values, head):
    lane = lax.broadcasted_iota(jnp.int32, values.shape, 1)
    return jnp.where(lane // HEAD == head, values, jnp.zeros_like(values))


def params(**more):
    return pltpu.CompilerParams(vmem_limit_bytes=VMEM_LIMIT, **more)


def whole(shape):
    zeros = (0,) * len(shape)
    return pl.BlockSpec(shape, lambda i, place: zeros, pipeline_mode=pl.Buffered(1))


def result(shape):
    zeros = (0,) * len(shape)
    return pl.BlockSpec(shape, lambda i, place: zeros)


def own_index(tensor):
    return lax.axis_index("dp") * tensor + lax.axis_index("tensor")


def device_at(index, tensor):
    return (index // tensor, lax.rem(index, tensor))


def greet_all(me, count, tensor):
    barrier = pltpu.get_barrier_semaphore()

    def greet(far, carry):
        pl.semaphore_signal(
            barrier,
            inc=1,
            device_id=device_at(lax.rem(me + far, count), tensor),
            device_id_type=pl.DeviceIdType.MESH,
        )
        return carry

    lax.fori_loop(1, count, greet, 0)
    pl.semaphore_wait(barrier, count - 1)


def for_all(me, count, tensor, source, target, send_sem, recv_sem, start):
    def act(far, carry):
        peer = lax.rem(me + far, count)
        copy = pltpu.make_async_remote_copy(
            src_ref=source(peer),
            dst_ref=target,
            send_sem=send_sem.at[far - 1],
            recv_sem=recv_sem.at[far - 1],
            device_id=device_at(peer, tensor),
            device_id_type=pl.DeviceIdType.MESH,
        )
        if start:
            copy.start()
        else:
            copy.wait()
        return carry

    lax.fori_loop(1, count, act, 0)


def swap_blocks_kernel(tensor, block_ref, out_ref, held, send_sem, recv_sem):
    count = held.shape[0]
    me = own_index(tensor)
    greet_all(me, count, tensor)
    for start in (True, False):
        for_all(
            me,
            count,
            tensor,
            lambda peer: block_ref.at[peer],
            held.at[me],
            send_sem,
            recv_sem,
            start,
        )
        if start:
            held[pl.ds(me, 1)] = block_ref[pl.ds(me, 1)]
    out_ref[...] = held[...]


def in_vmem():
    return pl.BlockSpec(memory_space=pltpu.VMEM)


def in_place():
    return pl.BlockSpec(memory_space=pl.ANY)


def swap_blocks(plan, blocks):
    return pl.pallas_call(
        functools.partial(swap_blocks_kernel, plan.tensor),
        name="swap_blocks",
        out_shape=jax.ShapeDtypeStruct(blocks.shape, blocks.dtype),
        in_specs=[in_vmem()],
        out_specs=in_vmem(),
        scratch_shapes=[
            pltpu.VMEM(blocks.shape, blocks.dtype),
            pltpu.SemaphoreType.DMA((plan.count - 1,)),
            pltpu.SemaphoreType.DMA((plan.count - 1,)),
        ],
        compiler_params=params(collective_id=0, has_side_effects=True),
    )(blocks)


def total_kernel(
    tensor, block_ref, out_ref, came, held, own, send_sem, recv_sem, late_send, late_recv
):
    count = held.shape[0]
    me = own_index(tensor)
    greet_all(me, count, tensor)
    for start in (True, False):
        for_all(
            me,
            count,
            tensor,
            lambda peer: block_ref.at[peer],
            came.at[me],
            send_sem,
            recv_sem,
            start,
        )
        if start:
            came[pl.ds(me, 1)] = block_ref[pl.ds(me, 1)]
    summed = jnp.sum(came[...], axis=0)
    own[...] = summed
    for start in (True, False):
        for_all(me, count, tensor, lambda peer: own, held.at[me], late_send, late_recv, start)
        if start:
            held[pl.ds(me, 1)] = summed[None]
    out_ref[...] = held[...]


def total(plan, values, scalar):
    count = plan.count
    part = -(-values.shape[0] // count)
    padded = jnp.pad(values, (0, part * count - values.shape[0])).reshape(count, part)
    tail = jnp.full((count, 8 * LANES - part), scalar, values.dtype)
    blocks = jnp.concatenate([padded, tail], axis=1).reshape(count, 8, LANES)
    sums = pl.pallas_call(
        functools.partial(total_kernel, plan.tensor),
        name="total",
        out_shape=jax.ShapeDtypeStruct(blocks.shape, blocks.dtype),
        in_specs=[in_vmem()],
        out_specs=in_vmem(),
        scratch_shapes=[
            pltpu.VMEM(blocks.shape, blocks.dtype),
            pltpu.VMEM(blocks.shape, blocks.dtype),
            pltpu.VMEM(blocks.shape[1:], blocks.dtype),
        ]
        + [pltpu.SemaphoreType.DMA((count - 1,))] * 4,
        compiler_params=params(collective_id=1, has_side_effects=True),
    )(blocks).reshape(count, 8 * LANES)
    return sums[:, :part].reshape(-1)[: values.shape[0]], sums[0, part]


class Transport:
    def __init__(self, plan, shard, out, at, order, send_sem, recv_sem):
        self.plan, self.shard, self.out, self.at, self.order = plan, shard, out, at, order
        self.send_sem, self.recv_sem = send_sem, recv_sem
        self.dp_index, self.y = lax.axis_index("dp"), lax.axis_index("tensor")
        self.c = lax.rem(self.dp_index, plan.nc)
        self.x = lax.rem(self.dp_index // plan.nc, plan.nx)
        self.z = self.dp_index // (plan.nc * plan.nx)

    def device(self, z, x, c, y):
        return ((z * self.plan.nx + x) * self.plan.nc + c, y)

    def copies(self, stage):
        plan = self.plan
        z, x, c, y = self.z, self.x, self.c, self.y
        if stage == 0:
            target = self.out.at[(y, z, x, c) + self.at]
            return [
                pltpu.make_async_remote_copy(
                    src_ref=self.shard.at[self.at],
                    dst_ref=target,
                    send_sem=self.send_sem.at[far - 1],
                    recv_sem=self.recv_sem.at[far - 1],
                    device_id=self.device(lax.rem(z + far, plan.nz), x, c, y),
                    device_id_type=pl.DeviceIdType.MESH,
                )
                for far in range(1, plan.nz)
            ]
        path = self.order + ("c",)
        done = path[: stage - 1]
        axis = path[stage - 1]
        every = slice(None)
        block = self.out.at[
            (
                every if "y" in done else y,
                every,
                every if "x" in done else x,
                every if "c" in done else c,
            )
            + self.at
        ]
        device = {
            "x": self.device(z, 1 - x, c, y),
            "y": self.device(z, x, c, 1 - y),
            "c": self.device(z, x, 1 - c, y),
        }[axis]
        slot = plan.nz - 2 + stage
        return [
            pltpu.make_async_remote_copy(
                src_ref=block,
                dst_ref=block,
                send_sem=self.send_sem.at[slot],
                recv_sem=self.recv_sem.at[slot],
                device_id=device,
                device_id_type=pl.DeviceIdType.MESH,
            )
        ]

    def own(self):
        slot = self.plan.nz + 2
        return pltpu.make_async_copy(
            self.shard.at[self.at],
            self.out.at[(self.y, self.z, self.x, self.c) + self.at],
            self.send_sem.at[slot],
        )

    def advance(self, stage):
        if stage == 0:
            self.own().start()
        elif stage == 1:
            self.own().wait()
        if stage > 0:
            for copy in self.copies(stage - 1):
                copy.wait_recv()
        if stage < 4:
            for copy in self.copies(stage):
                copy.start()
        else:
            for earlier in range(4):
                for copy in self.copies(earlier):
                    copy.wait_send()


def greet_neighbours(plan):
    dp_index, y = lax.axis_index("dp"), lax.axis_index("tensor")
    c = lax.rem(dp_index, plan.nc)
    x = lax.rem(dp_index // plan.nc, plan.nx)
    z = dp_index // (plan.nc * plan.nx)
    places = [(lax.rem(z + far, plan.nz), x, c, y) for far in range(1, plan.nz)]
    places += [(z, 1 - x, c, y), (z, x, c, 1 - y), (z, x, 1 - c, y)]
    barrier = pltpu.get_barrier_semaphore()
    for to_z, to_x, to_c, to_y in places:
        pl.semaphore_signal(
            barrier,
            inc=1,
            device_id=((to_z * plan.nx + to_x) * plan.nc + to_c, to_y),
            device_id_type=pl.DeviceIdType.MESH,
        )
    pl.semaphore_wait(barrier, len(places))


def transport_slots(plan):
    return plan.nz + 3


def fetch_kernel(plan, orders, rows_ref, *refs):
    number = len(orders)
    shards, came = refs[:number], refs[number]
    outs = refs[number + 1 : 2 * number + 1]
    send_sem, recv_sem, own_sem, weight_send, weight_recv = refs[2 * number + 1 :]
    count, tensor = plan.count, plan.tensor
    me = own_index(tensor)
    greet_all(me, count, tensor)
    units = [
        Transport(
            plan,
            shards[n],
            outs[n],
            (slice(None),),
            orders[n],
            weight_send.at[n],
            weight_recv.at[n],
        )
        for n in range(number)
    ]
    for unit in units:
        unit.advance(0)
    own = pltpu.make_async_copy(rows_ref.at[me], came.at[me], own_sem)
    own.start()

    def rows(start):
        for_all(
            me,
            count,
            tensor,
            lambda peer: rows_ref.at[peer],
            came.at[me],
            send_sem,
            recv_sem,
            start,
        )

    rows(True)
    for stage in range(1, 5):
        for unit in units:
            unit.advance(stage)
    own.wait()
    rows(False)


def fetch(plan, rows, shards, orders):
    number = len(shards)
    slots = transport_slots(plan)
    outs = pl.pallas_call(
        functools.partial(fetch_kernel, plan, orders),
        name="fetch",
        out_shape=[jax.ShapeDtypeStruct(rows.shape, rows.dtype)]
        + [plan.gathered_shape(shard) for shard in shards],
        in_specs=[in_place()] * (1 + number),
        out_specs=[in_place()] * (1 + number),
        scratch_shapes=[
            pltpu.SemaphoreType.DMA((plan.count - 1,)),
            pltpu.SemaphoreType.DMA((plan.count - 1,)),
            pltpu.SemaphoreType.DMA(()),
            pltpu.SemaphoreType.DMA((number, slots)),
            pltpu.SemaphoreType.DMA((number, slots)),
        ],
        compiler_params=params(collective_id=4, has_side_effects=True),
    )(rows, *shards)
    return outs[0], [w.reshape(plan.tensor, -1, w.shape[-1]) for w in outs[1:]]


def wire_scale(plan, peak):
    bound = peak[0, 0] * (plan.count // plan.nc)
    exponent = jnp.floor(jnp.log2(32768.0 / jnp.maximum(bound, 1e-30)))
    return jnp.exp2(jnp.clip(exponent, -60.0, 60.0))


class PeakExchange:
    def __init__(self, plan, own, held, send_sem, recv_sem):
        self.own, self.held, self.send_sem, self.recv_sem = own, held, send_sem, recv_sem
        dp_index, y = lax.axis_index("dp"), lax.axis_index("tensor")
        c = lax.rem(dp_index, plan.nc)
        x = lax.rem(dp_index // plan.nc, plan.nx)
        z = dp_index // (plan.nc * plan.nx)

        def device(z, x, y):
            return ((z * plan.nx + x) * plan.nc + c, y)

        self.peers = (
            [device(z, 1 - x, y), device(z, x, 1 - y), device(z, 1 - x, 1 - y)],
            [device(lax.rem(z + far, plan.nz), x, y) for far in range(1, plan.nz)],
        )

    def greet(self, more=()):
        barrier = pltpu.get_barrier_semaphore()
        peers = self.peers[0] + self.peers[1] + list(more)
        for peer in peers:
            pl.semaphore_signal(
                barrier, inc=1, device_id=peer, device_id_type=pl.DeviceIdType.MESH
            )
        pl.semaphore_wait(barrier, len(peers))

    def copies(self, stage):
        first = len(self.peers[0]) * stage
        return [
            pltpu.make_async_remote_copy(
                src_ref=self.own.at[stage],
                dst_ref=self.held.at[first + n],
                send_sem=self.send_sem.at[first + n],
                recv_sem=self.recv_sem.at[first + n],
                device_id=peer,
                device_id_type=pl.DeviceIdType.MESH,
            )
            for n, peer in enumerate(self.peers[stage])
        ]

    def start(self, stage, value):
        self.own[stage] = value
        for copy in self.copies(stage):
            copy.start()

    def finish(self, stage):
        for copy in self.copies(stage):
            copy.wait()
        value = self.own[stage]
        first = len(self.peers[0]) * stage
        for n in range(len(self.peers[stage])):
            value = jnp.maximum(value, self.held[first + n])
        return value

    @staticmethod
    def scratch(plan):
        number = 3 + plan.nz - 1
        return [
            pltpu.VMEM((2, 8, LANES), F32),
            pltpu.VMEM((number, 8, LANES), F32),
            pltpu.SemaphoreType.DMA((number,)),
            pltpu.SemaphoreType.DMA((number,)),
        ]


def token_places(slot_ids, length, vocab_shard):
    count = slot_ids.shape[0]
    order = jnp.arange(count, dtype=jnp.int32)
    key = jnp.where(order < length, slot_ids, -1)
    owner = key // vocab_shard
    row = key - owner * vocab_shard
    same = key[:, None] == key[None, :]
    first_at = jnp.min(jnp.where(same, order[None, :], count), axis=1)
    first = (first_at == order) & (key >= 0)
    earlier = first[None, :] & (owner[:, None] == owner[None, :])
    place = jnp.sum(
        (earlier & (order[None, :] < first_at[:, None])).astype(jnp.int32), axis=1
    )
    return owner, row, first, jnp.where(key >= 0, place, -1)


def round_slots(owner, place, room, turn):
    within = place - turn * room
    served = (within >= 0) & (within < room)
    return jnp.where(served, owner * room + within, -1)


def round_wants(slot, first, row, slots):
    wanted = first[None, :] & (slot[None, :] == jnp.arange(slots, dtype=jnp.int32)[:, None])
    return jnp.max(jnp.where(wanted, row[None, :], -1), axis=1)


def picked_rows(wants, table_low):
    chosen = wants.reshape(-1)[:, None] == jnp.arange(table_low.shape[0], dtype=jnp.int32)[None, :]
    return jnp.dot(chosen.astype(BF16), table_low, preferred_element_type=F32).astype(BF16)


def spread_rows(slot, rows):
    chosen = slot[:, None] == jnp.arange(rows.shape[0], dtype=jnp.int32)[None, :]
    return jnp.dot(chosen.astype(BF16), rows, preferred_element_type=F32)


def summed_rows(index, rows, count):
    chosen = jnp.arange(count, dtype=jnp.int32)[:, None] == index[None, :]
    return jnp.dot(chosen.astype(BF16), rows, preferred_element_type=F32)


def swap_rows(plan, rows):
    parts = rows.reshape(plan.count, rows.shape[0] // plan.count, rows.shape[1])
    return lax.all_to_all(parts, AXES, 0, 0, tiled=True).reshape(rows.shape)


def transport_units(plan, shards, outs, send_sem, recv_sem):
    units = []
    for n in range(len(shards)):
        half = shards[n].shape[1] // 2
        for side, order in enumerate((("x", "y"), ("y", "x"))):
            number = len(units)
            units.append(
                Transport(
                    plan,
                    shards[n],
                    outs[n],
                    (slice(None), pl.ds(side * half, half)),
                    order,
                    send_sem.at[number],
                    recv_sem.at[number],
                )
            )
    return units


SLOTS_PER_STEP = 4
TRANSPORT_SLOTS = {
    0: ((0, 0),),
    7: ((0, 1), (1, 0)),
    11: ((0, 2),),
    14: ((1, 1), (2, 0)),
    18: ((0, 3), (1, 2)),
    22: ((2, 1),),
}
TRANSPORT_END = ((1, 3), (2, 2), (2, 3), (0, 4), (1, 4), (2, 4))


def advance(units, events):
    for matrix, stage in events:
        for side in range(2):
            units[2 * matrix + side].advance(stage)


def attend_kernel(plan, number, place, *refs):
    (embedded, wq, wk, wv, wo, cosine, sine, norms) = refs[:8]
    shards = refs[8 : 8 + number]
    (q, k, v, mixed_out, log_total, low_one, normal_one, inverse_one) = refs[8 + number : 16 + number]
    (low_two, normal_two, inverse_two) = refs[16 + number : 19 + number]
    gathered = refs[19 + number : 19 + 2 * number]
    scratch = refs[19 + 2 * number :]
    weights, mixed = scratch[:2]
    rows = embedded.shape[0]
    step = pl.program_id(0)
    if number:
        units = transport_units(plan, shards, gathered, *scratch[2:4])

        @pl.when(step == 0)
        def _():
            greet_neighbours(plan)

    def transport(part):
        if number:
            for slot, events in TRANSPORT_SLOTS.items():
                if slot % SLOTS_PER_STEP == part:

                    @pl.when(step == slot // SLOTS_PER_STEP)
                    def _():
                        advance(units, events)

    @pl.when(step == 0)
    def _():
        for start in range(0, rows, ROW_BLOCK):
            at = slice(start, start + ROW_BLOCK)
            normal, inverse = normalize(embedded[at, :])
            normal_one[at, :] = normal
            inverse_one[at, :] = inverse
            low_one[at, :] = (normal * norms[0:1, :] + norms[1:2, :]).astype(BF16)

    transport(0)
    weights[:, :LANES] = wq[...]
    weights[:, LANES : 2 * LANES] = wk[...]
    weights[:, 2 * LANES :] = wv[...]
    for start in range(0, rows, ROW_BLOCK):
        at = slice(start, start + ROW_BLOCK)
        made = dot(low_one[at, :], weights[...])
        query, key = made[:, :LANES], made[:, LANES : 2 * LANES]
        query = query * cosine[at, :] + swap_halves(query) * sine[at, :]
        key = key * cosine[at, :] + swap_halves(key) * sine[at, :]
        q[at, :] = (query * HEAD**-0.5).astype(BF16)
        k[at, :] = key.astype(BF16)
        v[at, :] = made[:, 2 * LANES :].astype(BF16)
    position = lax.broadcasted_iota(jnp.int32, (rows, 1), 0)
    bias = jnp.where(position < place[4], 0.0, masked_score)
    keys = k[...]
    values = v[...].T
    for start in range(0, rows, ROW_BLOCK):
        at = slice(start, start + ROW_BLOCK)
        if start > 0:
            transport(start // ROW_BLOCK)
        outs = []
        for head in range(LANES // HEAD):
            scores = dot_last(keys, of_head(q[at, :], head)) + bias
            top = jnp.max(scores, axis=0, keepdims=True)
            exponent = jnp.exp(scores - top)
            summed = jnp.sum(exponent, axis=0, keepdims=True)
            out = dot(values[head * HEAD : (head + 1) * HEAD, :], exponent.astype(BF16))
            outs.append(out / summed)
            log_total[head : head + 1, at] = top + jnp.log(summed)
        made = jnp.concatenate(outs, axis=0).T.astype(BF16)
        mixed_out[at, :] = made
        mixed[step, at, :] = made

    @pl.when(step == pl.num_programs(0) - 1)
    def _():
        per_part = wo.shape[2] // LANES
        for start in range(0, rows, ROW_BLOCK):
            at = slice(start, start + ROW_BLOCK)
            product = normal_one[at, :] * norms[0:1, :] + norms[1:2, :]
            for part in range(plan.tensor):
                whole_mixed = jnp.concatenate(
                    [mixed[part * per_part + n, at, :] for n in range(per_part)], axis=1
                )
                product = product + dot_last(whole_mixed, wo[part])
            normal, inverse = normalize(product)
            normal_two[at, :] = normal
            inverse_two[at, :] = inverse
            low_two[at, :] = (normal * norms[2:3, :] + norms[3:4, :]).astype(BF16)
        if number:
            advance(units, TRANSPORT_END)


def attend(plan, place, embedded, wq, wk, wv, wo, cosine, sine, norms, shards):
    rows, width = embedded.shape
    pairs = wq.shape[-1] // LANES
    steps = plan.tensor * pairs
    number = len(shards)

    def locate(i):
        return i // pairs, lax.rem(i, pairs)

    by_pair = pl.BlockSpec((None, rows, LANES), lambda i, place: (i, 0, 0))
    shape = jax.ShapeDtypeStruct((steps, rows, LANES), BF16)
    normed = [
        jax.ShapeDtypeStruct((rows, width), BF16),
        jax.ShapeDtypeStruct((rows, width), F32),
        jax.ShapeDtypeStruct((rows, 1), F32),
    ]
    normed_specs = [result((rows, width)), result((rows, width)), result((rows, 1))]
    scratch = [pltpu.VMEM((width, 3 * LANES), BF16), pltpu.VMEM((steps, rows, LANES), BF16)]
    more = {}
    if number:
        slots = transport_slots(plan)
        scratch += [pltpu.SemaphoreType.DMA((2 * number, slots))] * 2
        more = dict(collective_id=5, has_side_effects=True)
    outs = pl.pallas_call(
        functools.partial(attend_kernel, plan, number),
        name="attend",
        out_shape=[
            shape,
            shape,
            shape,
            jax.ShapeDtypeStruct((rows, steps * LANES), BF16),
            jax.ShapeDtypeStruct((steps, 8, rows), F32),
        ]
        + normed
        + normed
        + [plan.gathered_shape(shard) for shard in shards],
        grid_spec=pltpu.PrefetchScalarGridSpec(
            num_scalar_prefetch=1,
            grid=(steps,),
            in_specs=[whole((rows, width))]
            + [plan.weight_spec(width, LANES, locate)] * 3
            + [
                whole(wo.shape),
                whole((rows, LANES)),
                whole((rows, LANES)),
                whole(norms.shape),
            ]
            + [in_place()] * number,
            out_specs=[
                by_pair,
                by_pair,
                by_pair,
                pl.BlockSpec((rows, LANES), lambda i, place: (0, i)),
                pl.BlockSpec((None, 8, rows), lambda i, place: (i, 0, 0)),
            ]
            + normed_specs
            + normed_specs
            + [in_place()] * number,
            scratch_shapes=scratch,
        ),
        compiler_params=params(**more),
        cost_estimate=pl.CostEstimate(
            flops=8 * rows * width * width + 16 * rows * rows * width,
            bytes_accessed=rows * width * 30,
            transcendentals=0,
        ),
    )(place, embedded, wq, wk, wv, wo, cosine, sine, norms, *shards)
    return outs[:11], [w.reshape(plan.tensor, -1, w.shape[-1]) for w in outs[11:]]


def feed_kernel(
    plan,
    place,
    x,
    wg,
    wu,
    wd,
    normal_two,
    norms,
    gate_out,
    up_out,
    hidden_out,
    normal_out,
    inverse_out,
    pool_out,
):
    rows, width = x.shape
    first = pl.program_id(0) == 0

    @pl.when(first)
    def _():
        normal_out[...] = jnp.zeros_like(normal_out)

    for start in range(0, rows, ROW_BLOCK):
        at = slice(start, start + ROW_BLOCK)
        gate, up = dot(x[at, :], wg[...]), dot(x[at, :], wu[...])
        hidden = (gate * jax.nn.sigmoid(gate) * up).astype(BF16)
        gate_out[at, :] = gate.astype(BF16)
        up_out[at, :] = up.astype(BF16)
        hidden_out[at, :] = hidden
        normal_out[at, :] = normal_out[at, :] + dot_last(hidden, wd[...])

    @pl.when(pl.program_id(0) == pl.num_programs(0) - 1)
    def _():
        pooled = jnp.zeros((1, width), F32)
        for start in range(0, rows, ROW_BLOCK):
            at = slice(start, start + ROW_BLOCK)
            second_out = normal_two[at, :] * norms[2:3, :] + norms[3:4, :]
            normal, inverse = normalize(second_out + normal_out[at, :])
            normal_out[at, :] = normal
            inverse_out[at, :] = inverse
            position = start + lax.broadcasted_iota(jnp.int32, (ROW_BLOCK, 1), 0)
            kept = jnp.where(position < place[4], normal, 0.0)
            pooled = pooled + jnp.sum(kept, axis=0, keepdims=True)
        pool_out[...] = pooled


def feed(plan, place, x, wg, wu, wd, normal_two, norms):
    rows, width = x.shape
    hidden = wg.shape[-1]
    chunks = hidden // HIDDEN_BLOCK
    steps = plan.tensor * chunks

    def locate(i):
        return i // chunks, lax.rem(i, chunks)

    by_chunk = pl.BlockSpec((rows, HIDDEN_BLOCK), lambda i, place: (0, i))
    shape = jax.ShapeDtypeStruct((rows, plan.tensor * hidden), BF16)
    return pl.pallas_call(
        functools.partial(feed_kernel, plan),
        name="feed",
        out_shape=[
            shape,
            shape,
            shape,
            jax.ShapeDtypeStruct((rows, width), F32),
            jax.ShapeDtypeStruct((rows, 1), F32),
            jax.ShapeDtypeStruct((1, width), F32),
        ],
        grid_spec=pltpu.PrefetchScalarGridSpec(
            num_scalar_prefetch=1,
            grid=(steps,),
            in_specs=[
                whole((rows, width)),
                plan.weight_spec(width, HIDDEN_BLOCK, locate),
                plan.weight_spec(width, HIDDEN_BLOCK, locate),
                plan.weight_spec(width, HIDDEN_BLOCK, locate),
                whole((rows, width)),
                whole(norms.shape),
            ],
            out_specs=[
                by_chunk,
                by_chunk,
                by_chunk,
                result((rows, width)),
                result((rows, 1)),
                result((1, width)),
            ],
        ),
        compiler_params=params(),
        cost_estimate=pl.CostEstimate(
            flops=6 * rows * width * plan.tensor * hidden,
            bytes_accessed=rows * width * 40,
            transcendentals=0,
        ),
    )(place, x, wg, wu, wd, normal_two, norms)


def contrast_kernel(
    tensor, place, pool_ref, norms, scale_ref, loss_ref, grad_ref, held, own, send_sem, recv_sem
):
    count = held.shape[0]
    me = own_index(tensor)
    greet_all(me, count, tensor)
    length = jnp.full((1, 1), place[4], jnp.int32).astype(F32)
    pooled = pool_ref[...] / length * norms[4:5, :] + norms[5:6, :]
    inverse = lax.rsqrt(jnp.sum(pooled * pooled, axis=-1, keepdims=True) + norm_epsilon)
    vector = pooled * inverse
    own[...] = vector
    for start in (True, False):
        for_all(me, count, tensor, lambda peer: own, held.at[me], send_sem, recv_sem, start)
        if start:
            held[pl.ds(me, 1)] = vector[None]
    vectors = held[...].reshape(count, held.shape[2])
    scale = jnp.exp(scale_ref[...])
    logits = scale * lax.dot_general(
        vectors,
        vectors,
        (((1,), (1,)), ((), ())),
        precision=lax.Precision.HIGHEST,
        preferred_element_type=F32,
    )
    row = lax.broadcasted_iota(jnp.int32, (count, count), 0)
    column = lax.broadcasted_iota(jnp.int32, (count, count), 1)
    crossed = (lax.rem(row, 2) == 0) & (lax.rem(column, 2) == 1)
    shown = jnp.where(crossed, logits, masked_score)
    row_max = jnp.max(shown, axis=1, keepdims=True)
    row_exp = jnp.where(crossed, jnp.exp(shown - row_max), 0.0)
    row_sum = jnp.sum(row_exp, axis=1, keepdims=True)
    column_max = jnp.max(shown, axis=0, keepdims=True)
    column_exp = jnp.where(crossed, jnp.exp(shown - column_max), 0.0)
    column_sum = jnp.sum(column_exp, axis=0, keepdims=True)
    even = lax.rem(lax.broadcasted_iota(jnp.int32, (count, 1), 0), 2) == 0
    odd = lax.rem(lax.broadcasted_iota(jnp.int32, (1, count), 1), 2) == 1
    row_safe = jnp.where(even, row_sum, 1.0)
    column_safe = jnp.where(odd, column_sum, 1.0)
    row_lse = jnp.where(even, row_max + jnp.log(row_safe), 0.0)
    column_lse = jnp.where(odd, column_max + jnp.log(column_safe), 0.0)
    own = crossed & (column == row + 1)
    diagonal = jnp.sum(jnp.where(own, logits, 0.0))
    half = 1.0 / count
    loss = half * (jnp.sum(row_lse) + jnp.sum(column_lse) - 2.0 * diagonal)
    grad_logits = half * (
        row_exp / row_safe + column_exp / column_safe - 2.0 * own.astype(F32)
    )
    grad_scale = jnp.sum(grad_logits * jnp.where(crossed, logits, 0.0))
    both = grad_logits + grad_logits.T
    grad_vectors = scale * lax.dot_general(
        both,
        vectors,
        (((1,), (0,)), ((), ())),
        precision=lax.Precision.HIGHEST,
        preferred_element_type=F32,
    )
    mine = lax.broadcasted_iota(jnp.int32, (count, 1), 0) == me
    grad_own = jnp.sum(jnp.where(mine, grad_vectors, 0.0), axis=0, keepdims=True)
    along = jnp.sum(grad_own * vector, axis=-1, keepdims=True)
    grad_ref[...] = inverse * (grad_own - vector * along) / length
    lane = lax.broadcasted_iota(jnp.int32, loss_ref.shape, 1)
    loss_ref[...] = jnp.where(lane == 0, loss, grad_scale)


def contrast(plan, place, pool, norms, log_scale):
    width = pool.shape[1]
    loss, grad = pl.pallas_call(
        functools.partial(contrast_kernel, plan.tensor),
        name="contrast",
        out_shape=[
            jax.ShapeDtypeStruct((1, LANES), F32),
            jax.ShapeDtypeStruct((1, width), F32),
        ],
        in_specs=[pl.BlockSpec(memory_space=pltpu.SMEM)] + [in_vmem()] * 3,
        out_specs=[in_vmem()] * 2,
        scratch_shapes=[
            pltpu.VMEM((plan.count, 1, width), F32),
            pltpu.VMEM((1, width), F32),
            pltpu.SemaphoreType.DMA((plan.count - 1,)),
            pltpu.SemaphoreType.DMA((plan.count - 1,)),
        ],
        compiler_params=params(collective_id=2, has_side_effects=True),
    )(place, pool, norms, log_scale.reshape(1, 1))
    return loss[0, 0], loss[0, 1], grad


def feed_back_kernel(plan, steps, place, *refs):
    (
        grad_pool,
        x,
        gate_ref,
        up_ref,
        hidden_ref,
        wg,
        wu,
        wd,
        normal_three,
        inverse_three,
        normal_two,
        inverse_two,
        norms,
        part_one,
        part_two,
        grad_out,
        low_out,
        norm_out,
        peak_out,
        low,
        low_turned,
        x_turned,
        made,
        product,
    ) = refs[:24]
    rows, width = x.shape
    step = pl.program_id(0)
    half = BACK_BLOCK // 2
    if plan.stepped:
        sums = SiblingSum.made_of(plan, steps, refs[24:-4])
        exchange = PeakExchange(plan, *refs[-4:])
    else:
        sums = SiblingSum.made_of(plan, steps, refs[24:])

    @pl.when(step == 0)
    def _():
        if plan.stepped:
            exchange.greet([sums.sibling])
        for start in range(0, rows, ROW_BLOCK):
            at = slice(start, start + ROW_BLOCK)
            position = start + lax.broadcasted_iota(jnp.int32, (ROW_BLOCK, 1), 0)
            grad_third = jnp.where(position < place[4], grad_pool[...], 0.0)
            grad = normalize_back(
                grad_third, normal_three[at, :], inverse_three[at, :], norms[4:5, :]
            )
            grad_out[at, :] = grad
            low[at, :] = grad.astype(BF16)
            low_turned[:, at] = grad.astype(BF16).T
            x_turned[:, at] = x[at, :].T

    @pl.when(step < steps)
    def _():
        for start in range(0, rows, ROW_BLOCK):
            at = slice(start, start + ROW_BLOCK)
            grad_hidden = dot(low[at, :], wd[...])
            gate = gate_ref[at, :].astype(F32)
            up = up_ref[at, :].astype(F32)
            share_gate = jax.nn.sigmoid(gate)
            grad_up = grad_hidden * gate * share_gate
            grad_gate = grad_hidden * up * share_gate * (1.0 + gate * (1.0 - share_gate))
            made[at, :BACK_BLOCK] = grad_gate.astype(BF16)
            made[at, BACK_BLOCK:] = grad_up.astype(BF16)
            grad_out[at, :] = (
                grad_out[at, :]
                + dot_last(made[at, :BACK_BLOCK], wg[...])
                + dot_last(made[at, BACK_BLOCK:], wu[...])
            )
        down = dot(low_turned[...], hidden_ref[...])
        product[:, :BACK_BLOCK] = dot(x_turned[...], made[:, :BACK_BLOCK])
        product[:, BACK_BLOCK : BACK_BLOCK + half] = down[:, :half]
        product[:, BACK_BLOCK + half : 2 * BACK_BLOCK + half] = dot(
            x_turned[...], made[:, BACK_BLOCK:]
        )
        product[:, 2 * BACK_BLOCK + half :] = down[:, half:]
        sums.push(step, product)

    @pl.when(step > 0)
    def _():
        sums.pull(step - 1, (part_one, part_two), (BACK_BLOCK + half,) * 2, peak_out)

    @pl.when(step == steps)
    def _():
        gain_grad = jnp.zeros((1, width), F32)
        shift_grad = jnp.zeros((1, width), F32)
        if plan.stepped:
            exchange.start(0, peak_out[...])
        for start in range(0, rows, ROW_BLOCK):
            at = slice(start, start + ROW_BLOCK)
            if plan.stepped and start == rows // 2:
                exchange.start(1, exchange.finish(0))
            grad_second = grad_out[at, :]
            normal = normal_two[at, :]
            grad = normalize_back(grad_second, normal, inverse_two[at, :], norms[2:3, :])
            gain_grad = gain_grad + jnp.sum(grad_second * normal, axis=0, keepdims=True)
            shift_grad = shift_grad + jnp.sum(grad_second, axis=0, keepdims=True)
            grad_out[at, :] = grad
            low_out[at, :] = grad.astype(BF16)
        norm_out[0:1, :] = gain_grad
        norm_out[1:2, :] = shift_grad
        if plan.stepped:
            peak_out[...] = exchange.finish(1)


def feed_back(
    plan,
    place,
    grad_pool,
    x,
    gate,
    up,
    hidden_low,
    wg,
    wu,
    wd,
    normal_three,
    inverse_three,
    normal_two,
    inverse_two,
    norms,
):
    rows, width = x.shape
    hidden = wg.shape[-1]
    chunks = hidden // BACK_BLOCK
    steps = plan.tensor * chunks

    def locate(i):
        now = jnp.minimum(i, steps - 1)
        return now // chunks, lax.rem(now, chunks)

    def locate_late(i):
        now = jnp.maximum(i - 1, 0)
        return now // chunks, lax.rem(now, chunks)

    by_chunk = pl.BlockSpec(
        (rows, BACK_BLOCK), lambda i, place: (0, jnp.minimum(i, steps - 1))
    )
    columns = BACK_BLOCK * 3 // 2
    return pl.pallas_call(
        functools.partial(feed_back_kernel, plan, steps),
        name="feed_back",
        out_shape=[
            plan.grad_shape("yx", columns * chunks),
            plan.grad_shape("xy", columns * chunks),
            jax.ShapeDtypeStruct((rows, width), F32),
            jax.ShapeDtypeStruct((rows, width), BF16),
            jax.ShapeDtypeStruct((8, width), F32),
            jax.ShapeDtypeStruct((8, LANES), F32),
        ],
        grid_spec=pltpu.PrefetchScalarGridSpec(
            num_scalar_prefetch=1,
            grid=(steps + 1,),
            in_specs=[
                whole((1, width)),
                whole((rows, width)),
                by_chunk,
                by_chunk,
                by_chunk,
                plan.weight_spec(width, BACK_BLOCK, locate),
                plan.weight_spec(width, BACK_BLOCK, locate),
                plan.weight_spec(width, BACK_BLOCK, locate),
                whole((rows, width)),
                whole((rows, 1)),
                whole((rows, width)),
                whole((rows, 1)),
                whole(norms.shape),
            ],
            out_specs=[
                plan.grad_spec("yx", columns, locate_late),
                plan.grad_spec("xy", columns, locate_late),
                result((rows, width)),
                result((rows, width)),
                result((8, width)),
                result((8, LANES)),
            ],
            scratch_shapes=[
                pltpu.VMEM((rows, width), BF16),
                pltpu.VMEM((width, rows), BF16),
                pltpu.VMEM((width, rows), BF16),
                pltpu.VMEM((rows, 2 * BACK_BLOCK), BF16),
                pltpu.VMEM((width, 3 * BACK_BLOCK), F32),
            ]
            + SiblingSum.scratch(plan, 3 * BACK_BLOCK)
            + (PeakExchange.scratch(plan) if plan.stepped else []),
        ),
        compiler_params=SiblingSum.params(plan, 6),
        cost_estimate=pl.CostEstimate(
            flops=20 * rows * width * plan.tensor * hidden,
            bytes_accessed=rows * width * 60,
            transcendentals=0,
        ),
    )(
        place,
        grad_pool,
        x,
        gate,
        up,
        hidden_low,
        wg,
        wu,
        wd,
        normal_three,
        inverse_three,
        normal_two,
        inverse_two,
        norms,
    )


def unfold_feed(part_one, part_two, hidden):
    rows = part_one.shape[0]
    half = BACK_BLOCK // 2
    one = part_one.reshape(rows, hidden // BACK_BLOCK, BACK_BLOCK + half)
    two = part_two.reshape(rows, hidden // BACK_BLOCK, BACK_BLOCK + half)
    down = jnp.concatenate([one[:, :, BACK_BLOCK:], two[:, :, BACK_BLOCK:]], axis=2)
    return (
        one[:, :, :BACK_BLOCK].reshape(rows, hidden),
        two[:, :, :BACK_BLOCK].reshape(rows, hidden),
        down.reshape(rows, hidden),
    )


def heads_back_kernel(
    place, ga, q, k, v, mixed, log_total, wo, cosine, sine, made, gm, key_grad, value_grad
):
    rows = ga.shape[0]
    for start in range(0, rows, ROW_BLOCK):
        at = slice(start, start + ROW_BLOCK)
        gm[at, :] = dot(ga[at, :], wo[...]).astype(BF16)
    position = lax.broadcasted_iota(jnp.int32, (rows, 1), 0)
    bias = jnp.where(position < place[4], 0.0, masked_score)
    keys, values = k[...], v[...]
    keys_turned = keys.T
    for start in range(0, rows, ROW_BLOCK):
        at = slice(start, start + ROW_BLOCK)
        inner = (gm[at, :].astype(F32) * mixed[at, :].astype(F32)).T
        outs = []
        for head in range(LANES // HEAD):
            of = slice(head * HEAD, (head + 1) * HEAD)
            query = of_head(q[at, :], head)
            grad = of_head(gm[at, :], head)
            inner_sum = jnp.sum(inner[of, :], axis=0, keepdims=True)
            scores = dot_last(keys, query) + bias
            probs = jnp.exp(scores - log_total[head : head + 1, at])
            grad_probs = dot_last(values, grad)
            grad_scores = (probs * (grad_probs - inner_sum)).astype(BF16)
            value_part = dot(probs.astype(BF16), grad)
            key_part = dot(grad_scores, query)
            if start == 0 and head == 0:
                value_grad[...] = value_part
                key_grad[...] = key_part
            else:
                value_grad[...] = value_grad[...] + value_part
                key_grad[...] = key_grad[...] + key_part
            outs.append(dot(keys_turned[of, :], grad_scores))
        grad_query = jnp.concatenate(outs, axis=0).T * HEAD**-0.5
        grad_query = grad_query * cosine[at, :] - swap_halves(grad_query) * sine[at, :]
        made[at, :LANES] = grad_query.astype(BF16)
    for start in range(0, rows, ROW_BLOCK):
        at = slice(start, start + ROW_BLOCK)
        grad_key = key_grad[at, :]
        grad_key = grad_key * cosine[at, :] - swap_halves(grad_key) * sine[at, :]
        made[at, LANES : 2 * LANES] = grad_key.astype(BF16)
        made[at, 2 * LANES :] = value_grad[at, :].astype(BF16)


def heads_back(plan, place, first, number, ga, q, k, v, mixed, log_total, wo, cosine, sine):
    rows, width = ga.shape
    pairs = wo.shape[-1] // LANES

    def locate(i):
        now = first + i
        return now // pairs, lax.rem(now, pairs)

    by_pair = pl.BlockSpec((None, rows, LANES), lambda i, place: (first + i, 0, 0))
    return pl.pallas_call(
        heads_back_kernel,
        name="heads_back",
        out_shape=jax.ShapeDtypeStruct((number, rows, 3 * LANES), BF16),
        grid_spec=pltpu.PrefetchScalarGridSpec(
            num_scalar_prefetch=1,
            grid=(number,),
            in_specs=[
                whole((rows, width)),
                by_pair,
                by_pair,
                by_pair,
                pl.BlockSpec((rows, LANES), lambda i, place: (0, first + i)),
                pl.BlockSpec((None, 8, rows), lambda i, place: (first + i, 0, 0)),
                plan.weight_spec(width, LANES, locate),
                whole((rows, LANES)),
                whole((rows, LANES)),
            ],
            out_specs=pl.BlockSpec((None, rows, 3 * LANES), lambda i, place: (i, 0, 0)),
            scratch_shapes=[
                pltpu.VMEM((rows, LANES), BF16),
                pltpu.VMEM((rows, LANES), F32),
                pltpu.VMEM((rows, LANES), F32),
            ],
        ),
        compiler_params=params(),
        cost_estimate=pl.CostEstimate(
            flops=number * 80 * rows * rows * LANES,
            bytes_accessed=rows * width * 2,
            transcendentals=0,
        ),
    )(place, ga, q, k, v, mixed, log_total, wo, cosine, sine)


def first_back_kernel(plan, number, *refs):
    groups = refs[:number]
    (wq, wk, wv, grad_res, normal_one, inverse_one, norms, peak) = refs[number : number + 8]
    low_out, norm_out, peak_out = refs[number + 8 : number + 11]
    step = pl.program_id(0)
    if plan.stepped:
        exchange = PeakExchange(plan, *refs[number + 11 :])

        @pl.when(step == 0)
        def _():
            exchange.greet()
            exchange.start(0, peak[...])

        @pl.when(step == 1)
        def _():
            exchange.start(1, exchange.finish(0))

    pairs = wq.shape[-1] // LANES
    total_grad = grad_res[...]
    places = [(group, n) for group in groups for n in range(group.shape[0])]
    for part in range(plan.tensor):
        for kind, weight in enumerate((wq, wk, wv)):
            lanes = slice(kind * LANES, (kind + 1) * LANES)
            made = []
            for group, n in places[part * pairs : (part + 1) * pairs]:
                made.append(group[n, :, lanes])
            total_grad = total_grad + dot_last(jnp.concatenate(made, axis=1), weight[part])
    normal = normal_one[...]
    grad = normalize_back(total_grad, normal, inverse_one[...], norms[0:1, :])
    low_out[...] = grad.astype(BF16)
    gain_grad = jnp.sum(total_grad * normal, axis=0, keepdims=True)
    shift_grad = jnp.sum(total_grad, axis=0, keepdims=True)

    @pl.when(pl.program_id(0) == 0)
    def _():
        norm_out[...] = jnp.zeros_like(norm_out)

    norm_out[0:1, :] = norm_out[0:1, :] + gain_grad
    norm_out[1:2, :] = norm_out[1:2, :] + shift_grad
    if plan.stepped:

        @pl.when(step == pl.num_programs(0) - 1)
        def _():
            peak_out[...] = exchange.finish(1)


def first_back(plan, groups, wq, wk, wv, grad_res, normal_one, inverse_one, norms, peak):
    rows, width = grad_res.shape
    by_rows = pl.BlockSpec((ROW_BLOCK, width), lambda i: (i, 0))

    def fixed(shape, **more):
        zeros = (0,) * len(shape)
        return pl.BlockSpec(shape, lambda i: zeros, **more)

    return pl.pallas_call(
        functools.partial(first_back_kernel, plan, len(groups)),
        name="first_back",
        out_shape=[
            jax.ShapeDtypeStruct((rows, width), BF16),
            jax.ShapeDtypeStruct((8, width), F32),
            jax.ShapeDtypeStruct((8, LANES), F32),
        ],
        grid=(rows // ROW_BLOCK,),
        in_specs=[
            pl.BlockSpec((g.shape[0], ROW_BLOCK, g.shape[2]), lambda i: (0, i, 0)) for g in groups
        ]
        + [fixed(wq.shape, pipeline_mode=pl.Buffered(1))] * 3
        + [
            by_rows,
            by_rows,
            pl.BlockSpec((ROW_BLOCK, 1), lambda i: (i, 0)),
            fixed(norms.shape),
            fixed((8, LANES)),
        ],
        out_specs=[by_rows, fixed((8, width)), fixed((8, LANES))],
        scratch_shapes=PeakExchange.scratch(plan) if plan.stepped else [],
        compiler_params=(
            params(collective_id=3, has_side_effects=True) if plan.stepped else params()
        ),
        cost_estimate=pl.CostEstimate(
            flops=8 * rows * width * width, bytes_accessed=rows * width * 20, transcendentals=0
        ),
    )(*groups, wq, wk, wv, grad_res, normal_one, inverse_one, norms, peak)


def attend_weights_kernel(plan, steps, number, *refs):
    groups = refs[:number]
    (x, ga, mixed, part_one, part_two, peak_out, x_turned, ga_turned, product) = refs[
        number : number + 9
    ]
    rows, width = x.shape
    step = pl.program_id(0)
    sums = SiblingSum.made_of(plan, steps, refs[number + 9 :])

    @pl.when(step == 0)
    def _():
        sums.greet()
        for start in range(0, rows, ROW_BLOCK):
            at = slice(start, start + ROW_BLOCK)
            ga_turned[:, at] = ga[at, :].T
            x_turned[:, at] = x[at, :].T

    begin = 0
    for group in groups:
        size = group.shape[0]

        @pl.when((step >= begin) & (step < begin + size))
        def _():
            product[:, : 3 * LANES] = dot(x_turned[...], group[step - begin])

        begin += size

    @pl.when(step < steps)
    def _():
        product[:, 3 * LANES :] = dot(ga_turned[...], mixed[...])
        sums.push(step, product)

    @pl.when(step > 0)
    def _():
        sums.pull(step - 1, (part_one, part_two), (2 * LANES,) * 2, peak_out)


def attend_weights(plan, groups, x, ga, mixed, part):
    rows, width = x.shape
    pairs = part // LANES
    steps = plan.tensor * pairs

    def late(order):
        def locate(i):
            now = jnp.maximum(i - 1, 0)
            return now // pairs, lax.rem(now, pairs)

        spec = plan.grad_spec(order, 2 * LANES, locate)
        return pl.BlockSpec(spec.block_shape, lambda i: spec.index_map(i, None))

    def fixed(shape):
        zeros = (0,) * len(shape)
        return pl.BlockSpec(shape, lambda i: zeros, pipeline_mode=pl.Buffered(1))

    return pl.pallas_call(
        functools.partial(attend_weights_kernel, plan, steps, len(groups)),
        name="attend_weights",
        out_shape=[
            plan.grad_shape("yx", 2 * part),
            plan.grad_shape("xy", 2 * part),
            jax.ShapeDtypeStruct((8, LANES), F32),
        ],
        grid=(steps + 1,),
        in_specs=[fixed(g.shape) for g in groups]
        + [
            fixed((rows, width)),
            fixed((rows, width)),
            pl.BlockSpec((rows, LANES), lambda i: (0, jnp.minimum(i, steps - 1))),
        ],
        out_specs=[
            late("yx"),
            late("xy"),
            pl.BlockSpec((8, LANES), lambda i: (0, 0)),
        ],
        scratch_shapes=[
            pltpu.VMEM((width, rows), BF16),
            pltpu.VMEM((width, rows), BF16),
            pltpu.VMEM((width, 4 * LANES), F32),
        ]
        + SiblingSum.scratch(plan, 4 * LANES),
        compiler_params=SiblingSum.params(plan, 7),
        cost_estimate=pl.CostEstimate(
            flops=12 * rows * width * width, bytes_accessed=rows * width * 20, transcendentals=0
        ),
    )(*groups, x, ga, mixed)


def unfold_attend(part_one, part_two):
    rows, columns = part_one.shape
    one = part_one.reshape(rows, columns // (2 * LANES), 2, LANES)
    two = part_two.reshape(rows, columns // (2 * LANES), 2, LANES)
    return [side[:, :, n].reshape(rows, columns // 2) for side in (one, two) for n in (0, 1)]


def adam_step(weight, first_moment, second_moment, gradient, factor):
    clipped = gradient * factor
    first_next = beta_one * first_moment + (1.0 - beta_one) * clipped
    second_next = beta_two * second_moment + (1.0 - beta_two) * clipped * clipped
    corrected_first = first_next / (1.0 - beta_one**STEP)
    corrected_second = second_next / (1.0 - beta_two**STEP)
    change = -learn_rate * (
        corrected_first / (jnp.sqrt(corrected_second) + adam_epsilon) + weight_decay * weight
    )
    return (first_next, second_next, change)


def per_device(
    plan,
    token_ids,
    lengths,
    token_table,
    table_first,
    table_second,
    qkv_weight,
    qkv_first,
    qkv_second,
    out_weight,
    out_first,
    out_second,
    gate_up_weight,
    gate_up_first,
    gate_up_second,
    down_weight,
    down_first,
    down_second,
    norm_params,
    norm_first,
    norm_second,
    log_inverse_warmth,
    scale_first,
    scale_second,
):
    slot_ids = token_ids[0]
    rows = slot_ids.shape[0]
    vocab_shard, width = token_table.shape
    own_length = lax.dynamic_index_in_dim(
        lengths[0], lax.axis_index("tensor"), 0, keepdims=False
    ).astype(jnp.int32)
    place = jnp.stack([jnp.asarray(p, jnp.int32) for p in plan.places()] + [own_length])
    me = lax.axis_index(AXES)

    qkv_low = qkv_weight.astype(BF16)
    gate_up_low = gate_up_weight.astype(BF16)
    early = [qkv_low[:, 0], qkv_low[:, 1], qkv_low[:, 2], out_weight.astype(BF16)]
    late = [gate_up_low[:, 0], gate_up_low[:, 1], down_weight.astype(BF16)]

    table_low = token_table.astype(BF16)
    room = 8 * -(-(5 * rows) // (4 * plan.count * 8))
    slots = room * plan.count
    owner, row, first, token_place = token_places(slot_ids, own_length, vocab_shard)
    slot = round_slots(owner, token_place, room, 0)
    wants = round_wants(slot, first, row, slots).reshape(plan.count, room)
    rounds = jnp.max(token_place) // room + 1
    note = jnp.concatenate(
        [wants, jnp.broadcast_to(rounds, (plan.count, 8 * LANES - room))], axis=1
    )
    notes = swap_blocks(plan, note.reshape(plan.count, 8, LANES)).reshape(plan.count, 8 * LANES)
    asked = notes[:, :room]
    rounds = jnp.max(notes[:, room])
    picked = picked_rows(asked, table_low)
    if plan.stepped:
        half = width // 2
        folded = jnp.concatenate(
            [
                picked[:, :half].reshape(plan.count, room, half),
                picked[:, half:].reshape(plan.count, room, half),
            ],
            axis=1,
        )
        came, (wq, wk, wv, wo) = fetch(
            plan, folded, early, (("x", "y"), ("y", "x"), ("x", "y"), ("y", "x"))
        )
        came = jnp.concatenate([came[:, :room], came[:, room:]], axis=2).reshape(slots, width)
    else:
        came = swap_rows(plan, picked)
        wq, wk, wv, wo = [plan.gather_whole(shard) for shard in early]
    embedded = spread_rows(slot, came)

    def ask(turn):
        later = round_slots(owner, token_place, room, turn)
        later_wants = round_wants(later, first, row, slots).reshape(plan.count, room)
        return later, lax.all_to_all(later_wants, AXES, 0, 0, tiled=True)

    def fetch_more(turn, sofar):
        later, later_asked = ask(turn)
        return sofar + spread_rows(later, swap_rows(plan, picked_rows(later_asked, table_low)))

    embedded = lax.fori_loop(1, rounds, fetch_more, embedded)
    cosine, sine = rotary_tables(rows)
    made, gathered = attend(
        plan,
        place,
        embedded,
        wq,
        wk,
        wv,
        wo,
        cosine,
        sine,
        norm_params,
        late if plan.stepped else [],
    )
    q, k, v, mixed, log_total, first_low, normal_one, inverse_one = made[:8]
    second_low, normal_two, inverse_two = made[8:]
    if plan.stepped:
        wg, wu, wd = gathered
    else:
        wg, wu, wd = [plan.gather_whole(shard) for shard in late]
    gate, up, hidden_low, normal_three, inverse_three, pool = feed(
        plan, place, second_low, wg, wu, wd, normal_two, norm_params
    )
    batch_loss, grad_log_scale, grad_pool = contrast(
        plan, place, pool, norm_params, log_inverse_warmth
    )
    part_one, part_two, grad_first_res, attended_low, norm_two, peak_two = feed_back(
        plan,
        place,
        grad_pool,
        second_low,
        gate,
        up,
        hidden_low,
        wg,
        wu,
        wd,
        normal_three,
        inverse_three,
        normal_two,
        inverse_two,
        norm_params,
    )
    scale_two = wire_scale(plan, peak_two)
    steps = q.shape[0]
    cut = steps * 2 // 3

    def heads(first, number, grad):
        return heads_back(
            plan, place, first, number, grad, q, k, v, mixed, log_total, wo, cosine, sine
        )

    if plan.stepped:
        part_one = plan.step_along(part_one, "y", scale_two)
        part_two = plan.step_along(part_two, "x", scale_two)
        group_one = heads(0, cut, attended_low)
        part_one, part_two, ready = lax.optimization_barrier((part_one, part_two, attended_low))
        part_one = plan.step_along(part_one, "x", scale_two)
        part_two = plan.step_along(part_two, "y", scale_two)
        group_two = heads(cut, steps - cut, ready)
        part_one, part_two, ready = lax.optimization_barrier((part_one, part_two, attended_low))
        shard_one = plan.step_along(part_one, "z", scale_two)
        shard_two = plan.step_along(part_two, "z", scale_two)
        groups = [group_one, group_two]
    else:
        shard_one, shard_two = plan.scatter_whole(part_one), plan.scatter_whole(part_two)
        groups = [heads(0, steps, attended_low)]
        ready = attended_low
    part_three, part_four, peak_one = attend_weights(
        plan, groups, first_low, ready, mixed, wq.shape[-1]
    )
    peak_one, shard_one, shard_two = lax.optimization_barrier((peak_one, shard_one, shard_two))
    embedded_low, norm_one, peak_one = first_back(
        plan, groups, wq, wk, wv, grad_first_res, normal_one, inverse_one, norm_params, peak_one
    )
    scale_one = wire_scale(plan, peak_one)
    grad_rows = summed_rows(slot, embedded_low, slots).astype(BF16)
    shard_three = plan.scatter(part_three, "yx", scale_one)
    shard_four = plan.scatter(part_four, "xy", scale_one)
    grad_table = summed_rows(asked.reshape(-1), swap_rows(plan, grad_rows), vocab_shard)

    def return_more(turn, sofar):
        later, later_asked = ask(turn)
        later_rows = summed_rows(later, embedded_low, slots).astype(BF16)
        return sofar + summed_rows(
            later_asked.reshape(-1), swap_rows(plan, later_rows), vocab_shard
        )

    grad_table = lax.fori_loop(1, rounds, return_more, grad_table)
    owned_squares = jnp.sum(grad_table * grad_table)
    for shard in (shard_one, shard_two, shard_three, shard_four):
        owned_squares = owned_squares + jnp.sum(shard * shard)
    grad_gate, grad_up, grad_down_own = unfold_feed(shard_one, shard_two, wg.shape[-1])
    grad_q, grad_k, grad_v, grad_out_own = unfold_attend(shard_three, shard_four)
    grad_qkv_own = jnp.stack([grad_q, grad_k, grad_v], axis=1)
    grad_gate_own = jnp.stack([grad_gate, grad_up], axis=1)
    length_float = own_length.astype(F32)
    norm_grads, square_total = total(
        plan,
        jnp.concatenate(
            [
                norm_one[0:2],
                norm_two[0:2],
                grad_pool * pool,
                grad_pool * length_float,
            ],
            axis=0,
        ).reshape(-1),
        owned_squares,
    )
    norm_grads = norm_grads.reshape(norm_params.shape)
    squares = square_total + jnp.sum(norm_grads * norm_grads) + grad_log_scale * grad_log_scale
    grad_norm = jnp.sqrt(squares)
    factor = jnp.minimum(1.0, clip_limit / (grad_norm + 1e-06))
    return (
        (batch_loss, grad_norm)
        + adam_step(token_table, table_first, table_second, grad_table, factor)
        + adam_step(qkv_weight, qkv_first, qkv_second, grad_qkv_own, factor)
        + adam_step(out_weight, out_first, out_second, grad_out_own, factor)
        + adam_step(gate_up_weight, gate_up_first, gate_up_second, grad_gate_own, factor)
        + adam_step(down_weight, down_first, down_second, grad_down_own, factor)
        + adam_step(norm_params, norm_first, norm_second, norm_grads, factor)
        + adam_step(log_inverse_warmth, scale_first, scale_second, grad_log_scale, factor)
    )


def solution(mesh):
    rows = P(AXES, None)
    deep = P("dp", None, "tensor")
    flat = P("dp", "tensor")
    in_specs = (
        (rows, P("dp", None)) + (rows,) * 3 + (deep,) * 3 + (flat,) * 3 + (deep,) * 3 + (flat,) * 3
    ) + (P(),) * 6
    out_specs = (
        (P(), P()) + (rows,) * 3 + (deep,) * 3 + (flat,) * 3 + (deep,) * 3 + (flat,) * 3
    ) + (P(),) * 6

    def run(*args):
        plan = Plan(mesh, args[2].shape[1])
        return jax.shard_map(
            functools.partial(per_device, plan),
            mesh=mesh,
            in_specs=in_specs,
            out_specs=out_specs,
            check_vma=False,
        )(*args)

    return run
```

```python
import functools

import jax
import jax.numpy as jnp
from jax import lax
from jax.experimental import pallas as pl
from jax.experimental.pallas import tpu as pltpu
from jax.sharding import PartitionSpec as P

HEAD = 64
STEP = 8

norm_epsilon = 1e-12
rope_base = 1000.0
beta_one = 0.9
beta_two = 0.999
adam_epsilon = 1e-08
learn_rate = 0.01
weight_decay = 0.01
clip_limit = 0.001
masked_score = -1e30

AXES = ("dp", "tensor")
F32 = jnp.float32
BF16 = jnp.bfloat16
LANES = 128
VMEM_LIMIT = 58 * 1024 * 1024
ROW_BLOCK = 256
HIDDEN_BLOCK = 256
BACK_BLOCK = 512


class Plan:
    def __init__(self, mesh, width):
        self.dp = mesh.shape["dp"]
        self.tensor = mesh.shape["tensor"]
        self.count = self.dp * self.tensor
        self.shard = width // self.dp
        self.stepped = self.dp % 4 == 0 and self.shard % 16 == 0
        if self.stepped:
            self.nc, self.nx, self.nz = 2, 2, self.dp // 4
        else:
            self.nc, self.nx, self.nz = 1, 1, 1
        self.rows = width // (self.nc * self.nx * self.nz)

    def places(self):
        dp_index, tensor_index = lax.axis_index("dp"), lax.axis_index("tensor")
        if not self.stepped:
            zero = jnp.int32(0)
            return zero, zero, zero, zero
        core = lax.rem(dp_index, self.nc)
        across = lax.rem(dp_index // self.nc, self.nx)
        return dp_index // (self.nc * self.nx), across, core, tensor_index

    def size(self, axis):
        return {"z": self.nz, "x": self.nx, "c": self.nc, "y": self.tensor}[axis]

    def shift(self, values, axis, by):
        pairs = []
        for z in range(self.nz):
            for x in range(self.nx):
                for c in range(self.nc):
                    for y in range(self.tensor):
                        place = {"z": z, "x": x, "c": c, "y": y}
                        source = self.flat(place)
                        place[axis] = (place[axis] + by) % self.size(axis)
                        pairs.append((source, self.flat(place)))
        return lax.ppermute(values, AXES, pairs)

    def flat(self, place):
        dp_index = (place["z"] * self.nx + place["x"]) * self.nc + place["c"]
        return dp_index * self.tensor + place["y"]

    def gather_whole(self, values):
        whole = lax.all_gather(values, ("tensor", "dp"), axis=0, tiled=True)
        return whole.reshape(self.tensor, -1, values.shape[1])

    def gathered_shape(self, shard):
        rows, columns = shard.shape
        return jax.ShapeDtypeStruct(
            (self.tensor, self.nz, self.nx, self.nc, rows, columns), shard.dtype
        )

    def scatter_whole(self, part):
        whole = part.reshape(self.tensor * self.rows, part.shape[-1])
        return lax.psum_scatter(whole, ("tensor", "dp"), scatter_dimension=0, tiled=True)

    def step_along(self, total, axis, scale):
        own_y = lax.axis_index("tensor")
        pick = functools.partial(lax.dynamic_index_in_dim, total, axis=0, keepdims=False)
        kept = pick(own_y) if axis == "y" else total[0]
        for far in range(1, self.size(axis)):
            other = pick(lax.rem(own_y + far, self.tensor)) if axis == "y" else total[far]
            sent = (other * scale).astype(jnp.float16)
            kept = kept + self.shift(sent, axis, far).astype(F32) / scale
        return kept

    def scatter(self, part, order, scale):
        if not self.stepped:
            return self.scatter_whole(part)
        for axis in tuple(order) + ("z",):
            part = self.step_along(part, axis, scale)
        return part


    def weight_spec(self, width, columns, locate):
        def index(i, place):
            part, column = locate(i)
            return (part, 0, column)

        return pl.BlockSpec((None, width, columns), index)

    def grad_spec(self, order, columns, locate):
        def index(i, place):
            part, column = locate(i)
            if order == "yx":
                return (part, 0, 0, 0, column)
            return (0, part, 0, 0, column)

        middle = (None, self.nx) if order == "yx" else (self.nx, None)
        return pl.BlockSpec(middle + (self.nz, self.rows, columns), index)

    def grad_shape(self, order, columns):
        middle = (self.tensor, self.nx) if order == "yx" else (self.nx, self.tensor)
        return jax.ShapeDtypeStruct(middle + (self.nz, self.rows, columns), F32)


class SiblingSum:
    def __init__(self, plan, steps, kept, sent, came, send_sem, recv_sem, free_sem):
        self.plan, self.steps = plan, steps
        self.kept, self.sent, self.came = kept, sent, came
        self.send_sem, self.recv_sem, self.free_sem = send_sem, recv_sem, free_sem
        dp_index, self.y = lax.axis_index("dp"), lax.axis_index("tensor")
        self.c = lax.rem(dp_index, plan.nc)
        self.x = lax.rem(dp_index // plan.nc, plan.nx)
        self.z = dp_index // (plan.nc * plan.nx)
        self.sibling = (dp_index + 1 - 2 * self.c, self.y)

    def greet(self):
        if self.plan.nc > 1:
            barrier = pltpu.get_barrier_semaphore()
            pl.semaphore_signal(
                barrier, inc=1, device_id=self.sibling, device_id_type=pl.DeviceIdType.MESH
            )
            pl.semaphore_wait(barrier, 1)

    def copy(self, slot):
        return pltpu.make_async_remote_copy(
            src_ref=self.sent.at[slot],
            dst_ref=self.came.at[slot],
            send_sem=self.send_sem.at[slot],
            recv_sem=self.recv_sem.at[slot],
            device_id=self.sibling,
            device_id_type=pl.DeviceIdType.MESH,
        )

    def push(self, step, product):
        plan = self.plan
        slot = lax.rem(step, 2)
        if plan.nc > 1:

            @pl.when(step >= 2)
            def _():
                self.copy(slot).wait_send()
                pl.semaphore_wait(self.free_sem, 1)

        for far_x in range(plan.nx):
            x = lax.rem(self.x + far_x, plan.nx)
            for far_z in range(plan.nz):
                z = lax.rem(self.z + far_z, plan.nz)
                base = (z * plan.nx + x) * plan.nc
                to = slice(
                    (far_x * plan.nz + far_z) * plan.rows,
                    (far_x * plan.nz + far_z + 1) * plan.rows,
                )
                start = pl.multiple_of((base + self.c) * plan.rows, 16)
                self.kept[slot, to, :] = product[pl.ds(start, plan.rows), :]
                if plan.nc > 1:
                    start = pl.multiple_of((base + 1 - self.c) * plan.rows, 16)
                    self.sent[slot, to, :] = product[pl.ds(start, plan.rows), :]
        if plan.nc > 1:
            self.copy(slot).start()

    def pull(self, step, targets, widths, peak_out):
        plan = self.plan
        slot = lax.rem(step, 2)
        if plan.nc > 1:
            self.copy(slot).wait_recv()
        peak = jnp.zeros((1, 1), F32)
        for far_x in range(plan.nx):
            for far_z in range(plan.nz):
                at = slice(
                    (far_x * plan.nz + far_z) * plan.rows,
                    (far_x * plan.nz + far_z + 1) * plan.rows,
                )
                value = self.kept[slot, at, :]
                if plan.nc > 1:
                    value = value + self.came[slot, at, :]
                start = 0
                for target, width in zip(targets, widths):
                    target[far_x, far_z] = value[:, start : start + width]
                    start += width
                largest = jnp.max(jnp.abs(value), axis=0, keepdims=True)
                peak = jnp.maximum(peak, jnp.max(largest, axis=1, keepdims=True))
        if plan.nc > 1:

            @pl.when(step < self.steps - 2)
            def _():
                pl.semaphore_signal(
                    self.free_sem,
                    inc=1,
                    device_id=self.sibling,
                    device_id_type=pl.DeviceIdType.MESH,
                )

            @pl.when(step == self.steps - 1)
            def _():
                for last in range(max(self.steps - 2, 0), self.steps):
                    self.copy(last % 2).wait_send()

        peak = jnp.broadcast_to(peak, peak_out.shape)

        @pl.when(step == 0)
        def _():
            peak_out[...] = peak

        @pl.when(step > 0)
        def _():
            peak_out[...] = jnp.maximum(peak_out[...], peak)

    @staticmethod
    def scratch(plan, columns):
        rows = plan.nx * plan.nz * plan.rows
        held = pltpu.VMEM((2, rows, columns), F32)
        if plan.nc == 1:
            return [held]
        return [
            held,
            held,
            held,
            pltpu.SemaphoreType.DMA((2,)),
            pltpu.SemaphoreType.DMA((2,)),
            pltpu.SemaphoreType.REGULAR,
        ]

    @staticmethod
    def made_of(plan, steps, refs):
        return SiblingSum(plan, steps, *(tuple(refs) + (None,) * (6 - len(refs))))

    @staticmethod
    def params(plan, collective_id):
        if plan.nc == 1:
            return params()
        return params(collective_id=collective_id, has_side_effects=True)


def dot(left, right):
    return lax.dot_general(left, right, (((1,), (0,)), ((), ())), preferred_element_type=F32)


def dot_last(left, right):
    return lax.dot_general(left, right, (((1,), (1,)), ((), ())), preferred_element_type=F32)


def normalize(values):
    centered = values - jnp.mean(values, axis=-1, keepdims=True)
    inverse = lax.rsqrt(jnp.mean(centered * centered, axis=-1, keepdims=True) + norm_epsilon)
    return centered * inverse, inverse


def normalize_back(grad_output, normal, inverse, gain):
    grad_normal = grad_output * gain
    mean_grad = jnp.mean(grad_normal, axis=-1, keepdims=True)
    mean_cross = jnp.mean(grad_normal * normal, axis=-1, keepdims=True)
    return inverse * (grad_normal - mean_grad - normal * mean_cross)


def rotary_tables(length):
    half_width = HEAD // 2
    steps_half = jnp.arange(half_width, dtype=jnp.int32).astype(F32)
    frequency = rope_base ** (-2.0 * steps_half / HEAD)
    positions = jnp.arange(length, dtype=jnp.int32).astype(F32)
    angles = positions[:, None] * frequency[None, :]
    cosine, sine = jnp.cos(angles), jnp.sin(angles)
    heads = LANES // HEAD
    return (
        jnp.concatenate([cosine, cosine] * heads, axis=1),
        jnp.concatenate([-sine, sine] * heads, axis=1),
    )


def swap_halves(values):
    lane = lax.broadcasted_iota(jnp.int32, values.shape, 1)
    ahead = pltpu.roll(values, LANES - HEAD // 2, 1)
    behind = pltpu.roll(values, HEAD // 2, 1)
    return jnp.where(lax.rem(lane, HEAD) < HEAD // 2, ahead, behind)


def of_head(values, head):
    lane = lax.broadcasted_iota(jnp.int32, values.shape, 1)
    return jnp.where(lane // HEAD == head, values, jnp.zeros_like(values))


def params(**more):
    return pltpu.CompilerParams(vmem_limit_bytes=VMEM_LIMIT, **more)


def whole(shape):
    zeros = (0,) * len(shape)
    return pl.BlockSpec(shape, lambda i, place: zeros, pipeline_mode=pl.Buffered(1))


def result(shape):
    zeros = (0,) * len(shape)
    return pl.BlockSpec(shape, lambda i, place: zeros)


def own_index(tensor):
    return lax.axis_index("dp") * tensor + lax.axis_index("tensor")


def device_at(index, tensor):
    return (index // tensor, lax.rem(index, tensor))


def greet_all(me, count, tensor):
    barrier = pltpu.get_barrier_semaphore()

    def greet(far, carry):
        pl.semaphore_signal(
            barrier,
            inc=1,
            device_id=device_at(lax.rem(me + far, count), tensor),
            device_id_type=pl.DeviceIdType.MESH,
        )
        return carry

    lax.fori_loop(1, count, greet, 0)
    pl.semaphore_wait(barrier, count - 1)


def for_all(me, count, tensor, source, target, send_sem, recv_sem, start):
    def act(far, carry):
        peer = lax.rem(me + far, count)
        copy = pltpu.make_async_remote_copy(
            src_ref=source(peer),
            dst_ref=target,
            send_sem=send_sem.at[far - 1],
            recv_sem=recv_sem.at[far - 1],
            device_id=device_at(peer, tensor),
            device_id_type=pl.DeviceIdType.MESH,
        )
        if start:
            copy.start()
        else:
            copy.wait()
        return carry

    lax.fori_loop(1, count, act, 0)


def swap_blocks_kernel(tensor, block_ref, out_ref, held, send_sem, recv_sem):
    count = held.shape[0]
    me = own_index(tensor)
    greet_all(me, count, tensor)
    for start in (True, False):
        for_all(
            me,
            count,
            tensor,
            lambda peer: block_ref.at[peer],
            held.at[me],
            send_sem,
            recv_sem,
            start,
        )
        if start:
            held[pl.ds(me, 1)] = block_ref[pl.ds(me, 1)]
    out_ref[...] = held[...]


def in_vmem():
    return pl.BlockSpec(memory_space=pltpu.VMEM)


def in_place():
    return pl.BlockSpec(memory_space=pl.ANY)


def swap_blocks(plan, blocks):
    return pl.pallas_call(
        functools.partial(swap_blocks_kernel, plan.tensor),
        name="swap_blocks",
        out_shape=jax.ShapeDtypeStruct(blocks.shape, blocks.dtype),
        in_specs=[in_vmem()],
        out_specs=in_vmem(),
        scratch_shapes=[
            pltpu.VMEM(blocks.shape, blocks.dtype),
            pltpu.SemaphoreType.DMA((plan.count - 1,)),
            pltpu.SemaphoreType.DMA((plan.count - 1,)),
        ],
        compiler_params=params(collective_id=0, has_side_effects=True),
    )(blocks)


def total_kernel(
    tensor, block_ref, out_ref, came, held, own, send_sem, recv_sem, late_send, late_recv
):
    count = held.shape[0]
    me = own_index(tensor)
    greet_all(me, count, tensor)
    for start in (True, False):
        for_all(
            me,
            count,
            tensor,
            lambda peer: block_ref.at[peer],
            came.at[me],
            send_sem,
            recv_sem,
            start,
        )
        if start:
            came[pl.ds(me, 1)] = block_ref[pl.ds(me, 1)]
    summed = jnp.sum(came[...], axis=0)
    own[...] = summed
    for start in (True, False):
        for_all(me, count, tensor, lambda peer: own, held.at[me], late_send, late_recv, start)
        if start:
            held[pl.ds(me, 1)] = summed[None]
    out_ref[...] = held[...]


def total(plan, values, scalar):
    count = plan.count
    part = -(-values.shape[0] // count)
    padded = jnp.pad(values, (0, part * count - values.shape[0])).reshape(count, part)
    tail = jnp.full((count, 8 * LANES - part), scalar, values.dtype)
    blocks = jnp.concatenate([padded, tail], axis=1).reshape(count, 8, LANES)
    sums = pl.pallas_call(
        functools.partial(total_kernel, plan.tensor),
        name="total",
        out_shape=jax.ShapeDtypeStruct(blocks.shape, blocks.dtype),
        in_specs=[in_vmem()],
        out_specs=in_vmem(),
        scratch_shapes=[
            pltpu.VMEM(blocks.shape, blocks.dtype),
            pltpu.VMEM(blocks.shape, blocks.dtype),
            pltpu.VMEM(blocks.shape[1:], blocks.dtype),
        ]
        + [pltpu.SemaphoreType.DMA((count - 1,))] * 4,
        compiler_params=params(collective_id=1, has_side_effects=True),
    )(blocks).reshape(count, 8 * LANES)
    return sums[:, :part].reshape(-1)[: values.shape[0]], sums[0, part]


class Transport:
    def __init__(self, plan, shard, out, at, order, send_sem, recv_sem):
        self.plan, self.shard, self.out, self.at, self.order = plan, shard, out, at, order
        self.send_sem, self.recv_sem = send_sem, recv_sem
        self.dp_index, self.y = lax.axis_index("dp"), lax.axis_index("tensor")
        self.c = lax.rem(self.dp_index, plan.nc)
        self.x = lax.rem(self.dp_index // plan.nc, plan.nx)
        self.z = self.dp_index // (plan.nc * plan.nx)

    def device(self, z, x, c, y):
        return ((z * self.plan.nx + x) * self.plan.nc + c, y)

    def copies(self, stage):
        plan = self.plan
        z, x, c, y = self.z, self.x, self.c, self.y
        if stage == 0:
            target = self.out.at[(y, z, x, c) + self.at]
            return [
                pltpu.make_async_remote_copy(
                    src_ref=self.shard.at[self.at],
                    dst_ref=target,
                    send_sem=self.send_sem.at[far - 1],
                    recv_sem=self.recv_sem.at[far - 1],
                    device_id=self.device(lax.rem(z + far, plan.nz), x, c, y),
                    device_id_type=pl.DeviceIdType.MESH,
                )
                for far in range(1, plan.nz)
            ]
        path = self.order + ("c",)
        done = path[: stage - 1]
        axis = path[stage - 1]
        every = slice(None)
        block = self.out.at[
            (
                every if "y" in done else y,
                every,
                every if "x" in done else x,
                every if "c" in done else c,
            )
            + self.at
        ]
        device = {
            "x": self.device(z, 1 - x, c, y),
            "y": self.device(z, x, c, 1 - y),
            "c": self.device(z, x, 1 - c, y),
        }[axis]
        slot = plan.nz - 2 + stage
        return [
            pltpu.make_async_remote_copy(
                src_ref=block,
                dst_ref=block,
                send_sem=self.send_sem.at[slot],
                recv_sem=self.recv_sem.at[slot],
                device_id=device,
                device_id_type=pl.DeviceIdType.MESH,
            )
        ]

    def own(self):
        slot = self.plan.nz + 2
        return pltpu.make_async_copy(
            self.shard.at[self.at],
            self.out.at[(self.y, self.z, self.x, self.c) + self.at],
            self.send_sem.at[slot],
        )

    def advance(self, stage):
        if stage == 0:
            self.own().start()
        elif stage == 1:
            self.own().wait()
        if stage > 0:
            for copy in self.copies(stage - 1):
                copy.wait_recv()
        if stage < 4:
            for copy in self.copies(stage):
                copy.start()
        else:
            for earlier in range(4):
                for copy in self.copies(earlier):
                    copy.wait_send()


def greet_neighbours(plan):
    dp_index, y = lax.axis_index("dp"), lax.axis_index("tensor")
    c = lax.rem(dp_index, plan.nc)
    x = lax.rem(dp_index // plan.nc, plan.nx)
    z = dp_index // (plan.nc * plan.nx)
    places = [(lax.rem(z + far, plan.nz), x, c, y) for far in range(1, plan.nz)]
    places += [(z, 1 - x, c, y), (z, x, c, 1 - y), (z, x, 1 - c, y)]
    barrier = pltpu.get_barrier_semaphore()
    for to_z, to_x, to_c, to_y in places:
        pl.semaphore_signal(
            barrier,
            inc=1,
            device_id=((to_z * plan.nx + to_x) * plan.nc + to_c, to_y),
            device_id_type=pl.DeviceIdType.MESH,
        )
    pl.semaphore_wait(barrier, len(places))


def transport_slots(plan):
    return plan.nz + 3


def fetch_kernel(plan, orders, rows_ref, *refs):
    number = len(orders)
    shards, came = refs[:number], refs[number]
    outs = refs[number + 1 : 2 * number + 1]
    send_sem, recv_sem, own_sem, weight_send, weight_recv = refs[2 * number + 1 :]
    count, tensor = plan.count, plan.tensor
    me = own_index(tensor)
    greet_all(me, count, tensor)
    units = [
        Transport(
            plan,
            shards[n],
            outs[n],
            (slice(None),),
            orders[n],
            weight_send.at[n],
            weight_recv.at[n],
        )
        for n in range(number)
    ]
    for unit in units:
        unit.advance(0)
    own = pltpu.make_async_copy(rows_ref.at[me], came.at[me], own_sem)
    own.start()

    def rows(start):
        for_all(
            me,
            count,
            tensor,
            lambda peer: rows_ref.at[peer],
            came.at[me],
            send_sem,
            recv_sem,
            start,
        )

    rows(True)
    for stage in range(1, 5):
        for unit in units:
            unit.advance(stage)
    own.wait()
    rows(False)


def fetch(plan, rows, shards, orders):
    number = len(shards)
    slots = transport_slots(plan)
    outs = pl.pallas_call(
        functools.partial(fetch_kernel, plan, orders),
        name="fetch",
        out_shape=[jax.ShapeDtypeStruct(rows.shape, rows.dtype)]
        + [plan.gathered_shape(shard) for shard in shards],
        in_specs=[in_place()] * (1 + number),
        out_specs=[in_place()] * (1 + number),
        scratch_shapes=[
            pltpu.SemaphoreType.DMA((plan.count - 1,)),
            pltpu.SemaphoreType.DMA((plan.count - 1,)),
            pltpu.SemaphoreType.DMA(()),
            pltpu.SemaphoreType.DMA((number, slots)),
            pltpu.SemaphoreType.DMA((number, slots)),
        ],
        compiler_params=params(collective_id=4, has_side_effects=True),
    )(rows, *shards)
    return outs[0], [w.reshape(plan.tensor, -1, w.shape[-1]) for w in outs[1:]]


def wire_scale(plan, peak):
    bound = peak[0, 0] * (plan.count // plan.nc)
    exponent = jnp.floor(jnp.log2(32768.0 / jnp.maximum(bound, 1e-30)))
    return jnp.exp2(jnp.clip(exponent, -60.0, 60.0))


class PeakExchange:
    def __init__(self, plan, own, held, send_sem, recv_sem):
        self.own, self.held, self.send_sem, self.recv_sem = own, held, send_sem, recv_sem
        dp_index, y = lax.axis_index("dp"), lax.axis_index("tensor")
        c = lax.rem(dp_index, plan.nc)
        x = lax.rem(dp_index // plan.nc, plan.nx)
        z = dp_index // (plan.nc * plan.nx)

        def device(z, x, y):
            return ((z * plan.nx + x) * plan.nc + c, y)

        self.peers = (
            [device(z, 1 - x, y), device(z, x, 1 - y), device(z, 1 - x, 1 - y)],
            [device(lax.rem(z + far, plan.nz), x, y) for far in range(1, plan.nz)],
        )

    def greet(self, more=()):
        barrier = pltpu.get_barrier_semaphore()
        peers = self.peers[0] + self.peers[1] + list(more)
        for peer in peers:
            pl.semaphore_signal(
                barrier, inc=1, device_id=peer, device_id_type=pl.DeviceIdType.MESH
            )
        pl.semaphore_wait(barrier, len(peers))

    def copies(self, stage):
        first = len(self.peers[0]) * stage
        return [
            pltpu.make_async_remote_copy(
                src_ref=self.own.at[stage],
                dst_ref=self.held.at[first + n],
                send_sem=self.send_sem.at[first + n],
                recv_sem=self.recv_sem.at[first + n],
                device_id=peer,
                device_id_type=pl.DeviceIdType.MESH,
            )
            for n, peer in enumerate(self.peers[stage])
        ]

    def start(self, stage, value):
        self.own[stage] = value
        for copy in self.copies(stage):
            copy.start()

    def finish(self, stage):
        for copy in self.copies(stage):
            copy.wait()
        value = self.own[stage]
        first = len(self.peers[0]) * stage
        for n in range(len(self.peers[stage])):
            value = jnp.maximum(value, self.held[first + n])
        return value

    @staticmethod
    def scratch(plan):
        number = 3 + plan.nz - 1
        return [
            pltpu.VMEM((2, 8, LANES), F32),
            pltpu.VMEM((number, 8, LANES), F32),
            pltpu.SemaphoreType.DMA((number,)),
            pltpu.SemaphoreType.DMA((number,)),
        ]


def token_places(slot_ids, length, vocab_shard):
    count = slot_ids.shape[0]
    order = jnp.arange(count, dtype=jnp.int32)
    key = jnp.where(order < length, slot_ids, -1)
    owner = key // vocab_shard
    row = key - owner * vocab_shard
    same = key[:, None] == key[None, :]
    first_at = jnp.min(jnp.where(same, order[None, :], count), axis=1)
    first = (first_at == order) & (key >= 0)
    earlier = first[None, :] & (owner[:, None] == owner[None, :])
    place = jnp.sum(
        (earlier & (order[None, :] < first_at[:, None])).astype(jnp.int32), axis=1
    )
    return owner, row, first, jnp.where(key >= 0, place, -1)


def round_slots(owner, place, room, turn):
    within = place - turn * room
    served = (within >= 0) & (within < room)
    return jnp.where(served, owner * room + within, -1)


def round_wants(slot, first, row, slots):
    wanted = first[None, :] & (slot[None, :] == jnp.arange(slots, dtype=jnp.int32)[:, None])
    return jnp.max(jnp.where(wanted, row[None, :], -1), axis=1)


def picked_rows(wants, table_low):
    chosen = wants.reshape(-1)[:, None] == jnp.arange(table_low.shape[0], dtype=jnp.int32)[None, :]
    return jnp.dot(chosen.astype(BF16), table_low, preferred_element_type=F32).astype(BF16)


def spread_rows(slot, rows):
    chosen = slot[:, None] == jnp.arange(rows.shape[0], dtype=jnp.int32)[None, :]
    return jnp.dot(chosen.astype(BF16), rows, preferred_element_type=F32)


def summed_rows(index, rows, count):
    chosen = jnp.arange(count, dtype=jnp.int32)[:, None] == index[None, :]
    return jnp.dot(chosen.astype(BF16), rows, preferred_element_type=F32)


def swap_rows(plan, rows):
    parts = rows.reshape(plan.count, rows.shape[0] // plan.count, rows.shape[1])
    return lax.all_to_all(parts, AXES, 0, 0, tiled=True).reshape(rows.shape)


def transport_units(plan, shards, outs, send_sem, recv_sem):
    units = []
    for n in range(len(shards)):
        half = shards[n].shape[1] // 2
        for side, order in enumerate((("x", "y"), ("y", "x"))):
            number = len(units)
            units.append(
                Transport(
                    plan,
                    shards[n],
                    outs[n],
                    (slice(None), pl.ds(side * half, half)),
                    order,
                    send_sem.at[number],
                    recv_sem.at[number],
                )
            )
    return units


SLOTS_PER_STEP = 4
TRANSPORT_SLOTS = {
    0: ((0, 0),),
    7: ((0, 1), (1, 0)),
    11: ((0, 2),),
    14: ((1, 1), (2, 0)),
    18: ((0, 3), (1, 2)),
    22: ((2, 1),),
}
TRANSPORT_END = ((1, 3), (2, 2), (2, 3), (0, 4), (1, 4), (2, 4))


def advance(units, events):
    for matrix, stage in events:
        for side in range(2):
            units[2 * matrix + side].advance(stage)


def attend_kernel(plan, number, place, *refs):
    (embedded, wq, wk, wv, wo, cosine, sine, norms) = refs[:8]
    shards = refs[8 : 8 + number]
    (q, k, v, mixed_out, log_total, low_one, normal_one, inverse_one) = refs[8 + number : 16 + number]
    (low_two, normal_two, inverse_two) = refs[16 + number : 19 + number]
    gathered = refs[19 + number : 19 + 2 * number]
    scratch = refs[19 + 2 * number :]
    weights, mixed = scratch[:2]
    rows = embedded.shape[0]
    step = pl.program_id(0)
    if number:
        units = transport_units(plan, shards, gathered, *scratch[2:4])

        @pl.when(step == 0)
        def _():
            greet_neighbours(plan)

    def transport(part):
        if number:
            for slot, events in TRANSPORT_SLOTS.items():
                if slot % SLOTS_PER_STEP == part:

                    @pl.when(step == slot // SLOTS_PER_STEP)
                    def _():
                        advance(units, events)

    @pl.when(step == 0)
    def _():
        for start in range(0, rows, ROW_BLOCK):
            at = slice(start, start + ROW_BLOCK)
            normal, inverse = normalize(embedded[at, :])
            normal_one[at, :] = normal
            inverse_one[at, :] = inverse
            low_one[at, :] = (normal * norms[0:1, :] + norms[1:2, :]).astype(BF16)

    transport(0)
    weights[:, :LANES] = wq[...]
    weights[:, LANES : 2 * LANES] = wk[...]
    weights[:, 2 * LANES :] = wv[...]
    for start in range(0, rows, ROW_BLOCK):
        at = slice(start, start + ROW_BLOCK)
        made = dot(low_one[at, :], weights[...])
        query, key = made[:, :LANES], made[:, LANES : 2 * LANES]
        query = query * cosine[at, :] + swap_halves(query) * sine[at, :]
        key = key * cosine[at, :] + swap_halves(key) * sine[at, :]
        q[at, :] = (query * HEAD**-0.5).astype(BF16)
        k[at, :] = key.astype(BF16)
        v[at, :] = made[:, 2 * LANES :].astype(BF16)
    position = lax.broadcasted_iota(jnp.int32, (rows, 1), 0)
    bias = jnp.where(position < place[4], 0.0, masked_score)
    keys = k[...]
    values = v[...].T
    for start in range(0, rows, ROW_BLOCK):
        at = slice(start, start + ROW_BLOCK)
        if start > 0:
            transport(start // ROW_BLOCK)
        outs = []
        for head in range(LANES // HEAD):
            scores = dot_last(keys, of_head(q[at, :], head)) + bias
            top = jnp.max(scores, axis=0, keepdims=True)
            exponent = jnp.exp(scores - top)
            summed = jnp.sum(exponent, axis=0, keepdims=True)
            out = dot(values[head * HEAD : (head + 1) * HEAD, :], exponent.astype(BF16))
            outs.append(out / summed)
            log_total[head : head + 1, at] = top + jnp.log(summed)
        made = jnp.concatenate(outs, axis=0).T.astype(BF16)
        mixed_out[at, :] = made
        mixed[step, at, :] = made

    @pl.when(step == pl.num_programs(0) - 1)
    def _():
        per_part = wo.shape[2] // LANES
        for start in range(0, rows, ROW_BLOCK):
            at = slice(start, start + ROW_BLOCK)
            product = normal_one[at, :] * norms[0:1, :] + norms[1:2, :]
            for part in range(plan.tensor):
                whole_mixed = jnp.concatenate(
                    [mixed[part * per_part + n, at, :] for n in range(per_part)], axis=1
                )
                product = product + dot_last(whole_mixed, wo[part])
            normal, inverse = normalize(product)
            normal_two[at, :] = normal
            inverse_two[at, :] = inverse
            low_two[at, :] = (normal * norms[2:3, :] + norms[3:4, :]).astype(BF16)
        if number:
            advance(units, TRANSPORT_END)


def attend(plan, place, embedded, wq, wk, wv, wo, cosine, sine, norms, shards):
    rows, width = embedded.shape
    pairs = wq.shape[-1] // LANES
    steps = plan.tensor * pairs
    number = len(shards)

    def locate(i):
        return i // pairs, lax.rem(i, pairs)

    by_pair = pl.BlockSpec((None, rows, LANES), lambda i, place: (i, 0, 0))
    shape = jax.ShapeDtypeStruct((steps, rows, LANES), BF16)
    normed = [
        jax.ShapeDtypeStruct((rows, width), BF16),
        jax.ShapeDtypeStruct((rows, width), F32),
        jax.ShapeDtypeStruct((rows, 1), F32),
    ]
    normed_specs = [result((rows, width)), result((rows, width)), result((rows, 1))]
    scratch = [pltpu.VMEM((width, 3 * LANES), BF16), pltpu.VMEM((steps, rows, LANES), BF16)]
    more = {}
    if number:
        slots = transport_slots(plan)
        scratch += [pltpu.SemaphoreType.DMA((2 * number, slots))] * 2
        more = dict(collective_id=5, has_side_effects=True)
    outs = pl.pallas_call(
        functools.partial(attend_kernel, plan, number),
        name="attend",
        out_shape=[
            shape,
            shape,
            shape,
            jax.ShapeDtypeStruct((rows, steps * LANES), BF16),
            jax.ShapeDtypeStruct((steps, 8, rows), F32),
        ]
        + normed
        + normed
        + [plan.gathered_shape(shard) for shard in shards],
        grid_spec=pltpu.PrefetchScalarGridSpec(
            num_scalar_prefetch=1,
            grid=(steps,),
            in_specs=[whole((rows, width))]
            + [plan.weight_spec(width, LANES, locate)] * 3
            + [
                whole(wo.shape),
                whole((rows, LANES)),
                whole((rows, LANES)),
                whole(norms.shape),
            ]
            + [in_place()] * number,
            out_specs=[
                by_pair,
                by_pair,
                by_pair,
                pl.BlockSpec((rows, LANES), lambda i, place: (0, i)),
                pl.BlockSpec((None, 8, rows), lambda i, place: (i, 0, 0)),
            ]
            + normed_specs
            + normed_specs
            + [in_place()] * number,
            scratch_shapes=scratch,
        ),
        compiler_params=params(**more),
        cost_estimate=pl.CostEstimate(
            flops=8 * rows * width * width + 16 * rows * rows * width,
            bytes_accessed=rows * width * 30,
            transcendentals=0,
        ),
    )(place, embedded, wq, wk, wv, wo, cosine, sine, norms, *shards)
    return outs[:11], [w.reshape(plan.tensor, -1, w.shape[-1]) for w in outs[11:]]


def feed_kernel(
    plan,
    place,
    x,
    wg,
    wu,
    wd,
    normal_two,
    norms,
    gate_out,
    up_out,
    hidden_out,
    normal_out,
    inverse_out,
    pool_out,
):
    rows, width = x.shape
    first = pl.program_id(0) == 0

    @pl.when(first)
    def _():
        normal_out[...] = jnp.zeros_like(normal_out)

    for start in range(0, rows, ROW_BLOCK):
        at = slice(start, start + ROW_BLOCK)
        gate, up = dot(x[at, :], wg[...]), dot(x[at, :], wu[...])
        hidden = (gate * jax.nn.sigmoid(gate) * up).astype(BF16)
        gate_out[at, :] = gate.astype(BF16)
        up_out[at, :] = up.astype(BF16)
        hidden_out[at, :] = hidden
        normal_out[at, :] = normal_out[at, :] + dot_last(hidden, wd[...])

    @pl.when(pl.program_id(0) == pl.num_programs(0) - 1)
    def _():
        pooled = jnp.zeros((1, width), F32)
        for start in range(0, rows, ROW_BLOCK):
            at = slice(start, start + ROW_BLOCK)
            second_out = normal_two[at, :] * norms[2:3, :] + norms[3:4, :]
            normal, inverse = normalize(second_out + normal_out[at, :])
            normal_out[at, :] = normal
            inverse_out[at, :] = inverse
            position = start + lax.broadcasted_iota(jnp.int32, (ROW_BLOCK, 1), 0)
            kept = jnp.where(position < place[4], normal, 0.0)
            pooled = pooled + jnp.sum(kept, axis=0, keepdims=True)
        pool_out[...] = pooled


def feed(plan, place, x, wg, wu, wd, normal_two, norms):
    rows, width = x.shape
    hidden = wg.shape[-1]
    chunks = hidden // HIDDEN_BLOCK
    steps = plan.tensor * chunks

    def locate(i):
        return i // chunks, lax.rem(i, chunks)

    by_chunk = pl.BlockSpec((rows, HIDDEN_BLOCK), lambda i, place: (0, i))
    shape = jax.ShapeDtypeStruct((rows, plan.tensor * hidden), BF16)
    return pl.pallas_call(
        functools.partial(feed_kernel, plan),
        name="feed",
        out_shape=[
            shape,
            shape,
            shape,
            jax.ShapeDtypeStruct((rows, width), F32),
            jax.ShapeDtypeStruct((rows, 1), F32),
            jax.ShapeDtypeStruct((1, width), F32),
        ],
        grid_spec=pltpu.PrefetchScalarGridSpec(
            num_scalar_prefetch=1,
            grid=(steps,),
            in_specs=[
                whole((rows, width)),
                plan.weight_spec(width, HIDDEN_BLOCK, locate),
                plan.weight_spec(width, HIDDEN_BLOCK, locate),
                plan.weight_spec(width, HIDDEN_BLOCK, locate),
                whole((rows, width)),
                whole(norms.shape),
            ],
            out_specs=[
                by_chunk,
                by_chunk,
                by_chunk,
                result((rows, width)),
                result((rows, 1)),
                result((1, width)),
            ],
        ),
        compiler_params=params(),
        cost_estimate=pl.CostEstimate(
            flops=6 * rows * width * plan.tensor * hidden,
            bytes_accessed=rows * width * 40,
            transcendentals=0,
        ),
    )(place, x, wg, wu, wd, normal_two, norms)


def contrast_kernel(
    tensor, place, pool_ref, norms, scale_ref, loss_ref, grad_ref, held, own, send_sem, recv_sem
):
    count = held.shape[0]
    me = own_index(tensor)
    greet_all(me, count, tensor)
    length = jnp.full((1, 1), place[4], jnp.int32).astype(F32)
    pooled = pool_ref[...] / length * norms[4:5, :] + norms[5:6, :]
    inverse = lax.rsqrt(jnp.sum(pooled * pooled, axis=-1, keepdims=True) + norm_epsilon)
    vector = pooled * inverse
    own[...] = vector
    for start in (True, False):
        for_all(me, count, tensor, lambda peer: own, held.at[me], send_sem, recv_sem, start)
        if start:
            held[pl.ds(me, 1)] = vector[None]
    vectors = held[...].reshape(count, held.shape[2])
    scale = jnp.exp(scale_ref[...])
    logits = scale * lax.dot_general(
        vectors,
        vectors,
        (((1,), (1,)), ((), ())),
        precision=lax.Precision.HIGHEST,
        preferred_element_type=F32,
    )
    row = lax.broadcasted_iota(jnp.int32, (count, count), 0)
    column = lax.broadcasted_iota(jnp.int32, (count, count), 1)
    crossed = (lax.rem(row, 2) == 0) & (lax.rem(column, 2) == 1)
    shown = jnp.where(crossed, logits, masked_score)
    row_max = jnp.max(shown, axis=1, keepdims=True)
    row_exp = jnp.where(crossed, jnp.exp(shown - row_max), 0.0)
    row_sum = jnp.sum(row_exp, axis=1, keepdims=True)
    column_max = jnp.max(shown, axis=0, keepdims=True)
    column_exp = jnp.where(crossed, jnp.exp(shown - column_max), 0.0)
    column_sum = jnp.sum(column_exp, axis=0, keepdims=True)
    even = lax.rem(lax.broadcasted_iota(jnp.int32, (count, 1), 0), 2) == 0
    odd = lax.rem(lax.broadcasted_iota(jnp.int32, (1, count), 1), 2) == 1
    row_safe = jnp.where(even, row_sum, 1.0)
    column_safe = jnp.where(odd, column_sum, 1.0)
    row_lse = jnp.where(even, row_max + jnp.log(row_safe), 0.0)
    column_lse = jnp.where(odd, column_max + jnp.log(column_safe), 0.0)
    own = crossed & (column == row + 1)
    diagonal = jnp.sum(jnp.where(own, logits, 0.0))
    half = 1.0 / count
    loss = half * (jnp.sum(row_lse) + jnp.sum(column_lse) - 2.0 * diagonal)
    grad_logits = half * (
        row_exp / row_safe + column_exp / column_safe - 2.0 * own.astype(F32)
    )
    grad_scale = jnp.sum(grad_logits * jnp.where(crossed, logits, 0.0))
    both = grad_logits + grad_logits.T
    grad_vectors = scale * lax.dot_general(
        both,
        vectors,
        (((1,), (0,)), ((), ())),
        precision=lax.Precision.HIGHEST,
        preferred_element_type=F32,
    )
    mine = lax.broadcasted_iota(jnp.int32, (count, 1), 0) == me
    grad_own = jnp.sum(jnp.where(mine, grad_vectors, 0.0), axis=0, keepdims=True)
    along = jnp.sum(grad_own * vector, axis=-1, keepdims=True)
    grad_ref[...] = inverse * (grad_own - vector * along) / length
    lane = lax.broadcasted_iota(jnp.int32, loss_ref.shape, 1)
    loss_ref[...] = jnp.where(lane == 0, loss, grad_scale)


def contrast(plan, place, pool, norms, log_scale):
    width = pool.shape[1]
    loss, grad = pl.pallas_call(
        functools.partial(contrast_kernel, plan.tensor),
        name="contrast",
        out_shape=[
            jax.ShapeDtypeStruct((1, LANES), F32),
            jax.ShapeDtypeStruct((1, width), F32),
        ],
        in_specs=[pl.BlockSpec(memory_space=pltpu.SMEM)] + [in_vmem()] * 3,
        out_specs=[in_vmem()] * 2,
        scratch_shapes=[
            pltpu.VMEM((plan.count, 1, width), F32),
            pltpu.VMEM((1, width), F32),
            pltpu.SemaphoreType.DMA((plan.count - 1,)),
            pltpu.SemaphoreType.DMA((plan.count - 1,)),
        ],
        compiler_params=params(collective_id=2, has_side_effects=True),
    )(place, pool, norms, log_scale.reshape(1, 1))
    return loss[0, 0], loss[0, 1], grad


def feed_back_kernel(plan, steps, place, *refs):
    (
        grad_pool,
        x,
        gate_ref,
        up_ref,
        hidden_ref,
        wg,
        wu,
        wd,
        normal_three,
        inverse_three,
        normal_two,
        inverse_two,
        norms,
        part_one,
        part_two,
        grad_out,
        low_out,
        norm_out,
        peak_out,
        low,
        low_turned,
        x_turned,
        made,
        product,
    ) = refs[:24]
    rows, width = x.shape
    step = pl.program_id(0)
    half = BACK_BLOCK // 2
    if plan.stepped:
        sums = SiblingSum.made_of(plan, steps, refs[24:-4])
        exchange = PeakExchange(plan, *refs[-4:])
    else:
        sums = SiblingSum.made_of(plan, steps, refs[24:])

    @pl.when(step == 0)
    def _():
        if plan.stepped:
            exchange.greet([sums.sibling])
        for start in range(0, rows, ROW_BLOCK):
            at = slice(start, start + ROW_BLOCK)
            position = start + lax.broadcasted_iota(jnp.int32, (ROW_BLOCK, 1), 0)
            grad_third = jnp.where(position < place[4], grad_pool[...], 0.0)
            grad = normalize_back(
                grad_third, normal_three[at, :], inverse_three[at, :], norms[4:5, :]
            )
            grad_out[at, :] = grad
            low[at, :] = grad.astype(BF16)
            low_turned[:, at] = grad.astype(BF16).T
            x_turned[:, at] = x[at, :].T

    @pl.when(step < steps)
    def _():
        for start in range(0, rows, ROW_BLOCK):
            at = slice(start, start + ROW_BLOCK)
            grad_hidden = dot(low[at, :], wd[...])
            gate = gate_ref[at, :].astype(F32)
            up = up_ref[at, :].astype(F32)
            share_gate = jax.nn.sigmoid(gate)
            grad_up = grad_hidden * gate * share_gate
            grad_gate = grad_hidden * up * share_gate * (1.0 + gate * (1.0 - share_gate))
            made[at, :BACK_BLOCK] = grad_gate.astype(BF16)
            made[at, BACK_BLOCK:] = grad_up.astype(BF16)
            grad_out[at, :] = (
                grad_out[at, :]
                + dot_last(made[at, :BACK_BLOCK], wg[...])
                + dot_last(made[at, BACK_BLOCK:], wu[...])
            )
        down = dot(low_turned[...], hidden_ref[...])
        product[:, :BACK_BLOCK] = dot(x_turned[...], made[:, :BACK_BLOCK])
        product[:, BACK_BLOCK : BACK_BLOCK + half] = down[:, :half]
        product[:, BACK_BLOCK + half : 2 * BACK_BLOCK + half] = dot(
            x_turned[...], made[:, BACK_BLOCK:]
        )
        product[:, 2 * BACK_BLOCK + half :] = down[:, half:]
        sums.push(step, product)

    @pl.when(step > 0)
    def _():
        sums.pull(step - 1, (part_one, part_two), (BACK_BLOCK + half,) * 2, peak_out)

    @pl.when(step == steps)
    def _():
        gain_grad = jnp.zeros((1, width), F32)
        shift_grad = jnp.zeros((1, width), F32)
        if plan.stepped:
            exchange.start(0, peak_out[...])
        for start in range(0, rows, ROW_BLOCK):
            at = slice(start, start + ROW_BLOCK)
            if plan.stepped and start == rows // 2:
                exchange.start(1, exchange.finish(0))
            grad_second = grad_out[at, :]
            normal = normal_two[at, :]
            grad = normalize_back(grad_second, normal, inverse_two[at, :], norms[2:3, :])
            gain_grad = gain_grad + jnp.sum(grad_second * normal, axis=0, keepdims=True)
            shift_grad = shift_grad + jnp.sum(grad_second, axis=0, keepdims=True)
            grad_out[at, :] = grad
            low_out[at, :] = grad.astype(BF16)
        norm_out[0:1, :] = gain_grad
        norm_out[1:2, :] = shift_grad
        if plan.stepped:
            peak_out[...] = exchange.finish(1)


def feed_back(
    plan,
    place,
    grad_pool,
    x,
    gate,
    up,
    hidden_low,
    wg,
    wu,
    wd,
    normal_three,
    inverse_three,
    normal_two,
    inverse_two,
    norms,
):
    rows, width = x.shape
    hidden = wg.shape[-1]
    chunks = hidden // BACK_BLOCK
    steps = plan.tensor * chunks

    def locate(i):
        now = jnp.minimum(i, steps - 1)
        return now // chunks, lax.rem(now, chunks)

    def locate_late(i):
        now = jnp.maximum(i - 1, 0)
        return now // chunks, lax.rem(now, chunks)

    by_chunk = pl.BlockSpec(
        (rows, BACK_BLOCK), lambda i, place: (0, jnp.minimum(i, steps - 1))
    )
    columns = BACK_BLOCK * 3 // 2
    return pl.pallas_call(
        functools.partial(feed_back_kernel, plan, steps),
        name="feed_back",
        out_shape=[
            plan.grad_shape("yx", columns * chunks),
            plan.grad_shape("xy", columns * chunks),
            jax.ShapeDtypeStruct((rows, width), F32),
            jax.ShapeDtypeStruct((rows, width), BF16),
            jax.ShapeDtypeStruct((8, width), F32),
            jax.ShapeDtypeStruct((8, LANES), F32),
        ],
        grid_spec=pltpu.PrefetchScalarGridSpec(
            num_scalar_prefetch=1,
            grid=(steps + 1,),
            in_specs=[
                whole((1, width)),
                whole((rows, width)),
                by_chunk,
                by_chunk,
                by_chunk,
                plan.weight_spec(width, BACK_BLOCK, locate),
                plan.weight_spec(width, BACK_BLOCK, locate),
                plan.weight_spec(width, BACK_BLOCK, locate),
                whole((rows, width)),
                whole((rows, 1)),
                whole((rows, width)),
                whole((rows, 1)),
                whole(norms.shape),
            ],
            out_specs=[
                plan.grad_spec("yx", columns, locate_late),
                plan.grad_spec("xy", columns, locate_late),
                result((rows, width)),
                result((rows, width)),
                result((8, width)),
                result((8, LANES)),
            ],
            scratch_shapes=[
                pltpu.VMEM((rows, width), BF16),
                pltpu.VMEM((width, rows), BF16),
                pltpu.VMEM((width, rows), BF16),
                pltpu.VMEM((rows, 2 * BACK_BLOCK), BF16),
                pltpu.VMEM((width, 3 * BACK_BLOCK), F32),
            ]
            + SiblingSum.scratch(plan, 3 * BACK_BLOCK)
            + (PeakExchange.scratch(plan) if plan.stepped else []),
        ),
        compiler_params=SiblingSum.params(plan, 6),
        cost_estimate=pl.CostEstimate(
            flops=20 * rows * width * plan.tensor * hidden,
            bytes_accessed=rows * width * 60,
            transcendentals=0,
        ),
    )(
        place,
        grad_pool,
        x,
        gate,
        up,
        hidden_low,
        wg,
        wu,
        wd,
        normal_three,
        inverse_three,
        normal_two,
        inverse_two,
        norms,
    )


def unfold_feed(part_one, part_two, hidden):
    rows = part_one.shape[0]
    half = BACK_BLOCK // 2
    one = part_one.reshape(rows, hidden // BACK_BLOCK, BACK_BLOCK + half)
    two = part_two.reshape(rows, hidden // BACK_BLOCK, BACK_BLOCK + half)
    down = jnp.concatenate([one[:, :, BACK_BLOCK:], two[:, :, BACK_BLOCK:]], axis=2)
    return (
        one[:, :, :BACK_BLOCK].reshape(rows, hidden),
        two[:, :, :BACK_BLOCK].reshape(rows, hidden),
        down.reshape(rows, hidden),
    )


def heads_back_kernel(
    place, ga, q, k, v, mixed, log_total, wo, cosine, sine, made, gm, key_grad, value_grad
):
    rows = ga.shape[0]
    for start in range(0, rows, ROW_BLOCK):
        at = slice(start, start + ROW_BLOCK)
        gm[at, :] = dot(ga[at, :], wo[...]).astype(BF16)
    position = lax.broadcasted_iota(jnp.int32, (rows, 1), 0)
    bias = jnp.where(position < place[4], 0.0, masked_score)
    keys, values = k[...], v[...]
    keys_turned = keys.T
    for start in range(0, rows, ROW_BLOCK):
        at = slice(start, start + ROW_BLOCK)
        inner = (gm[at, :].astype(F32) * mixed[at, :].astype(F32)).T
        outs = []
        for head in range(LANES // HEAD):
            of = slice(head * HEAD, (head + 1) * HEAD)
            query = of_head(q[at, :], head)
            grad = of_head(gm[at, :], head)
            inner_sum = jnp.sum(inner[of, :], axis=0, keepdims=True)
            scores = dot_last(keys, query) + bias
            probs = jnp.exp(scores - log_total[head : head + 1, at])
            grad_probs = dot_last(values, grad)
            grad_scores = (probs * (grad_probs - inner_sum)).astype(BF16)
            value_part = dot(probs.astype(BF16), grad)
            key_part = dot(grad_scores, query)
            if start == 0 and head == 0:
                value_grad[...] = value_part
                key_grad[...] = key_part
            else:
                value_grad[...] = value_grad[...] + value_part
                key_grad[...] = key_grad[...] + key_part
            outs.append(dot(keys_turned[of, :], grad_scores))
        grad_query = jnp.concatenate(outs, axis=0).T * HEAD**-0.5
        grad_query = grad_query * cosine[at, :] - swap_halves(grad_query) * sine[at, :]
        made[at, :LANES] = grad_query.astype(BF16)
    for start in range(0, rows, ROW_BLOCK):
        at = slice(start, start + ROW_BLOCK)
        grad_key = key_grad[at, :]
        grad_key = grad_key * cosine[at, :] - swap_halves(grad_key) * sine[at, :]
        made[at, LANES : 2 * LANES] = grad_key.astype(BF16)
        made[at, 2 * LANES :] = value_grad[at, :].astype(BF16)


def heads_back(plan, place, first, number, ga, q, k, v, mixed, log_total, wo, cosine, sine):
    rows, width = ga.shape
    pairs = wo.shape[-1] // LANES

    def locate(i):
        now = first + i
        return now // pairs, lax.rem(now, pairs)

    by_pair = pl.BlockSpec((None, rows, LANES), lambda i, place: (first + i, 0, 0))
    return pl.pallas_call(
        heads_back_kernel,
        name="heads_back",
        out_shape=jax.ShapeDtypeStruct((number, rows, 3 * LANES), BF16),
        grid_spec=pltpu.PrefetchScalarGridSpec(
            num_scalar_prefetch=1,
            grid=(number,),
            in_specs=[
                whole((rows, width)),
                by_pair,
                by_pair,
                by_pair,
                pl.BlockSpec((rows, LANES), lambda i, place: (0, first + i)),
                pl.BlockSpec((None, 8, rows), lambda i, place: (first + i, 0, 0)),
                plan.weight_spec(width, LANES, locate),
                whole((rows, LANES)),
                whole((rows, LANES)),
            ],
            out_specs=pl.BlockSpec((None, rows, 3 * LANES), lambda i, place: (i, 0, 0)),
            scratch_shapes=[
                pltpu.VMEM((rows, LANES), BF16),
                pltpu.VMEM((rows, LANES), F32),
                pltpu.VMEM((rows, LANES), F32),
            ],
        ),
        compiler_params=params(),
        cost_estimate=pl.CostEstimate(
            flops=number * 80 * rows * rows * LANES,
            bytes_accessed=rows * width * 2,
            transcendentals=0,
        ),
    )(place, ga, q, k, v, mixed, log_total, wo, cosine, sine)


def first_back_kernel(plan, number, *refs):
    groups = refs[:number]
    (wq, wk, wv, grad_res, normal_one, inverse_one, norms, peak) = refs[number : number + 8]
    low_out, norm_out, peak_out = refs[number + 8 : number + 11]
    step = pl.program_id(0)
    if plan.stepped:
        exchange = PeakExchange(plan, *refs[number + 11 :])

        @pl.when(step == 0)
        def _():
            exchange.greet()
            exchange.start(0, peak[...])

        @pl.when(step == 1)
        def _():
            exchange.start(1, exchange.finish(0))

    pairs = wq.shape[-1] // LANES
    total_grad = grad_res[...]
    places = [(group, n) for group in groups for n in range(group.shape[0])]
    for part in range(plan.tensor):
        for kind, weight in enumerate((wq, wk, wv)):
            lanes = slice(kind * LANES, (kind + 1) * LANES)
            made = []
            for group, n in places[part * pairs : (part + 1) * pairs]:
                made.append(group[n, :, lanes])
            total_grad = total_grad + dot_last(jnp.concatenate(made, axis=1), weight[part])
    normal = normal_one[...]
    grad = normalize_back(total_grad, normal, inverse_one[...], norms[0:1, :])
    low_out[...] = grad.astype(BF16)
    gain_grad = jnp.sum(total_grad * normal, axis=0, keepdims=True)
    shift_grad = jnp.sum(total_grad, axis=0, keepdims=True)

    @pl.when(pl.program_id(0) == 0)
    def _():
        norm_out[...] = jnp.zeros_like(norm_out)

    norm_out[0:1, :] = norm_out[0:1, :] + gain_grad
    norm_out[1:2, :] = norm_out[1:2, :] + shift_grad
    if plan.stepped:

        @pl.when(step == pl.num_programs(0) - 1)
        def _():
            peak_out[...] = exchange.finish(1)


def first_back(plan, groups, wq, wk, wv, grad_res, normal_one, inverse_one, norms, peak):
    rows, width = grad_res.shape
    by_rows = pl.BlockSpec((ROW_BLOCK, width), lambda i: (i, 0))

    def fixed(shape, **more):
        zeros = (0,) * len(shape)
        return pl.BlockSpec(shape, lambda i: zeros, **more)

    return pl.pallas_call(
        functools.partial(first_back_kernel, plan, len(groups)),
        name="first_back",
        out_shape=[
            jax.ShapeDtypeStruct((rows, width), BF16),
            jax.ShapeDtypeStruct((8, width), F32),
            jax.ShapeDtypeStruct((8, LANES), F32),
        ],
        grid=(rows // ROW_BLOCK,),
        in_specs=[
            pl.BlockSpec((g.shape[0], ROW_BLOCK, g.shape[2]), lambda i: (0, i, 0)) for g in groups
        ]
        + [fixed(wq.shape, pipeline_mode=pl.Buffered(1))] * 3
        + [
            by_rows,
            by_rows,
            pl.BlockSpec((ROW_BLOCK, 1), lambda i: (i, 0)),
            fixed(norms.shape),
            fixed((8, LANES)),
        ],
        out_specs=[by_rows, fixed((8, width)), fixed((8, LANES))],
        scratch_shapes=PeakExchange.scratch(plan) if plan.stepped else [],
        compiler_params=(
            params(collective_id=3, has_side_effects=True) if plan.stepped else params()
        ),
        cost_estimate=pl.CostEstimate(
            flops=8 * rows * width * width, bytes_accessed=rows * width * 20, transcendentals=0
        ),
    )(*groups, wq, wk, wv, grad_res, normal_one, inverse_one, norms, peak)


def attend_weights_kernel(plan, steps, number, *refs):
    groups = refs[:number]
    (x, ga, mixed, part_one, part_two, peak_out, x_turned, ga_turned, product) = refs[
        number : number + 9
    ]
    rows, width = x.shape
    step = pl.program_id(0)
    sums = SiblingSum.made_of(plan, steps, refs[number + 9 :])

    @pl.when(step == 0)
    def _():
        sums.greet()
        for start in range(0, rows, ROW_BLOCK):
            at = slice(start, start + ROW_BLOCK)
            ga_turned[:, at] = ga[at, :].T
            x_turned[:, at] = x[at, :].T

    begin = 0
    for group in groups:
        size = group.shape[0]

        @pl.when((step >= begin) & (step < begin + size))
        def _():
            product[:, : 3 * LANES] = dot(x_turned[...], group[step - begin])

        begin += size

    @pl.when(step < steps)
    def _():
        product[:, 3 * LANES :] = dot(ga_turned[...], mixed[...])
        sums.push(step, product)

    @pl.when(step > 0)
    def _():
        sums.pull(step - 1, (part_one, part_two), (2 * LANES,) * 2, peak_out)


def attend_weights(plan, groups, x, ga, mixed, part):
    rows, width = x.shape
    pairs = part // LANES
    steps = plan.tensor * pairs

    def late(order):
        def locate(i):
            now = jnp.maximum(i - 1, 0)
            return now // pairs, lax.rem(now, pairs)

        spec = plan.grad_spec(order, 2 * LANES, locate)
        return pl.BlockSpec(spec.block_shape, lambda i: spec.index_map(i, None))

    def fixed(shape):
        zeros = (0,) * len(shape)
        return pl.BlockSpec(shape, lambda i: zeros, pipeline_mode=pl.Buffered(1))

    return pl.pallas_call(
        functools.partial(attend_weights_kernel, plan, steps, len(groups)),
        name="attend_weights",
        out_shape=[
            plan.grad_shape("yx", 2 * part),
            plan.grad_shape("xy", 2 * part),
            jax.ShapeDtypeStruct((8, LANES), F32),
        ],
        grid=(steps + 1,),
        in_specs=[fixed(g.shape) for g in groups]
        + [
            fixed((rows, width)),
            fixed((rows, width)),
            pl.BlockSpec((rows, LANES), lambda i: (0, jnp.minimum(i, steps - 1))),
        ],
        out_specs=[
            late("yx"),
            late("xy"),
            pl.BlockSpec((8, LANES), lambda i: (0, 0)),
        ],
        scratch_shapes=[
            pltpu.VMEM((width, rows), BF16),
            pltpu.VMEM((width, rows), BF16),
            pltpu.VMEM((width, 4 * LANES), F32),
        ]
        + SiblingSum.scratch(plan, 4 * LANES),
        compiler_params=SiblingSum.params(plan, 7),
        cost_estimate=pl.CostEstimate(
            flops=12 * rows * width * width, bytes_accessed=rows * width * 20, transcendentals=0
        ),
    )(*groups, x, ga, mixed)


def unfold_attend(part_one, part_two):
    rows, columns = part_one.shape
    one = part_one.reshape(rows, columns // (2 * LANES), 2, LANES)
    two = part_two.reshape(rows, columns // (2 * LANES), 2, LANES)
    return [side[:, :, n].reshape(rows, columns // 2) for side in (one, two) for n in (0, 1)]


def adam_step(weight, first_moment, second_moment, gradient, factor):
    clipped = gradient * factor
    first_next = beta_one * first_moment + (1.0 - beta_one) * clipped
    second_next = beta_two * second_moment + (1.0 - beta_two) * clipped * clipped
    corrected_first = first_next / (1.0 - beta_one**STEP)
    corrected_second = second_next / (1.0 - beta_two**STEP)
    change = -learn_rate * (
        corrected_first / (jnp.sqrt(corrected_second) + adam_epsilon) + weight_decay * weight
    )
    return (first_next, second_next, change)


def per_device(
    plan,
    token_ids,
    lengths,
    token_table,
    table_first,
    table_second,
    qkv_weight,
    qkv_first,
    qkv_second,
    out_weight,
    out_first,
    out_second,
    gate_up_weight,
    gate_up_first,
    gate_up_second,
    down_weight,
    down_first,
    down_second,
    norm_params,
    norm_first,
    norm_second,
    log_inverse_warmth,
    scale_first,
    scale_second,
):
    slot_ids = token_ids[0]
    rows = slot_ids.shape[0]
    vocab_shard, width = token_table.shape
    own_length = lax.dynamic_index_in_dim(
        lengths[0], lax.axis_index("tensor"), 0, keepdims=False
    ).astype(jnp.int32)
    place = jnp.stack([jnp.asarray(p, jnp.int32) for p in plan.places()] + [own_length])
    me = lax.axis_index(AXES)

    qkv_low = qkv_weight.astype(BF16)
    gate_up_low = gate_up_weight.astype(BF16)
    early = [qkv_low[:, 0], qkv_low[:, 1], qkv_low[:, 2], out_weight.astype(BF16)]
    late = [gate_up_low[:, 0], gate_up_low[:, 1], down_weight.astype(BF16)]

    table_low = token_table.astype(BF16)
    room = 8 * -(-(5 * rows) // (4 * plan.count * 8))
    slots = room * plan.count
    owner, row, first, token_place = token_places(slot_ids, own_length, vocab_shard)
    slot = round_slots(owner, token_place, room, 0)
    wants = round_wants(slot, first, row, slots).reshape(plan.count, room)
    rounds = jnp.max(token_place) // room + 1
    note = jnp.concatenate(
        [wants, jnp.broadcast_to(rounds, (plan.count, 8 * LANES - room))], axis=1
    )
    notes = swap_blocks(plan, note.reshape(plan.count, 8, LANES)).reshape(plan.count, 8 * LANES)
    asked = notes[:, :room]
    rounds = jnp.max(notes[:, room])
    picked = picked_rows(asked, table_low)
    if plan.stepped:
        half = width // 2
        folded = jnp.concatenate(
            [
                picked[:, :half].reshape(plan.count, room, half),
                picked[:, half:].reshape(plan.count, room, half),
            ],
            axis=1,
        )
        came, (wq, wk, wv, wo) = fetch(
            plan, folded, early, (("x", "y"), ("y", "x"), ("x", "y"), ("y", "x"))
        )
        came = jnp.concatenate([came[:, :room], came[:, room:]], axis=2).reshape(slots, width)
    else:
        came = swap_rows(plan, picked)
        wq, wk, wv, wo = [plan.gather_whole(shard) for shard in early]
    embedded = spread_rows(slot, came)

    def ask(turn):
        later = round_slots(owner, token_place, room, turn)
        later_wants = round_wants(later, first, row, slots).reshape(plan.count, room)
        return later, lax.all_to_all(later_wants, AXES, 0, 0, tiled=True)

    def fetch_more(turn, sofar):
        later, later_asked = ask(turn)
        return sofar + spread_rows(later, swap_rows(plan, picked_rows(later_asked, table_low)))

    embedded = lax.cond(
        rounds > 1,
        lambda sofar: lax.fori_loop(1, rounds, fetch_more, sofar),
        lambda sofar: sofar,
        embedded,
    )
    cosine, sine = rotary_tables(rows)
    made, gathered = attend(
        plan,
        place,
        embedded,
        wq,
        wk,
        wv,
        wo,
        cosine,
        sine,
        norm_params,
        late if plan.stepped else [],
    )
    q, k, v, mixed, log_total, first_low, normal_one, inverse_one = made[:8]
    second_low, normal_two, inverse_two = made[8:]
    if plan.stepped:
        wg, wu, wd = gathered
    else:
        wg, wu, wd = [plan.gather_whole(shard) for shard in late]
    gate, up, hidden_low, normal_three, inverse_three, pool = feed(
        plan, place, second_low, wg, wu, wd, normal_two, norm_params
    )
    batch_loss, grad_log_scale, grad_pool = contrast(
        plan, place, pool, norm_params, log_inverse_warmth
    )
    part_one, part_two, grad_first_res, attended_low, norm_two, peak_two = feed_back(
        plan,
        place,
        grad_pool,
        second_low,
        gate,
        up,
        hidden_low,
        wg,
        wu,
        wd,
        normal_three,
        inverse_three,
        normal_two,
        inverse_two,
        norm_params,
    )
    scale_two = wire_scale(plan, peak_two)
    steps = q.shape[0]
    cut = steps * 2 // 3

    def heads(first, number, grad):
        return heads_back(
            plan, place, first, number, grad, q, k, v, mixed, log_total, wo, cosine, sine
        )

    if plan.stepped:
        part_one = plan.step_along(part_one, "y", scale_two)
        part_two = plan.step_along(part_two, "x", scale_two)
        group_one = heads(0, cut, attended_low)
        part_one, part_two, ready = lax.optimization_barrier((part_one, part_two, attended_low))
        part_one = plan.step_along(part_one, "x", scale_two)
        part_two = plan.step_along(part_two, "y", scale_two)
        group_two = heads(cut, steps - cut, ready)
        part_one, part_two, ready = lax.optimization_barrier((part_one, part_two, attended_low))
        shard_one = plan.step_along(part_one, "z", scale_two)
        shard_two = plan.step_along(part_two, "z", scale_two)
        groups = [group_one, group_two]
    else:
        shard_one, shard_two = plan.scatter_whole(part_one), plan.scatter_whole(part_two)
        groups = [heads(0, steps, attended_low)]
        ready = attended_low
    part_three, part_four, peak_one = attend_weights(
        plan, groups, first_low, ready, mixed, wq.shape[-1]
    )
    peak_one, shard_one, shard_two = lax.optimization_barrier((peak_one, shard_one, shard_two))
    embedded_low, norm_one, peak_one = first_back(
        plan, groups, wq, wk, wv, grad_first_res, normal_one, inverse_one, norm_params, peak_one
    )
    scale_one = wire_scale(plan, peak_one)
    grad_rows = summed_rows(slot, embedded_low, slots).astype(BF16)
    shard_three = plan.scatter(part_three, "yx", scale_one)
    shard_four = plan.scatter(part_four, "xy", scale_one)
    grad_table = summed_rows(asked.reshape(-1), swap_rows(plan, grad_rows), vocab_shard)

    def return_more(turn, sofar):
        later, later_asked = ask(turn)
        later_rows = summed_rows(later, embedded_low, slots).astype(BF16)
        return sofar + summed_rows(
            later_asked.reshape(-1), swap_rows(plan, later_rows), vocab_shard
        )

    grad_table = lax.fori_loop(1, rounds, return_more, grad_table)
    owned_squares = jnp.sum(grad_table * grad_table)
    for shard in (shard_one, shard_two, shard_three, shard_four):
        owned_squares = owned_squares + jnp.sum(shard * shard)
    grad_gate, grad_up, grad_down_own = unfold_feed(shard_one, shard_two, wg.shape[-1])
    grad_q, grad_k, grad_v, grad_out_own = unfold_attend(shard_three, shard_four)
    grad_qkv_own = jnp.stack([grad_q, grad_k, grad_v], axis=1)
    grad_gate_own = jnp.stack([grad_gate, grad_up], axis=1)
    length_float = own_length.astype(F32)
    norm_grads, square_total = total(
        plan,
        jnp.concatenate(
            [
                norm_one[0:2],
                norm_two[0:2],
                grad_pool * pool,
                grad_pool * length_float,
            ],
            axis=0,
        ).reshape(-1),
        owned_squares,
    )
    norm_grads = norm_grads.reshape(norm_params.shape)
    squares = square_total + jnp.sum(norm_grads * norm_grads) + grad_log_scale * grad_log_scale
    grad_norm = jnp.sqrt(squares)
    factor = jnp.minimum(1.0, clip_limit / (grad_norm + 1e-06))
    return (
        (batch_loss, grad_norm)
        + adam_step(token_table, table_first, table_second, grad_table, factor)
        + adam_step(qkv_weight, qkv_first, qkv_second, grad_qkv_own, factor)
        + adam_step(out_weight, out_first, out_second, grad_out_own, factor)
        + adam_step(gate_up_weight, gate_up_first, gate_up_second, grad_gate_own, factor)
        + adam_step(down_weight, down_first, down_second, grad_down_own, factor)
        + adam_step(norm_params, norm_first, norm_second, norm_grads, factor)
        + adam_step(log_inverse_warmth, scale_first, scale_second, grad_log_scale, factor)
    )


def solution(mesh):
    rows = P(AXES, None)
    deep = P("dp", None, "tensor")
    flat = P("dp", "tensor")
    in_specs = (
        (rows, P("dp", None)) + (rows,) * 3 + (deep,) * 3 + (flat,) * 3 + (deep,) * 3 + (flat,) * 3
    ) + (P(),) * 6
    out_specs = (
        (P(), P()) + (rows,) * 3 + (deep,) * 3 + (flat,) * 3 + (deep,) * 3 + (flat,) * 3
    ) + (P(),) * 6

    def run(*args):
        plan = Plan(mesh, args[2].shape[1])
        return jax.shard_map(
            functools.partial(per_device, plan),
            mesh=mesh,
            in_specs=in_specs,
            out_specs=out_specs,
            check_vma=False,
        )(*args)

    return run
```

```python
import functools

import jax
import jax.numpy as jnp
from jax import lax
from jax.experimental import pallas as pl
from jax.experimental.pallas import tpu as pltpu
from jax.sharding import PartitionSpec as P

HEAD = 64
STEP = 8

norm_epsilon = 1e-12
rope_base = 1000.0
beta_one = 0.9
beta_two = 0.999
adam_epsilon = 1e-08
learn_rate = 0.01
weight_decay = 0.01
clip_limit = 0.001
masked_score = -1e30

AXES = ("dp", "tensor")
F32 = jnp.float32
BF16 = jnp.bfloat16
LANES = 128
VMEM_LIMIT = 58 * 1024 * 1024
ROW_BLOCK = 256
HIDDEN_BLOCK = 512
BACK_BLOCK = 512


class Plan:
    def __init__(self, mesh, width):
        self.dp = mesh.shape["dp"]
        self.tensor = mesh.shape["tensor"]
        self.count = self.dp * self.tensor
        self.shard = width // self.dp
        self.stepped = self.dp % 4 == 0 and self.shard % 16 == 0
        if self.stepped:
            self.nc, self.nx, self.nz = 2, 2, self.dp // 4
        else:
            self.nc, self.nx, self.nz = 1, 1, 1
        self.rows = width // (self.nc * self.nx * self.nz)

    def places(self):
        dp_index, tensor_index = lax.axis_index("dp"), lax.axis_index("tensor")
        if not self.stepped:
            zero = jnp.int32(0)
            return zero, zero, zero, zero
        core = lax.rem(dp_index, self.nc)
        across = lax.rem(dp_index // self.nc, self.nx)
        return dp_index // (self.nc * self.nx), across, core, tensor_index

    def size(self, axis):
        return {"z": self.nz, "x": self.nx, "c": self.nc, "y": self.tensor}[axis]

    def shift(self, values, axis, by):
        pairs = []
        for z in range(self.nz):
            for x in range(self.nx):
                for c in range(self.nc):
                    for y in range(self.tensor):
                        place = {"z": z, "x": x, "c": c, "y": y}
                        source = self.flat(place)
                        place[axis] = (place[axis] + by) % self.size(axis)
                        pairs.append((source, self.flat(place)))
        return lax.ppermute(values, AXES, pairs)

    def flat(self, place):
        dp_index = (place["z"] * self.nx + place["x"]) * self.nc + place["c"]
        return dp_index * self.tensor + place["y"]

    def gather_whole(self, values):
        whole = lax.all_gather(values, ("tensor", "dp"), axis=0, tiled=True)
        return whole.reshape(self.tensor, -1, values.shape[1])

    def gathered_shape(self, shard):
        rows, columns = shard.shape
        return jax.ShapeDtypeStruct(
            (self.tensor, self.nz, self.nx, self.nc, rows, columns), shard.dtype
        )

    def scatter_whole(self, part):
        whole = part.reshape(self.tensor * self.rows, part.shape[-1])
        return lax.psum_scatter(whole, ("tensor", "dp"), scatter_dimension=0, tiled=True)

    def step_along(self, total, axis, scale):
        own_y = lax.axis_index("tensor")
        pick = functools.partial(lax.dynamic_index_in_dim, total, axis=0, keepdims=False)
        kept = pick(own_y) if axis == "y" else total[0]
        for far in range(1, self.size(axis)):
            other = pick(lax.rem(own_y + far, self.tensor)) if axis == "y" else total[far]
            sent = (other * scale).astype(jnp.float16)
            kept = kept + self.shift(sent, axis, far).astype(F32) / scale
        return kept

    def scatter(self, part, order, scale):
        if not self.stepped:
            return self.scatter_whole(part)
        for axis in tuple(order) + ("z",):
            part = self.step_along(part, axis, scale)
        return part


    def weight_spec(self, width, columns, locate):
        def index(i, place):
            part, column = locate(i)
            return (part, 0, column)

        return pl.BlockSpec((None, width, columns), index)

    def grad_spec(self, order, columns, locate):
        def index(i, place):
            part, column = locate(i)
            if order == "yx":
                return (part, 0, 0, 0, column)
            return (0, part, 0, 0, column)

        middle = (None, self.nx) if order == "yx" else (self.nx, None)
        return pl.BlockSpec(middle + (self.nz, self.rows, columns), index)

    def grad_shape(self, order, columns):
        middle = (self.tensor, self.nx) if order == "yx" else (self.nx, self.tensor)
        return jax.ShapeDtypeStruct(middle + (self.nz, self.rows, columns), F32)


class SiblingSum:
    def __init__(self, plan, steps, kept, sent, came, send_sem, recv_sem, free_sem):
        self.plan, self.steps = plan, steps
        self.kept, self.sent, self.came = kept, sent, came
        self.send_sem, self.recv_sem, self.free_sem = send_sem, recv_sem, free_sem
        dp_index, self.y = lax.axis_index("dp"), lax.axis_index("tensor")
        self.c = lax.rem(dp_index, plan.nc)
        self.x = lax.rem(dp_index // plan.nc, plan.nx)
        self.z = dp_index // (plan.nc * plan.nx)
        self.sibling = (dp_index + 1 - 2 * self.c, self.y)

    def greet(self):
        if self.plan.nc > 1:
            barrier = pltpu.get_barrier_semaphore()
            pl.semaphore_signal(
                barrier, inc=1, device_id=self.sibling, device_id_type=pl.DeviceIdType.MESH
            )
            pl.semaphore_wait(barrier, 1)

    def copy(self, slot):
        return pltpu.make_async_remote_copy(
            src_ref=self.sent.at[slot],
            dst_ref=self.came.at[slot],
            send_sem=self.send_sem.at[slot],
            recv_sem=self.recv_sem.at[slot],
            device_id=self.sibling,
            device_id_type=pl.DeviceIdType.MESH,
        )

    def push(self, step, product):
        plan = self.plan
        slot = lax.rem(step, 2)
        if plan.nc > 1:

            @pl.when(step >= 2)
            def _():
                self.copy(slot).wait_send()
                pl.semaphore_wait(self.free_sem, 1)

        for far_x in range(plan.nx):
            x = lax.rem(self.x + far_x, plan.nx)
            for far_z in range(plan.nz):
                z = lax.rem(self.z + far_z, plan.nz)
                base = (z * plan.nx + x) * plan.nc
                to = slice(
                    (far_x * plan.nz + far_z) * plan.rows,
                    (far_x * plan.nz + far_z + 1) * plan.rows,
                )
                start = pl.multiple_of((base + self.c) * plan.rows, 16)
                self.kept[slot, to, :] = product[pl.ds(start, plan.rows), :]
                if plan.nc > 1:
                    start = pl.multiple_of((base + 1 - self.c) * plan.rows, 16)
                    self.sent[slot, to, :] = product[pl.ds(start, plan.rows), :]
        if plan.nc > 1:
            self.copy(slot).start()

    def pull(self, step, targets, widths, peak_out):
        plan = self.plan
        slot = lax.rem(step, 2)
        if plan.nc > 1:
            self.copy(slot).wait_recv()
        peak = jnp.zeros((1, 1), F32)
        for far_x in range(plan.nx):
            for far_z in range(plan.nz):
                at = slice(
                    (far_x * plan.nz + far_z) * plan.rows,
                    (far_x * plan.nz + far_z + 1) * plan.rows,
                )
                value = self.kept[slot, at, :]
                if plan.nc > 1:
                    value = value + self.came[slot, at, :]
                start = 0
                for target, width in zip(targets, widths):
                    target[far_x, far_z] = value[:, start : start + width]
                    start += width
                largest = jnp.max(jnp.abs(value), axis=0, keepdims=True)
                peak = jnp.maximum(peak, jnp.max(largest, axis=1, keepdims=True))
        if plan.nc > 1:

            @pl.when(step < self.steps - 2)
            def _():
                pl.semaphore_signal(
                    self.free_sem,
                    inc=1,
                    device_id=self.sibling,
                    device_id_type=pl.DeviceIdType.MESH,
                )

            @pl.when(step == self.steps - 1)
            def _():
                for last in range(max(self.steps - 2, 0), self.steps):
                    self.copy(last % 2).wait_send()

        peak = jnp.broadcast_to(peak, peak_out.shape)

        @pl.when(step == 0)
        def _():
            peak_out[...] = peak

        @pl.when(step > 0)
        def _():
            peak_out[...] = jnp.maximum(peak_out[...], peak)

    @staticmethod
    def scratch(plan, columns):
        rows = plan.nx * plan.nz * plan.rows
        held = pltpu.VMEM((2, rows, columns), F32)
        if plan.nc == 1:
            return [held]
        return [
            held,
            held,
            held,
            pltpu.SemaphoreType.DMA((2,)),
            pltpu.SemaphoreType.DMA((2,)),
            pltpu.SemaphoreType.REGULAR,
        ]

    @staticmethod
    def made_of(plan, steps, refs):
        return SiblingSum(plan, steps, *(tuple(refs) + (None,) * (6 - len(refs))))

    @staticmethod
    def params(plan, collective_id):
        if plan.nc == 1:
            return params()
        return params(collective_id=collective_id, has_side_effects=True)


def dot(left, right):
    return lax.dot_general(left, right, (((1,), (0,)), ((), ())), preferred_element_type=F32)


def dot_last(left, right):
    return lax.dot_general(left, right, (((1,), (1,)), ((), ())), preferred_element_type=F32)


def normalize(values):
    centered = values - jnp.mean(values, axis=-1, keepdims=True)
    inverse = lax.rsqrt(jnp.mean(centered * centered, axis=-1, keepdims=True) + norm_epsilon)
    return centered * inverse, inverse


def normalize_back(grad_output, normal, inverse, gain):
    grad_normal = grad_output * gain
    mean_grad = jnp.mean(grad_normal, axis=-1, keepdims=True)
    mean_cross = jnp.mean(grad_normal * normal, axis=-1, keepdims=True)
    return inverse * (grad_normal - mean_grad - normal * mean_cross)


def rotary_tables(length):
    half_width = HEAD // 2
    steps_half = jnp.arange(half_width, dtype=jnp.int32).astype(F32)
    frequency = rope_base ** (-2.0 * steps_half / HEAD)
    positions = jnp.arange(length, dtype=jnp.int32).astype(F32)
    angles = positions[:, None] * frequency[None, :]
    cosine, sine = jnp.cos(angles), jnp.sin(angles)
    heads = LANES // HEAD
    return (
        jnp.concatenate([cosine, cosine] * heads, axis=1),
        jnp.concatenate([-sine, sine] * heads, axis=1),
    )


def swap_halves(values):
    lane = lax.broadcasted_iota(jnp.int32, values.shape, 1)
    ahead = pltpu.roll(values, LANES - HEAD // 2, 1)
    behind = pltpu.roll(values, HEAD // 2, 1)
    return jnp.where(lax.rem(lane, HEAD) < HEAD // 2, ahead, behind)


def of_head(values, head):
    lane = lax.broadcasted_iota(jnp.int32, values.shape, 1)
    return jnp.where(lane // HEAD == head, values, jnp.zeros_like(values))


def params(**more):
    return pltpu.CompilerParams(vmem_limit_bytes=VMEM_LIMIT, **more)


def whole(shape):
    zeros = (0,) * len(shape)
    return pl.BlockSpec(shape, lambda i, place: zeros, pipeline_mode=pl.Buffered(1))


def result(shape):
    zeros = (0,) * len(shape)
    return pl.BlockSpec(shape, lambda i, place: zeros)


def own_index(tensor):
    return lax.axis_index("dp") * tensor + lax.axis_index("tensor")


def device_at(index, tensor):
    return (index // tensor, lax.rem(index, tensor))


def greet_all(me, count, tensor):
    barrier = pltpu.get_barrier_semaphore()

    def greet(far, carry):
        pl.semaphore_signal(
            barrier,
            inc=1,
            device_id=device_at(lax.rem(me + far, count), tensor),
            device_id_type=pl.DeviceIdType.MESH,
        )
        return carry

    lax.fori_loop(1, count, greet, 0)
    pl.semaphore_wait(barrier, count - 1)


def for_all(me, count, tensor, source, target, send_sem, recv_sem, start):
    def act(far, carry):
        peer = lax.rem(me + far, count)
        copy = pltpu.make_async_remote_copy(
            src_ref=source(peer),
            dst_ref=target,
            send_sem=send_sem.at[far - 1],
            recv_sem=recv_sem.at[far - 1],
            device_id=device_at(peer, tensor),
            device_id_type=pl.DeviceIdType.MESH,
        )
        if start:
            copy.start()
        else:
            copy.wait()
        return carry

    lax.fori_loop(1, count, act, 0)


def swap_blocks_kernel(tensor, block_ref, out_ref, held, send_sem, recv_sem):
    count = held.shape[0]
    me = own_index(tensor)
    greet_all(me, count, tensor)
    for start in (True, False):
        for_all(
            me,
            count,
            tensor,
            lambda peer: block_ref.at[peer],
            held.at[me],
            send_sem,
            recv_sem,
            start,
        )
        if start:
            held[pl.ds(me, 1)] = block_ref[pl.ds(me, 1)]
    out_ref[...] = held[...]


def in_vmem():
    return pl.BlockSpec(memory_space=pltpu.VMEM)


def in_place():
    return pl.BlockSpec(memory_space=pl.ANY)


def swap_blocks(plan, blocks):
    return pl.pallas_call(
        functools.partial(swap_blocks_kernel, plan.tensor),
        name="swap_blocks",
        out_shape=jax.ShapeDtypeStruct(blocks.shape, blocks.dtype),
        in_specs=[in_vmem()],
        out_specs=in_vmem(),
        scratch_shapes=[
            pltpu.VMEM(blocks.shape, blocks.dtype),
            pltpu.SemaphoreType.DMA((plan.count - 1,)),
            pltpu.SemaphoreType.DMA((plan.count - 1,)),
        ],
        compiler_params=params(collective_id=0, has_side_effects=True),
    )(blocks)


def total_kernel(
    tensor, block_ref, out_ref, came, held, own, send_sem, recv_sem, late_send, late_recv
):
    count = held.shape[0]
    me = own_index(tensor)
    greet_all(me, count, tensor)
    for start in (True, False):
        for_all(
            me,
            count,
            tensor,
            lambda peer: block_ref.at[peer],
            came.at[me],
            send_sem,
            recv_sem,
            start,
        )
        if start:
            came[pl.ds(me, 1)] = block_ref[pl.ds(me, 1)]
    summed = jnp.sum(came[...], axis=0)
    own[...] = summed
    for start in (True, False):
        for_all(me, count, tensor, lambda peer: own, held.at[me], late_send, late_recv, start)
        if start:
            held[pl.ds(me, 1)] = summed[None]
    out_ref[...] = held[...]


def total(plan, values, scalar):
    count = plan.count
    part = -(-values.shape[0] // count)
    padded = jnp.pad(values, (0, part * count - values.shape[0])).reshape(count, part)
    tail = jnp.full((count, 8 * LANES - part), scalar, values.dtype)
    blocks = jnp.concatenate([padded, tail], axis=1).reshape(count, 8, LANES)
    sums = pl.pallas_call(
        functools.partial(total_kernel, plan.tensor),
        name="total",
        out_shape=jax.ShapeDtypeStruct(blocks.shape, blocks.dtype),
        in_specs=[in_vmem()],
        out_specs=in_vmem(),
        scratch_shapes=[
            pltpu.VMEM(blocks.shape, blocks.dtype),
            pltpu.VMEM(blocks.shape, blocks.dtype),
            pltpu.VMEM(blocks.shape[1:], blocks.dtype),
        ]
        + [pltpu.SemaphoreType.DMA((count - 1,))] * 4,
        compiler_params=params(collective_id=1, has_side_effects=True),
    )(blocks).reshape(count, 8 * LANES)
    return sums[:, :part].reshape(-1)[: values.shape[0]], sums[0, part]


class Transport:
    def __init__(self, plan, shard, out, at, order, send_sem, recv_sem):
        self.plan, self.shard, self.out, self.at, self.order = plan, shard, out, at, order
        self.send_sem, self.recv_sem = send_sem, recv_sem
        self.dp_index, self.y = lax.axis_index("dp"), lax.axis_index("tensor")
        self.c = lax.rem(self.dp_index, plan.nc)
        self.x = lax.rem(self.dp_index // plan.nc, plan.nx)
        self.z = self.dp_index // (plan.nc * plan.nx)

    def device(self, z, x, c, y):
        return ((z * self.plan.nx + x) * self.plan.nc + c, y)

    def copies(self, stage):
        plan = self.plan
        z, x, c, y = self.z, self.x, self.c, self.y
        if stage == 0:
            target = self.out.at[(y, z, x, c) + self.at]
            return [
                pltpu.make_async_remote_copy(
                    src_ref=self.shard.at[self.at],
                    dst_ref=target,
                    send_sem=self.send_sem.at[far - 1],
                    recv_sem=self.recv_sem.at[far - 1],
                    device_id=self.device(lax.rem(z + far, plan.nz), x, c, y),
                    device_id_type=pl.DeviceIdType.MESH,
                )
                for far in range(1, plan.nz)
            ]
        path = self.order + ("c",)
        done = path[: stage - 1]
        axis = path[stage - 1]
        every = slice(None)
        block = self.out.at[
            (
                every if "y" in done else y,
                every,
                every if "x" in done else x,
                every if "c" in done else c,
            )
            + self.at
        ]
        device = {
            "x": self.device(z, 1 - x, c, y),
            "y": self.device(z, x, c, 1 - y),
            "c": self.device(z, x, 1 - c, y),
        }[axis]
        slot = plan.nz - 2 + stage
        return [
            pltpu.make_async_remote_copy(
                src_ref=block,
                dst_ref=block,
                send_sem=self.send_sem.at[slot],
                recv_sem=self.recv_sem.at[slot],
                device_id=device,
                device_id_type=pl.DeviceIdType.MESH,
            )
        ]

    def own(self):
        slot = self.plan.nz + 2
        return pltpu.make_async_copy(
            self.shard.at[self.at],
            self.out.at[(self.y, self.z, self.x, self.c) + self.at],
            self.send_sem.at[slot],
        )

    def advance(self, stage):
        if stage == 0:
            self.own().start()
        elif stage == 1:
            self.own().wait()
        if stage > 0:
            for copy in self.copies(stage - 1):
                copy.wait_recv()
        if stage < 4:
            for copy in self.copies(stage):
                copy.start()
        else:
            for earlier in range(4):
                for copy in self.copies(earlier):
                    copy.wait_send()


def greet_neighbours(plan):
    dp_index, y = lax.axis_index("dp"), lax.axis_index("tensor")
    c = lax.rem(dp_index, plan.nc)
    x = lax.rem(dp_index // plan.nc, plan.nx)
    z = dp_index // (plan.nc * plan.nx)
    places = [(lax.rem(z + far, plan.nz), x, c, y) for far in range(1, plan.nz)]
    places += [(z, 1 - x, c, y), (z, x, c, 1 - y), (z, x, 1 - c, y)]
    barrier = pltpu.get_barrier_semaphore()
    for to_z, to_x, to_c, to_y in places:
        pl.semaphore_signal(
            barrier,
            inc=1,
            device_id=((to_z * plan.nx + to_x) * plan.nc + to_c, to_y),
            device_id_type=pl.DeviceIdType.MESH,
        )
    pl.semaphore_wait(barrier, len(places))


def transport_slots(plan):
    return plan.nz + 3


def fetch_kernel(plan, orders, rows_ref, *refs):
    number = len(orders)
    shards, came = refs[:number], refs[number]
    outs = refs[number + 1 : 2 * number + 1]
    send_sem, recv_sem, own_sem, weight_send, weight_recv = refs[2 * number + 1 :]
    count, tensor = plan.count, plan.tensor
    me = own_index(tensor)
    greet_all(me, count, tensor)
    units = [
        Transport(
            plan,
            shards[n],
            outs[n],
            (slice(None),),
            orders[n],
            weight_send.at[n],
            weight_recv.at[n],
        )
        for n in range(number)
    ]
    for unit in units:
        unit.advance(0)
    own = pltpu.make_async_copy(rows_ref.at[me], came.at[me], own_sem)
    own.start()

    def rows(start):
        for_all(
            me,
            count,
            tensor,
            lambda peer: rows_ref.at[peer],
            came.at[me],
            send_sem,
            recv_sem,
            start,
        )

    rows(True)
    for stage in range(1, 5):
        for unit in units:
            unit.advance(stage)
    own.wait()
    rows(False)


def fetch(plan, rows, shards, orders):
    number = len(shards)
    slots = transport_slots(plan)
    outs = pl.pallas_call(
        functools.partial(fetch_kernel, plan, orders),
        name="fetch",
        out_shape=[jax.ShapeDtypeStruct(rows.shape, rows.dtype)]
        + [plan.gathered_shape(shard) for shard in shards],
        in_specs=[in_place()] * (1 + number),
        out_specs=[in_place()] * (1 + number),
        scratch_shapes=[
            pltpu.SemaphoreType.DMA((plan.count - 1,)),
            pltpu.SemaphoreType.DMA((plan.count - 1,)),
            pltpu.SemaphoreType.DMA(()),
            pltpu.SemaphoreType.DMA((number, slots)),
            pltpu.SemaphoreType.DMA((number, slots)),
        ],
        compiler_params=params(collective_id=4, has_side_effects=True),
    )(rows, *shards)
    return outs[0], [w.reshape(plan.tensor, -1, w.shape[-1]) for w in outs[1:]]


def wire_scale(plan, peak):
    bound = peak[0, 0] * (plan.count // plan.nc)
    exponent = jnp.floor(jnp.log2(32768.0 / jnp.maximum(bound, 1e-30)))
    return jnp.exp2(jnp.clip(exponent, -60.0, 60.0))


class PeakExchange:
    def __init__(self, plan, own, held, send_sem, recv_sem):
        self.own, self.held, self.send_sem, self.recv_sem = own, held, send_sem, recv_sem
        dp_index, y = lax.axis_index("dp"), lax.axis_index("tensor")
        c = lax.rem(dp_index, plan.nc)
        x = lax.rem(dp_index // plan.nc, plan.nx)
        z = dp_index // (plan.nc * plan.nx)

        def device(z, x, y):
            return ((z * plan.nx + x) * plan.nc + c, y)

        self.peers = (
            [device(z, 1 - x, y), device(z, x, 1 - y), device(z, 1 - x, 1 - y)],
            [device(lax.rem(z + far, plan.nz), x, y) for far in range(1, plan.nz)],
        )

    def greet(self, more=()):
        barrier = pltpu.get_barrier_semaphore()
        peers = self.peers[0] + self.peers[1] + list(more)
        for peer in peers:
            pl.semaphore_signal(
                barrier, inc=1, device_id=peer, device_id_type=pl.DeviceIdType.MESH
            )
        pl.semaphore_wait(barrier, len(peers))

    def copies(self, stage):
        first = len(self.peers[0]) * stage
        return [
            pltpu.make_async_remote_copy(
                src_ref=self.own.at[stage],
                dst_ref=self.held.at[first + n],
                send_sem=self.send_sem.at[first + n],
                recv_sem=self.recv_sem.at[first + n],
                device_id=peer,
                device_id_type=pl.DeviceIdType.MESH,
            )
            for n, peer in enumerate(self.peers[stage])
        ]

    def start(self, stage, value):
        self.own[stage] = value
        for copy in self.copies(stage):
            copy.start()

    def finish(self, stage):
        for copy in self.copies(stage):
            copy.wait()
        value = self.own[stage]
        first = len(self.peers[0]) * stage
        for n in range(len(self.peers[stage])):
            value = jnp.maximum(value, self.held[first + n])
        return value

    @staticmethod
    def scratch(plan):
        number = 3 + plan.nz - 1
        return [
            pltpu.VMEM((2, 8, LANES), F32),
            pltpu.VMEM((number, 8, LANES), F32),
            pltpu.SemaphoreType.DMA((number,)),
            pltpu.SemaphoreType.DMA((number,)),
        ]


def token_places(slot_ids, length, vocab_shard):
    count = slot_ids.shape[0]
    order = jnp.arange(count, dtype=jnp.int32)
    key = jnp.where(order < length, slot_ids, -1)
    owner = key // vocab_shard
    row = key - owner * vocab_shard
    same = key[:, None] == key[None, :]
    first_at = jnp.min(jnp.where(same, order[None, :], count), axis=1)
    first = (first_at == order) & (key >= 0)
    earlier = first[None, :] & (owner[:, None] == owner[None, :])
    place = jnp.sum(
        (earlier & (order[None, :] < first_at[:, None])).astype(jnp.int32), axis=1
    )
    return owner, row, first, jnp.where(key >= 0, place, -1)


def round_slots(owner, place, room, turn):
    within = place - turn * room
    served = (within >= 0) & (within < room)
    return jnp.where(served, owner * room + within, -1)


def round_wants(slot, first, row, slots):
    wanted = first[None, :] & (slot[None, :] == jnp.arange(slots, dtype=jnp.int32)[:, None])
    return jnp.max(jnp.where(wanted, row[None, :], -1), axis=1)


def picked_rows(wants, table_low):
    chosen = wants.reshape(-1)[:, None] == jnp.arange(table_low.shape[0], dtype=jnp.int32)[None, :]
    return jnp.dot(chosen.astype(BF16), table_low, preferred_element_type=F32).astype(BF16)


def spread_rows(slot, rows):
    chosen = slot[:, None] == jnp.arange(rows.shape[0], dtype=jnp.int32)[None, :]
    return jnp.dot(chosen.astype(BF16), rows, preferred_element_type=F32)


def summed_rows(index, rows, count):
    chosen = jnp.arange(count, dtype=jnp.int32)[:, None] == index[None, :]
    return jnp.dot(chosen.astype(BF16), rows, preferred_element_type=F32)


def swap_rows(plan, rows):
    parts = rows.reshape(plan.count, rows.shape[0] // plan.count, rows.shape[1])
    return lax.all_to_all(parts, AXES, 0, 0, tiled=True).reshape(rows.shape)


def transport_units(plan, shards, outs, send_sem, recv_sem):
    units = []
    for n in range(len(shards)):
        half = shards[n].shape[1] // 2
        for side, order in enumerate((("x", "y"), ("y", "x"))):
            number = len(units)
            units.append(
                Transport(
                    plan,
                    shards[n],
                    outs[n],
                    (slice(None), pl.ds(side * half, half)),
                    order,
                    send_sem.at[number],
                    recv_sem.at[number],
                )
            )
    return units


SLOTS_PER_STEP = 4
TRANSPORT_SLOTS = {
    0: ((0, 0),),
    7: ((0, 1), (1, 0)),
    11: ((0, 2),),
    14: ((1, 1), (2, 0)),
    18: ((0, 3), (1, 2)),
    22: ((2, 1),),
}
TRANSPORT_END = ((1, 3), (2, 2), (2, 3), (0, 4), (1, 4), (2, 4))


def advance(units, events):
    for matrix, stage in events:
        for side in range(2):
            units[2 * matrix + side].advance(stage)


def attend_kernel(plan, number, place, *refs):
    (embedded, wq, wk, wv, wo, cosine, sine, norms) = refs[:8]
    shards = refs[8 : 8 + number]
    (q, k, v, mixed_out, log_total, low_one, normal_one, inverse_one) = refs[8 + number : 16 + number]
    (low_two, normal_two, inverse_two) = refs[16 + number : 19 + number]
    gathered = refs[19 + number : 19 + 2 * number]
    scratch = refs[19 + 2 * number :]
    weights, mixed = scratch[:2]
    rows = embedded.shape[0]
    step = pl.program_id(0)
    if number:
        units = transport_units(plan, shards, gathered, *scratch[2:4])

        @pl.when(step == 0)
        def _():
            greet_neighbours(plan)

    def transport(part):
        if number:
            for slot, events in TRANSPORT_SLOTS.items():
                if slot % SLOTS_PER_STEP == part:

                    @pl.when(step == slot // SLOTS_PER_STEP)
                    def _():
                        advance(units, events)

    @pl.when(step == 0)
    def _():
        for start in range(0, rows, ROW_BLOCK):
            at = slice(start, start + ROW_BLOCK)
            normal, inverse = normalize(embedded[at, :])
            normal_one[at, :] = normal
            inverse_one[at, :] = inverse
            low_one[at, :] = (normal * norms[0:1, :] + norms[1:2, :]).astype(BF16)

    transport(0)
    weights[:, :LANES] = wq[...]
    weights[:, LANES : 2 * LANES] = wk[...]
    weights[:, 2 * LANES :] = wv[...]
    for start in range(0, rows, ROW_BLOCK):
        at = slice(start, start + ROW_BLOCK)
        made = dot(low_one[at, :], weights[...])
        query, key = made[:, :LANES], made[:, LANES : 2 * LANES]
        query = query * cosine[at, :] + swap_halves(query) * sine[at, :]
        key = key * cosine[at, :] + swap_halves(key) * sine[at, :]
        q[at, :] = (query * HEAD**-0.5).astype(BF16)
        k[at, :] = key.astype(BF16)
        v[at, :] = made[:, 2 * LANES :].astype(BF16)
    position = lax.broadcasted_iota(jnp.int32, (rows, 1), 0)
    bias = jnp.where(position < place[4], 0.0, masked_score)
    keys = k[...]
    values = v[...].T
    for start in range(0, rows, ROW_BLOCK):
        at = slice(start, start + ROW_BLOCK)
        if start > 0:
            transport(start // ROW_BLOCK)
        outs = []
        for head in range(LANES // HEAD):
            scores = dot_last(keys, of_head(q[at, :], head)) + bias
            top = jnp.max(scores, axis=0, keepdims=True)
            exponent = jnp.exp(scores - top)
            summed = jnp.sum(exponent, axis=0, keepdims=True)
            out = dot(values[head * HEAD : (head + 1) * HEAD, :], exponent.astype(BF16))
            outs.append(out / summed)
            log_total[head : head + 1, at] = top + jnp.log(summed)
        made = jnp.concatenate(outs, axis=0).T.astype(BF16)
        mixed_out[at, :] = made
        mixed[step, at, :] = made

    @pl.when(step == pl.num_programs(0) - 1)
    def _():
        per_part = wo.shape[2] // LANES
        for start in range(0, rows, ROW_BLOCK):
            at = slice(start, start + ROW_BLOCK)
            product = normal_one[at, :] * norms[0:1, :] + norms[1:2, :]
            for part in range(plan.tensor):
                whole_mixed = jnp.concatenate(
                    [mixed[part * per_part + n, at, :] for n in range(per_part)], axis=1
                )
                product = product + dot_last(whole_mixed, wo[part])
            normal, inverse = normalize(product)
            normal_two[at, :] = normal
            inverse_two[at, :] = inverse
            low_two[at, :] = (normal * norms[2:3, :] + norms[3:4, :]).astype(BF16)
        if number:
            advance(units, TRANSPORT_END)


def attend(plan, place, embedded, wq, wk, wv, wo, cosine, sine, norms, shards):
    rows, width = embedded.shape
    pairs = wq.shape[-1] // LANES
    steps = plan.tensor * pairs
    number = len(shards)

    def locate(i):
        return i // pairs, lax.rem(i, pairs)

    by_pair = pl.BlockSpec((None, rows, LANES), lambda i, place: (i, 0, 0))
    shape = jax.ShapeDtypeStruct((steps, rows, LANES), BF16)
    normed = [
        jax.ShapeDtypeStruct((rows, width), BF16),
        jax.ShapeDtypeStruct((rows, width), F32),
        jax.ShapeDtypeStruct((rows, 1), F32),
    ]
    normed_specs = [result((rows, width)), result((rows, width)), result((rows, 1))]
    scratch = [pltpu.VMEM((width, 3 * LANES), BF16), pltpu.VMEM((steps, rows, LANES), BF16)]
    more = {}
    if number:
        slots = transport_slots(plan)
        scratch += [pltpu.SemaphoreType.DMA((2 * number, slots))] * 2
        more = dict(collective_id=5, has_side_effects=True)
    outs = pl.pallas_call(
        functools.partial(attend_kernel, plan, number),
        name="attend",
        out_shape=[
            shape,
            shape,
            shape,
            jax.ShapeDtypeStruct((rows, steps * LANES), BF16),
            jax.ShapeDtypeStruct((steps, 8, rows), F32),
        ]
        + normed
        + normed
        + [plan.gathered_shape(shard) for shard in shards],
        grid_spec=pltpu.PrefetchScalarGridSpec(
            num_scalar_prefetch=1,
            grid=(steps,),
            in_specs=[whole((rows, width))]
            + [plan.weight_spec(width, LANES, locate)] * 3
            + [
                whole(wo.shape),
                whole((rows, LANES)),
                whole((rows, LANES)),
                whole(norms.shape),
            ]
            + [in_place()] * number,
            out_specs=[
                by_pair,
                by_pair,
                by_pair,
                pl.BlockSpec((rows, LANES), lambda i, place: (0, i)),
                pl.BlockSpec((None, 8, rows), lambda i, place: (i, 0, 0)),
            ]
            + normed_specs
            + normed_specs
            + [in_place()] * number,
            scratch_shapes=scratch,
        ),
        compiler_params=params(**more),
        cost_estimate=pl.CostEstimate(
            flops=8 * rows * width * width + 16 * rows * rows * width,
            bytes_accessed=rows * width * 30,
            transcendentals=0,
        ),
    )(place, embedded, wq, wk, wv, wo, cosine, sine, norms, *shards)
    return outs[:11], [w.reshape(plan.tensor, -1, w.shape[-1]) for w in outs[11:]]


def feed_kernel(
    plan,
    place,
    x,
    wg,
    wu,
    wd,
    normal_two,
    norms,
    gate_out,
    up_out,
    hidden_out,
    normal_out,
    inverse_out,
    pool_out,
):
    rows, width = x.shape
    first = pl.program_id(0) == 0

    @pl.when(first)
    def _():
        normal_out[...] = jnp.zeros_like(normal_out)

    for start in range(0, rows, ROW_BLOCK):
        at = slice(start, start + ROW_BLOCK)
        gate, up = dot(x[at, :], wg[...]), dot(x[at, :], wu[...])
        hidden = (gate * jax.nn.sigmoid(gate) * up).astype(BF16)
        gate_out[at, :] = gate.astype(BF16)
        up_out[at, :] = up.astype(BF16)
        hidden_out[at, :] = hidden
        normal_out[at, :] = normal_out[at, :] + dot_last(hidden, wd[...])

    @pl.when(pl.program_id(0) == pl.num_programs(0) - 1)
    def _():
        pooled = jnp.zeros((1, width), F32)
        for start in range(0, rows, ROW_BLOCK):
            at = slice(start, start + ROW_BLOCK)
            second_out = normal_two[at, :] * norms[2:3, :] + norms[3:4, :]
            normal, inverse = normalize(second_out + normal_out[at, :])
            normal_out[at, :] = normal
            inverse_out[at, :] = inverse
            position = start + lax.broadcasted_iota(jnp.int32, (ROW_BLOCK, 1), 0)
            kept = jnp.where(position < place[4], normal, 0.0)
            pooled = pooled + jnp.sum(kept, axis=0, keepdims=True)
        pool_out[...] = pooled


def feed(plan, place, x, wg, wu, wd, normal_two, norms):
    rows, width = x.shape
    hidden = wg.shape[-1]
    chunks = hidden // HIDDEN_BLOCK
    steps = plan.tensor * chunks

    def locate(i):
        return i // chunks, lax.rem(i, chunks)

    by_chunk = pl.BlockSpec((rows, HIDDEN_BLOCK), lambda i, place: (0, i))
    shape = jax.ShapeDtypeStruct((rows, plan.tensor * hidden), BF16)
    return pl.pallas_call(
        functools.partial(feed_kernel, plan),
        name="feed",
        out_shape=[
            shape,
            shape,
            shape,
            jax.ShapeDtypeStruct((rows, width), F32),
            jax.ShapeDtypeStruct((rows, 1), F32),
            jax.ShapeDtypeStruct((1, width), F32),
        ],
        grid_spec=pltpu.PrefetchScalarGridSpec(
            num_scalar_prefetch=1,
            grid=(steps,),
            in_specs=[
                whole((rows, width)),
                plan.weight_spec(width, HIDDEN_BLOCK, locate),
                plan.weight_spec(width, HIDDEN_BLOCK, locate),
                plan.weight_spec(width, HIDDEN_BLOCK, locate),
                whole((rows, width)),
                whole(norms.shape),
            ],
            out_specs=[
                by_chunk,
                by_chunk,
                by_chunk,
                result((rows, width)),
                result((rows, 1)),
                result((1, width)),
            ],
        ),
        compiler_params=params(),
        cost_estimate=pl.CostEstimate(
            flops=6 * rows * width * plan.tensor * hidden,
            bytes_accessed=rows * width * 40,
            transcendentals=0,
        ),
    )(place, x, wg, wu, wd, normal_two, norms)


def contrast_kernel(
    tensor, place, pool_ref, norms, scale_ref, loss_ref, grad_ref, held, own, send_sem, recv_sem
):
    count = held.shape[0]
    me = own_index(tensor)
    greet_all(me, count, tensor)
    length = jnp.full((1, 1), place[4], jnp.int32).astype(F32)
    pooled = pool_ref[...] / length * norms[4:5, :] + norms[5:6, :]
    inverse = lax.rsqrt(jnp.sum(pooled * pooled, axis=-1, keepdims=True) + norm_epsilon)
    vector = pooled * inverse
    own[...] = vector
    for start in (True, False):
        for_all(me, count, tensor, lambda peer: own, held.at[me], send_sem, recv_sem, start)
        if start:
            held[pl.ds(me, 1)] = vector[None]
    vectors = held[...].reshape(count, held.shape[2])
    scale = jnp.exp(scale_ref[...])
    logits = scale * lax.dot_general(
        vectors,
        vectors,
        (((1,), (1,)), ((), ())),
        precision=lax.Precision.HIGHEST,
        preferred_element_type=F32,
    )
    row = lax.broadcasted_iota(jnp.int32, (count, count), 0)
    column = lax.broadcasted_iota(jnp.int32, (count, count), 1)
    crossed = (lax.rem(row, 2) == 0) & (lax.rem(column, 2) == 1)
    shown = jnp.where(crossed, logits, masked_score)
    row_max = jnp.max(shown, axis=1, keepdims=True)
    row_exp = jnp.where(crossed, jnp.exp(shown - row_max), 0.0)
    row_sum = jnp.sum(row_exp, axis=1, keepdims=True)
    column_max = jnp.max(shown, axis=0, keepdims=True)
    column_exp = jnp.where(crossed, jnp.exp(shown - column_max), 0.0)
    column_sum = jnp.sum(column_exp, axis=0, keepdims=True)
    even = lax.rem(lax.broadcasted_iota(jnp.int32, (count, 1), 0), 2) == 0
    odd = lax.rem(lax.broadcasted_iota(jnp.int32, (1, count), 1), 2) == 1
    row_safe = jnp.where(even, row_sum, 1.0)
    column_safe = jnp.where(odd, column_sum, 1.0)
    row_lse = jnp.where(even, row_max + jnp.log(row_safe), 0.0)
    column_lse = jnp.where(odd, column_max + jnp.log(column_safe), 0.0)
    own = crossed & (column == row + 1)
    diagonal = jnp.sum(jnp.where(own, logits, 0.0))
    half = 1.0 / count
    loss = half * (jnp.sum(row_lse) + jnp.sum(column_lse) - 2.0 * diagonal)
    grad_logits = half * (
        row_exp / row_safe + column_exp / column_safe - 2.0 * own.astype(F32)
    )
    grad_scale = jnp.sum(grad_logits * jnp.where(crossed, logits, 0.0))
    both = grad_logits + grad_logits.T
    grad_vectors = scale * lax.dot_general(
        both,
        vectors,
        (((1,), (0,)), ((), ())),
        precision=lax.Precision.HIGHEST,
        preferred_element_type=F32,
    )
    mine = lax.broadcasted_iota(jnp.int32, (count, 1), 0) == me
    grad_own = jnp.sum(jnp.where(mine, grad_vectors, 0.0), axis=0, keepdims=True)
    along = jnp.sum(grad_own * vector, axis=-1, keepdims=True)
    grad_ref[...] = inverse * (grad_own - vector * along) / length
    lane = lax.broadcasted_iota(jnp.int32, loss_ref.shape, 1)
    loss_ref[...] = jnp.where(lane == 0, loss, grad_scale)


def contrast(plan, place, pool, norms, log_scale):
    width = pool.shape[1]
    loss, grad = pl.pallas_call(
        functools.partial(contrast_kernel, plan.tensor),
        name="contrast",
        out_shape=[
            jax.ShapeDtypeStruct((1, LANES), F32),
            jax.ShapeDtypeStruct((1, width), F32),
        ],
        in_specs=[pl.BlockSpec(memory_space=pltpu.SMEM)] + [in_vmem()] * 3,
        out_specs=[in_vmem()] * 2,
        scratch_shapes=[
            pltpu.VMEM((plan.count, 1, width), F32),
            pltpu.VMEM((1, width), F32),
            pltpu.SemaphoreType.DMA((plan.count - 1,)),
            pltpu.SemaphoreType.DMA((plan.count - 1,)),
        ],
        compiler_params=params(collective_id=2, has_side_effects=True),
    )(place, pool, norms, log_scale.reshape(1, 1))
    return loss[0, 0], loss[0, 1], grad


def feed_back_kernel(plan, steps, place, *refs):
    (
        grad_pool,
        x,
        gate_ref,
        up_ref,
        hidden_ref,
        wg,
        wu,
        wd,
        normal_three,
        inverse_three,
        normal_two,
        inverse_two,
        norms,
        part_one,
        part_two,
        grad_out,
        low_out,
        norm_out,
        peak_out,
        low,
        low_turned,
        x_turned,
        made,
        product,
    ) = refs[:24]
    rows, width = x.shape
    step = pl.program_id(0)
    half = BACK_BLOCK // 2
    if plan.stepped:
        sums = SiblingSum.made_of(plan, steps, refs[24:-4])
        exchange = PeakExchange(plan, *refs[-4:])
    else:
        sums = SiblingSum.made_of(plan, steps, refs[24:])

    @pl.when(step == 0)
    def _():
        if plan.stepped:
            exchange.greet([sums.sibling])
        for start in range(0, rows, ROW_BLOCK):
            at = slice(start, start + ROW_BLOCK)
            position = start + lax.broadcasted_iota(jnp.int32, (ROW_BLOCK, 1), 0)
            grad_third = jnp.where(position < place[4], grad_pool[...], 0.0)
            grad = normalize_back(
                grad_third, normal_three[at, :], inverse_three[at, :], norms[4:5, :]
            )
            grad_out[at, :] = grad
            low[at, :] = grad.astype(BF16)
            low_turned[:, at] = grad.astype(BF16).T
            x_turned[:, at] = x[at, :].T

    @pl.when(step < steps)
    def _():
        for start in range(0, rows, ROW_BLOCK):
            at = slice(start, start + ROW_BLOCK)
            grad_hidden = dot(low[at, :], wd[...])
            gate = gate_ref[at, :].astype(F32)
            up = up_ref[at, :].astype(F32)
            share_gate = jax.nn.sigmoid(gate)
            grad_up = grad_hidden * gate * share_gate
            grad_gate = grad_hidden * up * share_gate * (1.0 + gate * (1.0 - share_gate))
            made[at, :BACK_BLOCK] = grad_gate.astype(BF16)
            made[at, BACK_BLOCK:] = grad_up.astype(BF16)
            grad_out[at, :] = (
                grad_out[at, :]
                + dot_last(made[at, :BACK_BLOCK], wg[...])
                + dot_last(made[at, BACK_BLOCK:], wu[...])
            )
        down = dot(low_turned[...], hidden_ref[...])
        product[:, :BACK_BLOCK] = dot(x_turned[...], made[:, :BACK_BLOCK])
        product[:, BACK_BLOCK : BACK_BLOCK + half] = down[:, :half]
        product[:, BACK_BLOCK + half : 2 * BACK_BLOCK + half] = dot(
            x_turned[...], made[:, BACK_BLOCK:]
        )
        product[:, 2 * BACK_BLOCK + half :] = down[:, half:]
        sums.push(step, product)

    @pl.when(step > 0)
    def _():
        sums.pull(step - 1, (part_one, part_two), (BACK_BLOCK + half,) * 2, peak_out)

    @pl.when(step == steps)
    def _():
        gain_grad = jnp.zeros((1, width), F32)
        shift_grad = jnp.zeros((1, width), F32)
        if plan.stepped:
            exchange.start(0, peak_out[...])
        for start in range(0, rows, ROW_BLOCK):
            at = slice(start, start + ROW_BLOCK)
            if plan.stepped and start == rows // 2:
                exchange.start(1, exchange.finish(0))
            grad_second = grad_out[at, :]
            normal = normal_two[at, :]
            grad = normalize_back(grad_second, normal, inverse_two[at, :], norms[2:3, :])
            gain_grad = gain_grad + jnp.sum(grad_second * normal, axis=0, keepdims=True)
            shift_grad = shift_grad + jnp.sum(grad_second, axis=0, keepdims=True)
            grad_out[at, :] = grad
            low_out[at, :] = grad.astype(BF16)
        norm_out[0:1, :] = gain_grad
        norm_out[1:2, :] = shift_grad
        if plan.stepped:
            peak_out[...] = exchange.finish(1)


def feed_back(
    plan,
    place,
    grad_pool,
    x,
    gate,
    up,
    hidden_low,
    wg,
    wu,
    wd,
    normal_three,
    inverse_three,
    normal_two,
    inverse_two,
    norms,
):
    rows, width = x.shape
    hidden = wg.shape[-1]
    chunks = hidden // BACK_BLOCK
    steps = plan.tensor * chunks

    def locate(i):
        now = jnp.minimum(i, steps - 1)
        return now // chunks, lax.rem(now, chunks)

    def locate_late(i):
        now = jnp.maximum(i - 1, 0)
        return now // chunks, lax.rem(now, chunks)

    by_chunk = pl.BlockSpec(
        (rows, BACK_BLOCK), lambda i, place: (0, jnp.minimum(i, steps - 1))
    )
    columns = BACK_BLOCK * 3 // 2
    return pl.pallas_call(
        functools.partial(feed_back_kernel, plan, steps),
        name="feed_back",
        out_shape=[
            plan.grad_shape("yx", columns * chunks),
            plan.grad_shape("xy", columns * chunks),
            jax.ShapeDtypeStruct((rows, width), F32),
            jax.ShapeDtypeStruct((rows, width), BF16),
            jax.ShapeDtypeStruct((8, width), F32),
            jax.ShapeDtypeStruct((8, LANES), F32),
        ],
        grid_spec=pltpu.PrefetchScalarGridSpec(
            num_scalar_prefetch=1,
            grid=(steps + 1,),
            in_specs=[
                whole((1, width)),
                whole((rows, width)),
                by_chunk,
                by_chunk,
                by_chunk,
                plan.weight_spec(width, BACK_BLOCK, locate),
                plan.weight_spec(width, BACK_BLOCK, locate),
                plan.weight_spec(width, BACK_BLOCK, locate),
                whole((rows, width)),
                whole((rows, 1)),
                whole((rows, width)),
                whole((rows, 1)),
                whole(norms.shape),
            ],
            out_specs=[
                plan.grad_spec("yx", columns, locate_late),
                plan.grad_spec("xy", columns, locate_late),
                result((rows, width)),
                result((rows, width)),
                result((8, width)),
                result((8, LANES)),
            ],
            scratch_shapes=[
                pltpu.VMEM((rows, width), BF16),
                pltpu.VMEM((width, rows), BF16),
                pltpu.VMEM((width, rows), BF16),
                pltpu.VMEM((rows, 2 * BACK_BLOCK), BF16),
                pltpu.VMEM((width, 3 * BACK_BLOCK), F32),
            ]
            + SiblingSum.scratch(plan, 3 * BACK_BLOCK)
            + (PeakExchange.scratch(plan) if plan.stepped else []),
        ),
        compiler_params=SiblingSum.params(plan, 6),
        cost_estimate=pl.CostEstimate(
            flops=20 * rows * width * plan.tensor * hidden,
            bytes_accessed=rows * width * 60,
            transcendentals=0,
        ),
    )(
        place,
        grad_pool,
        x,
        gate,
        up,
        hidden_low,
        wg,
        wu,
        wd,
        normal_three,
        inverse_three,
        normal_two,
        inverse_two,
        norms,
    )


def unfold_feed(part_one, part_two, hidden):
    rows = part_one.shape[0]
    half = BACK_BLOCK // 2
    one = part_one.reshape(rows, hidden // BACK_BLOCK, BACK_BLOCK + half)
    two = part_two.reshape(rows, hidden // BACK_BLOCK, BACK_BLOCK + half)
    down = jnp.concatenate([one[:, :, BACK_BLOCK:], two[:, :, BACK_BLOCK:]], axis=2)
    return (
        one[:, :, :BACK_BLOCK].reshape(rows, hidden),
        two[:, :, :BACK_BLOCK].reshape(rows, hidden),
        down.reshape(rows, hidden),
    )


def heads_back_kernel(
    place, ga, q, k, v, mixed, log_total, wo, cosine, sine, made, gm, key_grad, value_grad
):
    rows = ga.shape[0]
    for start in range(0, rows, ROW_BLOCK):
        at = slice(start, start + ROW_BLOCK)
        gm[at, :] = dot(ga[at, :], wo[...]).astype(BF16)
    position = lax.broadcasted_iota(jnp.int32, (rows, 1), 0)
    bias = jnp.where(position < place[4], 0.0, masked_score)
    keys, values = k[...], v[...]
    keys_turned = keys.T
    for start in range(0, rows, ROW_BLOCK):
        at = slice(start, start + ROW_BLOCK)
        inner = (gm[at, :].astype(F32) * mixed[at, :].astype(F32)).T
        outs = []
        for head in range(LANES // HEAD):
            of = slice(head * HEAD, (head + 1) * HEAD)
            query = of_head(q[at, :], head)
            grad = of_head(gm[at, :], head)
            inner_sum = jnp.sum(inner[of, :], axis=0, keepdims=True)
            scores = dot_last(keys, query) + bias
            probs = jnp.exp(scores - log_total[head : head + 1, at])
            grad_probs = dot_last(values, grad)
            grad_scores = (probs * (grad_probs - inner_sum)).astype(BF16)
            value_part = dot(probs.astype(BF16), grad)
            key_part = dot(grad_scores, query)
            if start == 0 and head == 0:
                value_grad[...] = value_part
                key_grad[...] = key_part
            else:
                value_grad[...] = value_grad[...] + value_part
                key_grad[...] = key_grad[...] + key_part
            outs.append(dot(keys_turned[of, :], grad_scores))
        grad_query = jnp.concatenate(outs, axis=0).T * HEAD**-0.5
        grad_query = grad_query * cosine[at, :] - swap_halves(grad_query) * sine[at, :]
        made[at, :LANES] = grad_query.astype(BF16)
    for start in range(0, rows, ROW_BLOCK):
        at = slice(start, start + ROW_BLOCK)
        grad_key = key_grad[at, :]
        grad_key = grad_key * cosine[at, :] - swap_halves(grad_key) * sine[at, :]
        made[at, LANES : 2 * LANES] = grad_key.astype(BF16)
        made[at, 2 * LANES :] = value_grad[at, :].astype(BF16)


def heads_back(plan, place, first, number, ga, q, k, v, mixed, log_total, wo, cosine, sine):
    rows, width = ga.shape
    pairs = wo.shape[-1] // LANES

    def locate(i):
        now = first + i
        return now // pairs, lax.rem(now, pairs)

    by_pair = pl.BlockSpec((None, rows, LANES), lambda i, place: (first + i, 0, 0))
    return pl.pallas_call(
        heads_back_kernel,
        name="heads_back",
        out_shape=jax.ShapeDtypeStruct((number, rows, 3 * LANES), BF16),
        grid_spec=pltpu.PrefetchScalarGridSpec(
            num_scalar_prefetch=1,
            grid=(number,),
            in_specs=[
                whole((rows, width)),
                by_pair,
                by_pair,
                by_pair,
                pl.BlockSpec((rows, LANES), lambda i, place: (0, first + i)),
                pl.BlockSpec((None, 8, rows), lambda i, place: (first + i, 0, 0)),
                plan.weight_spec(width, LANES, locate),
                whole((rows, LANES)),
                whole((rows, LANES)),
            ],
            out_specs=pl.BlockSpec((None, rows, 3 * LANES), lambda i, place: (i, 0, 0)),
            scratch_shapes=[
                pltpu.VMEM((rows, LANES), BF16),
                pltpu.VMEM((rows, LANES), F32),
                pltpu.VMEM((rows, LANES), F32),
            ],
        ),
        compiler_params=params(),
        cost_estimate=pl.CostEstimate(
            flops=number * 80 * rows * rows * LANES,
            bytes_accessed=rows * width * 2,
            transcendentals=0,
        ),
    )(place, ga, q, k, v, mixed, log_total, wo, cosine, sine)


def first_back_kernel(plan, number, *refs):
    groups = refs[:number]
    (wq, wk, wv, grad_res, normal_one, inverse_one, norms, peak) = refs[number : number + 8]
    low_out, norm_out, peak_out = refs[number + 8 : number + 11]
    step = pl.program_id(0)
    if plan.stepped:
        exchange = PeakExchange(plan, *refs[number + 11 :])

        @pl.when(step == 0)
        def _():
            exchange.greet()
            exchange.start(0, peak[...])

        @pl.when(step == 1)
        def _():
            exchange.start(1, exchange.finish(0))

    pairs = wq.shape[-1] // LANES
    total_grad = grad_res[...]
    places = [(group, n) for group in groups for n in range(group.shape[0])]
    for part in range(plan.tensor):
        for kind, weight in enumerate((wq, wk, wv)):
            lanes = slice(kind * LANES, (kind + 1) * LANES)
            made = []
            for group, n in places[part * pairs : (part + 1) * pairs]:
                made.append(group[n, :, lanes])
            total_grad = total_grad + dot_last(jnp.concatenate(made, axis=1), weight[part])
    normal = normal_one[...]
    grad = normalize_back(total_grad, normal, inverse_one[...], norms[0:1, :])
    low_out[...] = grad.astype(BF16)
    gain_grad = jnp.sum(total_grad * normal, axis=0, keepdims=True)
    shift_grad = jnp.sum(total_grad, axis=0, keepdims=True)

    @pl.when(pl.program_id(0) == 0)
    def _():
        norm_out[...] = jnp.zeros_like(norm_out)

    norm_out[0:1, :] = norm_out[0:1, :] + gain_grad
    norm_out[1:2, :] = norm_out[1:2, :] + shift_grad
    if plan.stepped:

        @pl.when(step == pl.num_programs(0) - 1)
        def _():
            peak_out[...] = exchange.finish(1)


def first_back(plan, groups, wq, wk, wv, grad_res, normal_one, inverse_one, norms, peak):
    rows, width = grad_res.shape
    by_rows = pl.BlockSpec((ROW_BLOCK, width), lambda i: (i, 0))

    def fixed(shape, **more):
        zeros = (0,) * len(shape)
        return pl.BlockSpec(shape, lambda i: zeros, **more)

    return pl.pallas_call(
        functools.partial(first_back_kernel, plan, len(groups)),
        name="first_back",
        out_shape=[
            jax.ShapeDtypeStruct((rows, width), BF16),
            jax.ShapeDtypeStruct((8, width), F32),
            jax.ShapeDtypeStruct((8, LANES), F32),
        ],
        grid=(rows // ROW_BLOCK,),
        in_specs=[
            pl.BlockSpec((g.shape[0], ROW_BLOCK, g.shape[2]), lambda i: (0, i, 0)) for g in groups
        ]
        + [fixed(wq.shape, pipeline_mode=pl.Buffered(1))] * 3
        + [
            by_rows,
            by_rows,
            pl.BlockSpec((ROW_BLOCK, 1), lambda i: (i, 0)),
            fixed(norms.shape),
            fixed((8, LANES)),
        ],
        out_specs=[by_rows, fixed((8, width)), fixed((8, LANES))],
        scratch_shapes=PeakExchange.scratch(plan) if plan.stepped else [],
        compiler_params=(
            params(collective_id=3, has_side_effects=True) if plan.stepped else params()
        ),
        cost_estimate=pl.CostEstimate(
            flops=8 * rows * width * width, bytes_accessed=rows * width * 20, transcendentals=0
        ),
    )(*groups, wq, wk, wv, grad_res, normal_one, inverse_one, norms, peak)


def attend_weights_kernel(plan, steps, number, *refs):
    groups = refs[:number]
    (x, ga, mixed, part_one, part_two, peak_out, x_turned, ga_turned, product) = refs[
        number : number + 9
    ]
    rows, width = x.shape
    step = pl.program_id(0)
    sums = SiblingSum.made_of(plan, steps, refs[number + 9 :])

    @pl.when(step == 0)
    def _():
        sums.greet()
        for start in range(0, rows, ROW_BLOCK):
            at = slice(start, start + ROW_BLOCK)
            ga_turned[:, at] = ga[at, :].T
            x_turned[:, at] = x[at, :].T

    begin = 0
    for group in groups:
        size = group.shape[0]

        @pl.when((step >= begin) & (step < begin + size))
        def _():
            product[:, : 3 * LANES] = dot(x_turned[...], group[step - begin])

        begin += size

    @pl.when(step < steps)
    def _():
        product[:, 3 * LANES :] = dot(ga_turned[...], mixed[...])
        sums.push(step, product)

    @pl.when(step > 0)
    def _():
        sums.pull(step - 1, (part_one, part_two), (2 * LANES,) * 2, peak_out)


def attend_weights(plan, groups, x, ga, mixed, part):
    rows, width = x.shape
    pairs = part // LANES
    steps = plan.tensor * pairs

    def late(order):
        def locate(i):
            now = jnp.maximum(i - 1, 0)
            return now // pairs, lax.rem(now, pairs)

        spec = plan.grad_spec(order, 2 * LANES, locate)
        return pl.BlockSpec(spec.block_shape, lambda i: spec.index_map(i, None))

    def fixed(shape):
        zeros = (0,) * len(shape)
        return pl.BlockSpec(shape, lambda i: zeros, pipeline_mode=pl.Buffered(1))

    return pl.pallas_call(
        functools.partial(attend_weights_kernel, plan, steps, len(groups)),
        name="attend_weights",
        out_shape=[
            plan.grad_shape("yx", 2 * part),
            plan.grad_shape("xy", 2 * part),
            jax.ShapeDtypeStruct((8, LANES), F32),
        ],
        grid=(steps + 1,),
        in_specs=[fixed(g.shape) for g in groups]
        + [
            fixed((rows, width)),
            fixed((rows, width)),
            pl.BlockSpec((rows, LANES), lambda i: (0, jnp.minimum(i, steps - 1))),
        ],
        out_specs=[
            late("yx"),
            late("xy"),
            pl.BlockSpec((8, LANES), lambda i: (0, 0)),
        ],
        scratch_shapes=[
            pltpu.VMEM((width, rows), BF16),
            pltpu.VMEM((width, rows), BF16),
            pltpu.VMEM((width, 4 * LANES), F32),
        ]
        + SiblingSum.scratch(plan, 4 * LANES),
        compiler_params=SiblingSum.params(plan, 7),
        cost_estimate=pl.CostEstimate(
            flops=12 * rows * width * width, bytes_accessed=rows * width * 20, transcendentals=0
        ),
    )(*groups, x, ga, mixed)


def unfold_attend(part_one, part_two):
    rows, columns = part_one.shape
    one = part_one.reshape(rows, columns // (2 * LANES), 2, LANES)
    two = part_two.reshape(rows, columns // (2 * LANES), 2, LANES)
    return [side[:, :, n].reshape(rows, columns // 2) for side in (one, two) for n in (0, 1)]


def adam_step(weight, first_moment, second_moment, gradient, factor):
    clipped = gradient * factor
    first_next = beta_one * first_moment + (1.0 - beta_one) * clipped
    second_next = beta_two * second_moment + (1.0 - beta_two) * clipped * clipped
    corrected_first = first_next / (1.0 - beta_one**STEP)
    corrected_second = second_next / (1.0 - beta_two**STEP)
    change = -learn_rate * (
        corrected_first / (jnp.sqrt(corrected_second) + adam_epsilon) + weight_decay * weight
    )
    return (first_next, second_next, change)


def per_device(
    plan,
    token_ids,
    lengths,
    token_table,
    table_first,
    table_second,
    qkv_weight,
    qkv_first,
    qkv_second,
    out_weight,
    out_first,
    out_second,
    gate_up_weight,
    gate_up_first,
    gate_up_second,
    down_weight,
    down_first,
    down_second,
    norm_params,
    norm_first,
    norm_second,
    log_inverse_warmth,
    scale_first,
    scale_second,
):
    slot_ids = token_ids[0]
    rows = slot_ids.shape[0]
    vocab_shard, width = token_table.shape
    own_length = lax.dynamic_index_in_dim(
        lengths[0], lax.axis_index("tensor"), 0, keepdims=False
    ).astype(jnp.int32)
    place = jnp.stack([jnp.asarray(p, jnp.int32) for p in plan.places()] + [own_length])
    me = lax.axis_index(AXES)

    qkv_low = qkv_weight.astype(BF16)
    gate_up_low = gate_up_weight.astype(BF16)
    early = [qkv_low[:, 0], qkv_low[:, 1], qkv_low[:, 2], out_weight.astype(BF16)]
    late = [gate_up_low[:, 0], gate_up_low[:, 1], down_weight.astype(BF16)]

    table_low = token_table.astype(BF16)
    room = 8 * -(-(5 * rows) // (4 * plan.count * 8))
    slots = room * plan.count
    owner, row, first, token_place = token_places(slot_ids, own_length, vocab_shard)
    slot = round_slots(owner, token_place, room, 0)
    wants = round_wants(slot, first, row, slots).reshape(plan.count, room)
    rounds = jnp.max(token_place) // room + 1
    note = jnp.concatenate(
        [wants, jnp.broadcast_to(rounds, (plan.count, 8 * LANES - room))], axis=1
    )
    notes = swap_blocks(plan, note.reshape(plan.count, 8, LANES)).reshape(plan.count, 8 * LANES)
    asked = notes[:, :room]
    rounds = jnp.max(notes[:, room])
    picked = picked_rows(asked, table_low)
    if plan.stepped:
        half = width // 2
        folded = jnp.concatenate(
            [
                picked[:, :half].reshape(plan.count, room, half),
                picked[:, half:].reshape(plan.count, room, half),
            ],
            axis=1,
        )
        came, (wq, wk, wv, wo) = fetch(
            plan, folded, early, (("x", "y"), ("y", "x"), ("x", "y"), ("y", "x"))
        )
        came = jnp.concatenate([came[:, :room], came[:, room:]], axis=2).reshape(slots, width)
    else:
        came = swap_rows(plan, picked)
        wq, wk, wv, wo = [plan.gather_whole(shard) for shard in early]
    embedded = spread_rows(slot, came)

    def ask(turn):
        later = round_slots(owner, token_place, room, turn)
        later_wants = round_wants(later, first, row, slots).reshape(plan.count, room)
        return later, lax.all_to_all(later_wants, AXES, 0, 0, tiled=True)

    def fetch_more(turn, sofar):
        later, later_asked = ask(turn)
        return sofar + spread_rows(later, swap_rows(plan, picked_rows(later_asked, table_low)))

    embedded = lax.cond(
        rounds > 1,
        lambda sofar: lax.fori_loop(1, rounds, fetch_more, sofar),
        lambda sofar: sofar,
        embedded,
    )
    cosine, sine = rotary_tables(rows)
    made, gathered = attend(
        plan,
        place,
        embedded,
        wq,
        wk,
        wv,
        wo,
        cosine,
        sine,
        norm_params,
        late if plan.stepped else [],
    )
    q, k, v, mixed, log_total, first_low, normal_one, inverse_one = made[:8]
    second_low, normal_two, inverse_two = made[8:]
    if plan.stepped:
        wg, wu, wd = gathered
    else:
        wg, wu, wd = [plan.gather_whole(shard) for shard in late]
    gate, up, hidden_low, normal_three, inverse_three, pool = feed(
        plan, place, second_low, wg, wu, wd, normal_two, norm_params
    )
    batch_loss, grad_log_scale, grad_pool = contrast(
        plan, place, pool, norm_params, log_inverse_warmth
    )
    part_one, part_two, grad_first_res, attended_low, norm_two, peak_two = feed_back(
        plan,
        place,
        grad_pool,
        second_low,
        gate,
        up,
        hidden_low,
        wg,
        wu,
        wd,
        normal_three,
        inverse_three,
        normal_two,
        inverse_two,
        norm_params,
    )
    scale_two = wire_scale(plan, peak_two)
    steps = q.shape[0]
    cut = steps * 2 // 3

    def heads(first, number, grad):
        return heads_back(
            plan, place, first, number, grad, q, k, v, mixed, log_total, wo, cosine, sine
        )

    if plan.stepped:
        part_one = plan.step_along(part_one, "y", scale_two)
        part_two = plan.step_along(part_two, "x", scale_two)
        group_one = heads(0, cut, attended_low)
        part_one, part_two, ready = lax.optimization_barrier((part_one, part_two, attended_low))
        part_one = plan.step_along(part_one, "x", scale_two)
        part_two = plan.step_along(part_two, "y", scale_two)
        group_two = heads(cut, steps - cut, ready)
        part_one, part_two, ready = lax.optimization_barrier((part_one, part_two, attended_low))
        shard_one = plan.step_along(part_one, "z", scale_two)
        shard_two = plan.step_along(part_two, "z", scale_two)
        groups = [group_one, group_two]
    else:
        shard_one, shard_two = plan.scatter_whole(part_one), plan.scatter_whole(part_two)
        groups = [heads(0, steps, attended_low)]
        ready = attended_low
    part_three, part_four, peak_one = attend_weights(
        plan, groups, first_low, ready, mixed, wq.shape[-1]
    )
    peak_one, shard_one, shard_two = lax.optimization_barrier((peak_one, shard_one, shard_two))
    embedded_low, norm_one, peak_one = first_back(
        plan, groups, wq, wk, wv, grad_first_res, normal_one, inverse_one, norm_params, peak_one
    )
    scale_one = wire_scale(plan, peak_one)
    grad_rows = summed_rows(slot, embedded_low, slots).astype(BF16)
    shard_three = plan.scatter(part_three, "yx", scale_one)
    shard_four = plan.scatter(part_four, "xy", scale_one)
    grad_table = summed_rows(asked.reshape(-1), swap_rows(plan, grad_rows), vocab_shard)

    def return_more(turn, sofar):
        later, later_asked = ask(turn)
        later_rows = summed_rows(later, embedded_low, slots).astype(BF16)
        return sofar + summed_rows(
            later_asked.reshape(-1), swap_rows(plan, later_rows), vocab_shard
        )

    grad_table = lax.fori_loop(1, rounds, return_more, grad_table)
    owned_squares = jnp.sum(grad_table * grad_table)
    for shard in (shard_one, shard_two, shard_three, shard_four):
        owned_squares = owned_squares + jnp.sum(shard * shard)
    grad_gate, grad_up, grad_down_own = unfold_feed(shard_one, shard_two, wg.shape[-1])
    grad_q, grad_k, grad_v, grad_out_own = unfold_attend(shard_three, shard_four)
    grad_qkv_own = jnp.stack([grad_q, grad_k, grad_v], axis=1)
    grad_gate_own = jnp.stack([grad_gate, grad_up], axis=1)
    length_float = own_length.astype(F32)
    norm_grads, square_total = total(
        plan,
        jnp.concatenate(
            [
                norm_one[0:2],
                norm_two[0:2],
                grad_pool * pool,
                grad_pool * length_float,
            ],
            axis=0,
        ).reshape(-1),
        owned_squares,
    )
    norm_grads = norm_grads.reshape(norm_params.shape)
    squares = square_total + jnp.sum(norm_grads * norm_grads) + grad_log_scale * grad_log_scale
    grad_norm = jnp.sqrt(squares)
    factor = jnp.minimum(1.0, clip_limit / (grad_norm + 1e-06))
    return (
        (batch_loss, grad_norm)
        + adam_step(token_table, table_first, table_second, grad_table, factor)
        + adam_step(qkv_weight, qkv_first, qkv_second, grad_qkv_own, factor)
        + adam_step(out_weight, out_first, out_second, grad_out_own, factor)
        + adam_step(gate_up_weight, gate_up_first, gate_up_second, grad_gate_own, factor)
        + adam_step(down_weight, down_first, down_second, grad_down_own, factor)
        + adam_step(norm_params, norm_first, norm_second, norm_grads, factor)
        + adam_step(log_inverse_warmth, scale_first, scale_second, grad_log_scale, factor)
    )


def solution(mesh):
    rows = P(AXES, None)
    deep = P("dp", None, "tensor")
    flat = P("dp", "tensor")
    in_specs = (
        (rows, P("dp", None)) + (rows,) * 3 + (deep,) * 3 + (flat,) * 3 + (deep,) * 3 + (flat,) * 3
    ) + (P(),) * 6
    out_specs = (
        (P(), P()) + (rows,) * 3 + (deep,) * 3 + (flat,) * 3 + (deep,) * 3 + (flat,) * 3
    ) + (P(),) * 6

    def run(*args):
        plan = Plan(mesh, args[2].shape[1])
        return jax.shard_map(
            functools.partial(per_device, plan),
            mesh=mesh,
            in_specs=in_specs,
            out_specs=out_specs,
            check_vma=False,
        )(*args)

    return run
```
